128 devices in a mesh: batch: 32 (over z, x, core), hidden: 4 (over y).
Axes of the slice: x: 4, y: 4, z: 4, core: 2. Of those that a mesh axis runs over, the one named last changes fastest.
Arguments:
- tables: float32 [26, 131072, 16], P(None, ('batch', 'hidden')), may hold values from -6 to 6
- dense: float32 [16384, 13], P('batch'), may hold values from -6 to 6
- dense_weight: float32 [13, 96], replicated, may hold values from -1.75 to 1.75
- expert_in: float32 [512, 8, 256], P(None, None, 'hidden'), may hold values from -0.25 to 0.25
- expert_out: float32 [8, 256, 128], P(None, 'hidden'), may hold values from -0.375 to 0.375
- gate_weight: float32 [2, 512, 8], replicated, may hold values from -0.125 to 0.125
- tower_weight: float32 [2, 128, 64], replicated, may hold values from -0.5 to 0.5
- head_weight: float32 [2, 64], replicated, may hold values from -0.75 to 0.75
- slots: int32 [16384, 26], P('batch'), may hold values from 0 to 4095, as said below
- requests: int32 [32, 128, 32], P('batch'), may hold values from 0 to 26623
- pred_cot: float32 [16384, 2], P(('batch', 'hidden')), may hold values from -6 to 6
Outputs:
- predictions: float32 [16384, 2], P(('batch', 'hidden'))
- dense_grad: float32 [16384, 13], P('batch')
- table_grad: float32 [26, 131072, 16], P(None, ('batch', 'hidden'))
- dense_weight_grad: float32 [13, 96], replicated
- expert_in_grad: float32 [512, 8, 256], P(None, None, 'hidden')
- expert_out_grad: float32 [8, 256, 128], P(None, 'hidden')
- gate_grad: float32 [2, 512, 8], replicated
- tower_grad: float32 [2, 128, 64], replicated
- head_grad: float32 [2, 64], replicated
The draws below stay inside these ranges and needn't reach their ends.
Inputs may be any that keep to these rules, and one draw needn't show every extreme that they name: slots[e, t] = o * 32 + j names slot j of owner o in the fetch list of the example's group; in every group some owner has all 32 slots named, and every owner is named. requests[g, o, j] = v names row o * 1024 + (v mod 1024) of table floor(v / 1024).
All inputs are finite; a program needn't handle non-finite values.
Results may differ from the reference program's by a relative error of at most 0.0003.
Values sent between devices are 32-bit elements; how exact they have to be, the bound alone decides.
A program may use at most 64 MiB of HBM per device.

```python
import jax
import jax.numpy as jnp
from jax import lax

NTAB = 26
ED = 16
NDENSE = 13
DPROJ = 96
NEXP = 8
HID = 256
OUT = 128
NTASK = 2
TW = 64
EX_DEV = 512
TR_DEV = 1024
CAP = 32
D = 512
GROUPS = 32
OWNERS = 128
EXAMPLES = 16384
TAB_ROWS = 131072


def draw_slots(key, part):
    key = jax.random.fold_in(key, 11)
    key_spread, key_rank, key_perm, key_slot = jax.random.split(key, 4)
    lookups = EX_DEV * NTAB
    spread = jax.random.randint(key_spread, (GROUPS, lookups), 1, OWNERS + 1)
    ranked = jax.random.randint(key_rank, (GROUPS, lookups), 0, spread)
    orders = jax.vmap(lambda subkey: jax.random.permutation(subkey, OWNERS))(jax.random.split(key_perm, GROUPS))
    owner = jnp.take_along_axis(orders, ranked, axis=1)
    chosen = jax.random.randint(key_slot, (GROUPS, lookups), 0, CAP)
    position = jnp.arange(lookups, dtype=jnp.int32)[None, :]
    owner = jnp.where(position < CAP, orders[:, :1], owner)
    chosen = jnp.where(position < CAP, position, chosen)
    sweep = (position >= CAP) & (position < CAP + OWNERS)
    owner = jnp.where(sweep, position - CAP, owner)
    return (owner * CAP + chosen).reshape(GROUPS * EX_DEV, NTAB).astype(jnp.int32)


def plant(array, own_key, smallest, top_value):
    longest = array.shape.index(max(array.shape))
    spots = []
    for shift in (0, 1):
        where = [jax.random.randint(jax.random.fold_in(own_key, axis), (), 0, length) for axis, length in enumerate(array.shape)]
        where[longest] = (where[longest] + shift) % array.shape[longest]
        spots.append(tuple(where))
    return array.at[spots[0]].set(smallest).at[spots[1]].set(top_value)


def block_scale(stream_key, shape, pieces, least, high):
    loudness, own = 1.0, jax.random.fold_in(stream_key, 6)
    for dim, blocks in pieces:
        steps = jnp.exp(jax.random.uniform(jax.random.fold_in(own, dim), (blocks,), jnp.float32, least / len(pieces), high / len(pieces)))
        loudness = loudness * jnp.repeat(steps, shape[dim] // blocks).reshape([-1 if axis == dim else 1 for axis in range(len(shape))])
    return loudness


def bell_draw(key, dims, scale, most, pieces=(), held_as=jnp.bfloat16):
    entries = scale * jax.random.normal(key, dims, jnp.float32)
    if pieces:
        entries = entries * block_scale(key, dims, pieces, -0.22, 0.18)
    return jnp.clip(entries, -most, most).astype(held_as)


def setup_inputs(seed: int = 0) -> dict:
    key_of = jax.random.split(jax.random.key(seed), 12)
    return {
        "tables": bell_draw(key_of[0], (NTAB, TAB_ROWS, ED), 1.0, 6.0, ((1, 128),), jnp.float32),
        "dense": bell_draw(key_of[1], (EXAMPLES, NDENSE), 1.0, 6.0, ((0, 32),), jnp.float32),
        "dense_weight": bell_draw(key_of[2], (NDENSE, DPROJ), NDENSE ** -0.5, 1.75, (), jnp.float32),
        "expert_in": bell_draw(key_of[3], (D, NEXP, HID), D ** -0.5, 0.25, ((2, 4),), jnp.float32),
        "expert_out": bell_draw(key_of[4], (NEXP, HID, OUT), HID ** -0.5, 0.375, ((1, 4),), jnp.float32),
        "gate_weight": bell_draw(key_of[5], (NTASK, D, NEXP), (4 * D) ** -0.5, 0.125, (), jnp.float32),
        "tower_weight": bell_draw(key_of[6], (NTASK, OUT, TW), OUT ** -0.5, 0.5, (), jnp.float32),
        "head_weight": bell_draw(key_of[7], (NTASK, TW), TW ** -0.5, 0.75, (), jnp.float32),
        "slots": draw_slots(jax.random.fold_in(key_of[11], 71), 0),
        "requests": plant(jax.random.randint(key_of[9], (GROUPS, OWNERS, CAP), 0, NTAB * TR_DEV), jax.random.fold_in(key_of[9], 1), 0, (NTAB * TR_DEV) - 1).astype(jnp.int32),
        "pred_cot": bell_draw(key_of[10], (EXAMPLES, NTASK), 1.0, 6.0, ((0, 128),), jnp.float32),
    }


@jax.custom_vjp
def low(v):
    return lax.optimization_barrier(v.astype(jnp.bfloat16)).astype(jnp.float32)

@jax.custom_vjp
def low_back(v):
    return v

def low_keep(v):
    return (low(v), None)

def low_pass(kept, grad):
    return (grad,)

def back_keep(v):
    return (v, None)

def back_low(kept, grad):
    return (low(grad),)
low.defvjp(low_keep, low_pass)
low_back.defvjp(back_keep, back_low)

def silu_plain(value):
    return value * jax.nn.sigmoid(value)

def forward(tables, dense, dense_weight, expert_in, expert_out, gate_weight, tower_weight, head_weight, slots, requests):
    highest = lax.Precision.HIGHEST
    group_of = (jnp.arange(EXAMPLES, dtype=jnp.int32) // EX_DEV)[:, None]
    owner_of = slots // CAP
    local_id = requests[group_of, owner_of, slots % CAP]
    embed = tables[local_id // TR_DEV, owner_of * TR_DEV + local_id % TR_DEV]
    projected = jnp.dot(dense, dense_weight, precision=highest)
    features = jnp.concatenate([embed.reshape(EXAMPLES, NTAB * ED), projected], axis=1)
    inner = silu_plain(jnp.einsum('nd,dek->nek', features, expert_in, precision=highest))
    expert_outputs = silu_plain(jnp.einsum('nek,eko->neo', inner, expert_out, precision=highest))
    gates = jax.nn.softmax(jnp.einsum('nd,tde->nte', features, gate_weight, precision=highest), axis=-1)
    mixed = jnp.einsum('nte,neo->nto', gates, expert_outputs, precision=highest)
    towers = silu_plain(jnp.einsum('nto,tow->ntw', mixed, tower_weight, precision=highest))
    return jax.nn.sigmoid(jnp.einsum('ntw,tw->nt', towers, head_weight, precision=highest))

def reference(tables, dense, dense_weight, expert_in, expert_out, gate_weight, tower_weight, head_weight, slots, requests, pred_cot):

    def model(tables_in, dense_in, dense_w, first_w, second_w, gate_w, tower_w, head_w):
        return forward(tables_in, dense_in, dense_w, first_w, second_w, gate_w, tower_w, head_w, slots, requests)
    predictions, pullback = jax.vjp(model, tables, dense, dense_weight, expert_in, expert_out, gate_weight, tower_weight, head_weight)
    grads = pullback(pred_cot)
    return (predictions, grads[1], grads[0], grads[2], grads[3], grads[4], grads[5], grads[6], grads[7])
```

```python
import jax
import jax.numpy as jnp
from jax import lax
from jax.experimental import pallas as pl
from jax.experimental.pallas import tpu as pltpu
from jax.sharding import PartitionSpec as P

f32 = jnp.float32
bf16 = jnp.bfloat16
MESH = pl.DeviceIdType.MESH
VMEM = pl.BlockSpec(memory_space=pltpu.VMEM)
LIMIT = 56 * 2**20

TABLES, ROWS, ENTRY = 26, 1024, 16
BATCH, HIDDEN = 32, 4
DEVICES = BATCH * HIDDEN
EXPERTS, UNITS, OUT, WIDTH = 8, 64, 128, 512
TASKS, TOWER, DENSE, PROJ = 2, 64, 13, 96
EXAMPLES = 512
EMBED = TABLES * ENTRY

IN_ROWS, OUT_ROWS, GATE_ROWS, TOWER_ROWS = 2048, 512, 64, 128
OUT_AT = IN_ROWS
GATE_AT = OUT_AT + OUT_ROWS
TOWER_AT = GATE_AT + GATE_ROWS
DENSE_AT = TOWER_AT + TOWER_ROWS
HEAD_AT = DENSE_AT + 16
PIECE = 88
HALF = 16 * PIECE
SUMMED = 2 * HALF


def split(value):
    high = value.astype(bf16)
    return high, (value - high.astype(f32)).astype(bf16)


def dot_nn(a, b):
    return lax.dot_general(a, b, (((1,), (0,)), ((), ())), preferred_element_type=f32)


def dot_nt(a, b):
    return lax.dot_general(a, b, (((1,), (1,)), ((), ())), preferred_element_type=f32)


def dot3_nn(a, b):
    (ah, al), (bh, bl) = a, b
    return dot_nn(jnp.concatenate([ah, al, ah], 1), jnp.concatenate([bh, bh, bl], 0))


def dot3_nt(a, b):
    (ah, al), (bh, bl) = a, b
    return dot_nt(jnp.concatenate([ah, al, ah], 1), jnp.concatenate([bh, bh, bl], 1))


def sigmoid(value):
    return 0.5 * jnp.tanh(0.5 * value) + 0.5


def silu_both(value):
    sigma = sigmoid(value)
    result = value * sigma
    return result, sigma + result * (1.0 - sigma)


def iota(shape, axis):
    return lax.broadcasted_iota(jnp.int32, shape, axis)


def place():
    b, h = lax.axis_index("batch"), lax.axis_index("hidden")
    return b, h, lax.rem(b, 2)


def target(b, h):
    return {"batch": b, "hidden": h}


def remote(src, dst, send, recv, b, h):
    return pltpu.make_async_remote_copy(src, dst, send, recv, device_id=target(b, h), device_id_type=MESH)


def bulk_wait(ref, sem):
    pltpu.make_async_copy(ref, ref, sem).wait()


def ids_by_query(received):
    turned = jnp.concatenate([received] * 4, 0).T
    lane = iota((8, 128), 1) // 32
    out = jnp.zeros((8, 128), jnp.int32)
    for q in range(4):
        out = jnp.where(lane == q, turned[q * 8 : q * 8 + 8, :], out)
    return out


def fetch_kernel(
    req, tab, win, wout, cot,
    rows_out, ids_out, win_all, wout_all, cot_all,
    id_turned, id_send, id_recv, row_send, tab_split,
    y_send, y_recv, core_send, core_recv, cot_send, cot_recv, id_ssem, id_rsem, row_ssem, row_rsem, local_sem,
):
    b, h, core = place()
    sibling = b + 1 - 2 * core
    me = b * HIDDEN + h
    barrier = pltpu.get_barrier_semaphore()

    def greet(i, carry):
        other = lax.rem(me + i, DEVICES)
        pl.semaphore_signal(
            barrier, inc=1, device_id=target(other // HIDDEN, lax.rem(other, HIDDEN)), device_id_type=MESH
        )
        return carry

    lax.fori_loop(1, DEVICES, greet, 0)
    id_turned[...] = jnp.concatenate([req[...]] * 4, 0).T
    id_send[...] = id_turned[pl.ds(h, BATCH, stride=HIDDEN), :]
    pl.semaphore_wait(barrier, DEVICES - 1)

    def send_ids(i, carry):
        other = lax.rem(b + i, BATCH)
        remote(id_send.at[pl.ds(other, 1)], id_recv.at[pl.ds(b, 1)], id_ssem, id_rsem, other, h).start()
        return carry

    lax.fori_loop(1, BATCH, send_ids, 0)
    half = pl.ds(pl.multiple_of(core * 256, 256), 256)
    y_copies = []
    for i in range(1, HIDDEN):
        other = lax.rem(h + i, HIDDEN)
        y_copies.append(
            (
                remote(win.at[half], win_all.at[h, half], y_send.at[i - 1, 0], y_recv.at[i - 1, 0], b, other),
                remote(wout.at[half], wout_all.at[h, half], y_send.at[i - 1, 1], y_recv.at[i - 1, 1], b, other),
                remote(cot, cot_all.at[h], cot_send.at[i - 1], cot_recv.at[i - 1], b, other),
            )
        )
        for copy in y_copies[-1]:
            copy.start()
    own = (
        pltpu.make_async_copy(win, win_all.at[h], local_sem.at[0]),
        pltpu.make_async_copy(wout, wout_all.at[h], local_sem.at[1]),
        pltpu.make_async_copy(cot, cot_all.at[h], local_sem.at[2]),
    )
    for copy in own:
        copy.start()
    high, low = split(tab[...])
    tab_split[0:EMBED, :] = high
    tab_split[EMBED : 2 * EMBED, :] = low
    id_recv[pl.ds(b, 1), :] = id_send[pl.ds(b, 1), :]
    bulk_wait(id_recv.at[pl.ds(0, BATCH - 1)], id_rsem)
    ids = ids_by_query(id_recv[...])
    ids_out[...] = ids
    table, row = ids // ROWS, lax.rem(ids, ROWS)
    found = []
    for pair in range(4):
        hot = jnp.concatenate(
            [(iota((ROWS, 128), 0) == row[j : j + 1, :]).astype(f32).astype(bf16) for j in (2 * pair, 2 * pair + 1)], 1
        )
        got = dot_nn(tab_split[...], hot)
        for part in range(2):
            wanted = table[2 * pair + part : 2 * pair + part + 1, :]
            total = jnp.zeros((ENTRY, 128), f32)
            for t in range(TABLES):
                block = got[t * ENTRY : (t + 1) * ENTRY, part * 128 : part * 128 + 128]
                rest = got[EMBED + t * ENTRY : EMBED + (t + 1) * ENTRY, part * 128 : part * 128 + 128]
                total = jnp.where(wanted == t, block + rest, total)
            found.append(total)
    turned = jnp.concatenate(found, 0).T
    for q in range(4):
        row_send[pl.ds(q, BATCH, stride=4), :] = turned[q * 32 : q * 32 + 32, :]
    mine = pl.ds(me * 4, 4)

    def send_rows(i, carry):
        other = lax.rem(me + i, DEVICES)
        group = other // HIDDEN
        remote(
            row_send.at[pl.ds(group * 4, 4)], rows_out.at[mine], row_ssem, row_rsem, group, lax.rem(other, HIDDEN)
        ).start()
        return carry

    lax.fori_loop(1, DEVICES, send_rows, 0)
    rows_out[mine, :] = row_send[pl.ds(b * 4, 4), :]
    forwards = []
    for i in range(1, HIDDEN):
        source = lax.rem(h - i + HIDDEN, HIDDEN)
        for which, whole in ((0, win_all), (1, wout_all)):
            y_copies[i - 1][which].wait_recv()
            block = whole.at[source, half]
            forwards.append(
                remote(block, block, core_send.at[i - 1, which], core_recv.at[i - 1, which], sibling, h)
            )
            forwards[-1].start()
        y_copies[i - 1][2].wait_recv()
    bulk_wait(rows_out.at[pl.ds(0, (DEVICES - 1) * 4)], row_rsem)
    for copy in forwards:
        copy.wait()
    for copies in y_copies:
        for copy in copies:
            copy.wait_send()
    for copy in own:
        copy.wait()
    bulk_wait(id_send.at[pl.ds(0, BATCH - 1)], id_ssem)
    bulk_wait(rows_out.at[pl.ds(0, (DEVICES - 1) * 4)], row_ssem)


def hot_of(code, count):
    return (iota((count, code.shape[1]), 0) == code).astype(f32).astype(bf16)


def model_kernel(
    rows, slots, dense, dense_weight, win_all, wout_all, gate_weight, tower_weight, head, cot_all,
    pred_out, dense_grad_out, sums, message,
    wh, wl, wth, wtl, oh, ol, oth, otl,
    lists, feat_h, feat_l, dense_pad, weight_pad, head_pad,
    inner_h, inner_l, slope, ig_h, ig_l, eo, eslope, ep_h, ep_l, gates, gate_slope, mixed, mixed_grad, fg, slot_sum, slot_done,
):
    b, h, core = place()
    for e in range(EXPERTS):
        at = pl.ds(e * UNITS, UNITS)
        value = jnp.concatenate([win_all[i, at, :] for i in range(HIDDEN)], 0)
        wh[e], wl[e] = split(value)
        wth[e], wtl[e] = split(value.T)
        value = jnp.concatenate([wout_all[i, at, :] for i in range(HIDDEN)], 0)
        oh[e], ol[e] = split(value)
        oth[e], otl[e] = split(value.T)
    for q in range(4):
        high, low = split(rows[pl.ds(q, DEVICES, stride=4), :].T)
        lists[0:128, q * 128 : q * 128 + 128] = high
        lists[128:256, q * 128 : q * 128 + 128] = low

    def codes(t):
        slot = slots[pl.ds(t, 1), :]
        return (slot % 32) // 8 * 128 + slot // 32, slot % 8

    def gather(t, carry):
        code, low = codes(t)
        got = dot_nn(lists[...], hot_of(code, 512))
        high_sum = jnp.zeros((ENTRY, EXAMPLES), f32)
        low_sum = jnp.zeros((ENTRY, EXAMPLES), f32)
        for j in range(8):
            high_sum = jnp.where(low == j, got[j * 16 : j * 16 + 16, :], high_sum)
            low_sum = jnp.where(low == j, got[128 + j * 16 : 128 + j * 16 + 16, :], low_sum)
        at = pl.ds(pl.multiple_of(t * ENTRY, ENTRY), ENTRY)
        feat_h[at, :] = high_sum.astype(bf16)
        feat_l[at, :] = low_sum.astype(bf16)
        return carry

    lax.fori_loop(0, TABLES, gather, 0)
    dense_pad[...] = jnp.zeros_like(dense_pad)
    dense_pad[0:DENSE, :] = dense[...]
    weight_pad[...] = jnp.zeros_like(weight_pad)
    weight_pad[0:DENSE, 0:PROJ] = dense_weight[...]
    head_pad[...] = jnp.zeros_like(head_pad)
    head_pad[0:TASKS, 0:TOWER] = head[...]
    dense_split = split(dense_pad[...])
    projected = dot3_nn(split(weight_pad[...].T), dense_split)
    high, low = split(projected[0:PROJ, :])
    feat_h[EMBED:WIDTH, :] = high
    feat_l[EMBED:WIDTH, :] = low
    gate_split = split(gate_weight[...])
    logits = dot3_nn(gate_split, (feat_h[...], feat_l[...]))
    for k in range(TASKS):
        part = logits[k * 8 : k * 8 + 8, :]
        raised = jnp.exp(part - jnp.max(part, axis=0, keepdims=True))
        gates[k * 8 : k * 8 + 8, :] = raised / jnp.sum(raised, axis=0, keepdims=True)
    mixed[...] = jnp.zeros_like(mixed)

    def forward(e, carry):
        pre = dot3_nn((wh[e], wl[e]), (feat_h[...], feat_l[...]))
        inner, slope[e] = silu_both(pre)
        high, low = split(inner)
        inner_h[e], inner_l[e] = high, low
        outputs, eslope[e] = silu_both(dot3_nn((oth[e], otl[e]), (high, low)))
        eo[e] = outputs
        for k in range(TASKS):
            mixed[k] = mixed[k] + gates[pl.ds(k * 8 + e, 1), :] * outputs
        return carry

    lax.fori_loop(0, EXPERTS, forward, 0)
    head_turned = head_pad[...].T
    tower_turned = split(tower_weight[...].T)
    tower_grads, score_grads, tower_list = [], [], []
    for k in range(TASKS):
        at = slice(k * TOWER, (k + 1) * TOWER)
        mixed_split = split(mixed[k])
        towers, tower_slope = silu_both(dot3_nn(split(tower_weight[at, :]), mixed_split))
        column = jnp.broadcast_to(head_turned[0:TOWER, k : k + 1], (TOWER, EXAMPLES))
        predicted = sigmoid(jnp.sum(towers * column, axis=0, keepdims=True))
        mixed_grad[k, 0:1, :] = predicted
        pred_out[k : k + 1, :] = mixed_grad[k, 0:1, pl.ds(pl.multiple_of(h * 128, 128), 128)]
        cotangent = jnp.concatenate([cot_all[i, k : k + 1, :] for i in range(HIDDEN)], 1)
        score = cotangent * predicted * (1.0 - predicted)
        pre_grad = score * column * tower_slope
        sums[TOWER_AT + k * TOWER : TOWER_AT + (k + 1) * TOWER, :] = dot3_nt(split(pre_grad), mixed_split)
        tower_grads.append(pre_grad)
        score_grads.append(score)
        tower_list.append(towers)
    nothing = jnp.zeros((TOWER, EXAMPLES), f32)
    mixed_grad[0] = dot3_nn(tower_turned, split(jnp.concatenate([tower_grads[0], nothing], 0)))
    mixed_grad[1] = dot3_nn(tower_turned, split(jnp.concatenate([nothing, tower_grads[1]], 0)))
    scores = jnp.concatenate(score_grads + [jnp.zeros((14, EXAMPLES), f32)], 0)
    head_rows = dot3_nt(split(scores), split(jnp.concatenate(tower_list, 0)))
    sums[HEAD_AT:SUMMED, :] = jnp.zeros((SUMMED - HEAD_AT, 128), f32)
    sums[HEAD_AT : HEAD_AT + 1, :] = jnp.where(iota((1, 128), 1) < TOWER, head_rows[0:1, :], head_rows[1:2, :])
    fg[...] = jnp.zeros_like(fg)
    mine = pl.ds(pl.multiple_of(h * UNITS, UNITS), UNITS)

    def backward(e, carry):
        outputs = eo[e]
        total = jnp.zeros((OUT, EXAMPLES), f32)
        for k in range(TASKS):
            grad = mixed_grad[k]
            gate_slope[pl.ds(k * 8 + e, 1), :] = jnp.sum(grad * outputs, axis=0, keepdims=True)
            total = total + gates[pl.ds(k * 8 + e, 1), :] * grad
        high, low = split(total * eslope[e])
        ep_h[e], ep_l[e] = high, low
        inner_grad = dot3_nn((oh[e], ol[e]), (high, low)) * slope[e]
        ig = split(inner_grad)
        ig_h[e], ig_l[e] = ig
        fg[...] += dot3_nn((wth[e], wtl[e]), ig)
        own = (inner_h[e, mine, :], inner_l[e, mine, :])
        sums[pl.ds(pl.multiple_of(OUT_AT + e * UNITS, UNITS), UNITS), :] = dot3_nt(own, (high, low))
        return carry

    lax.fori_loop(0, EXPERTS, backward, 0)
    feat = (feat_h[...], feat_l[...])
    own = tuple(jnp.concatenate([ref[e, mine, :] for e in range(EXPERTS)], 0) for ref in (ig_h, ig_l))
    in_grad = dot3_nt(own, feat)
    for q in range(4):
        sums[q * 512 : (q + 1) * 512, :] = in_grad[:, q * 128 : (q + 1) * 128]
    logit_grads = []
    for k in range(TASKS):
        gate, slopes = gates[k * 8 : k * 8 + 8, :], gate_slope[k * 8 : k * 8 + 8, :]
        logit_grads.append(gate * (slopes - jnp.sum(gate * slopes, axis=0, keepdims=True)))
    lgh, lgl = split(jnp.concatenate(logit_grads, 0))
    gate_grad = dot3_nt((lgh, lgl), feat)
    for q in range(4):
        sums[GATE_AT + q * 16 : GATE_AT + q * 16 + 16, :] = gate_grad[:, q * 128 : (q + 1) * 128]
    gh, gl = (part.astype(f32) for part in gate_split)
    stacked = jnp.concatenate([gh, gl, gh, jnp.zeros((80, WIDTH), f32)], 0).T.astype(bf16)
    fg[...] += dot_nn(stacked, jnp.concatenate([lgh, lgh, lgl, jnp.zeros((80, EXAMPLES), bf16)], 0))
    projected_grad = split(jnp.concatenate([fg[EMBED:WIDTH, :], jnp.zeros((32, EXAMPLES), f32)], 0))
    dense_grad_out[...] = dot3_nn(split(weight_pad[...]), projected_grad)[0:DENSE, :]
    sums[DENSE_AT : DENSE_AT + 16, :] = dot3_nt(dense_split, projected_grad)[0:16, :]
    slot_sum[...] = jnp.zeros_like(slot_sum)

    def scatter(t, carry):
        code, low = codes(t)
        grad = fg[pl.ds(pl.multiple_of(t * ENTRY, ENTRY), ENTRY), :]
        high = grad.astype(bf16).astype(f32)
        rest = grad - high
        parts = [jnp.where(low == j, part, 0.0) for part in (high, rest) for j in range(8)]
        spread = jnp.concatenate(parts, 0).astype(bf16)
        slot_sum[...] += dot_nt(hot_of(code, 512), spread)
        return carry

    lax.fori_loop(0, TABLES, scatter, 0)
    slot_done[...] = slot_sum[:, 0:128] + slot_sum[:, 128:256]
    for q in range(4):
        message[pl.ds(q, BATCH, stride=4), :] = slot_done[pl.ds(q * 128 + h, BATCH, stride=HIDDEN), :]


def sum_kernel(
    sums, message, ids,
    table_grad, total,
    got, from_core, reduced, pieces,
    core_send, core_recv, slot_ssem, slot_rsem, piece_ssem, piece_rsem, full_ssem, full_rsem,
):
    b, h, core = place()
    sibling = b + 1 - 2 * core
    chip = b // 2
    barrier = pltpu.get_barrier_semaphore()

    def greet(i, carry):
        pl.semaphore_signal(barrier, inc=1, device_id=target(lax.rem(b + i, BATCH), h), device_id_type=MESH)
        return carry

    lax.fori_loop(1, BATCH, greet, 0)
    pl.semaphore_wait(barrier, BATCH - 1)
    mine = pl.ds(pl.multiple_of(core * HALF, HALF), HALF)
    theirs = pl.ds(pl.multiple_of((1 - core) * HALF, HALF), HALF)
    exchange = remote(sums.at[theirs], from_core, core_send.at[0], core_recv.at[0], sibling, h)
    exchange.start()

    def send_slots(i, carry):
        other = lax.rem(b + i, BATCH)
        remote(message.at[pl.ds(other * 4, 4)], got.at[pl.ds(b * 4, 4)], slot_ssem, slot_rsem, other, h).start()
        return carry

    lax.fori_loop(1, BATCH, send_slots, 0)
    got[pl.ds(b * 4, 4), :] = message[pl.ds(b * 4, 4), :]
    exchange.wait()
    reduced[...] = sums[mine, :] + from_core[...]

    def send_pieces(i, carry):
        other = lax.rem(chip + i, 16)
        remote(
            reduced.at[pl.ds(pl.multiple_of(other * PIECE, 8), PIECE)],
            pieces.at[pl.ds(pl.multiple_of(chip * PIECE, 8), PIECE)],
            piece_ssem, piece_rsem, other * 2 + core, h,
        ).start()
        return carry

    lax.fori_loop(1, 16, send_pieces, 0)
    own = pl.ds(pl.multiple_of(chip * PIECE, 8), PIECE)
    pieces[own, :] = reduced[own, :]
    bulk_wait(got.at[pl.ds(0, (BATCH - 1) * 4)], slot_rsem)
    turned = jnp.concatenate([got[pl.ds(q, BATCH, stride=4), :] for q in range(4)], 0).T
    table, row = ids[...] // ROWS, lax.rem(ids[...], ROWS)
    high = turned.astype(bf16).astype(f32)
    rest = turned - high
    spread = []
    for j in range(8):
        parts = [
            jnp.where(table[j : j + 1, :] == t, part[j * 16 : j * 16 + 16, :], 0.0)
            for part in (high, rest)
            for t in range(TABLES)
        ]
        spread.append(jnp.concatenate(parts, 0).astype(bf16))
    spread = jnp.concatenate(spread, 1)
    for part in range(4):
        hot = jnp.concatenate(
            [(iota((256, 128), 0) + part * 256 == row[j : j + 1, :]).astype(f32).astype(bf16) for j in range(8)], 1
        )
        both = dot_nt(spread, hot)
        table_grad[:, part * 256 : (part + 1) * 256] = both[0:EMBED, :] + both[EMBED : 2 * EMBED, :]
    bulk_wait(pieces.at[pl.ds(0, 15 * PIECE)], piece_rsem)
    bulk_wait(pieces.at[pl.ds(0, 15 * PIECE)], piece_ssem)
    value = pieces[0:PIECE, :]
    for i in range(1, 16):
        value = value + pieces[i * PIECE : (i + 1) * PIECE, :]
    place_of = pl.ds(pl.multiple_of(core * HALF + chip * PIECE, 8), PIECE)
    total[place_of, :] = value

    def send_full(i, carry):
        other = lax.rem(chip + i, 16)
        remote(total.at[place_of], total.at[place_of], full_ssem, full_rsem, other * 2 + core, h).start()
        return carry

    lax.fori_loop(1, 16, send_full, 0)
    bulk_wait(total.at[pl.ds(0, 15 * PIECE)], full_rsem)
    last = remote(total.at[mine], total.at[mine], core_send.at[1], core_recv.at[1], sibling, h)
    last.start()
    last.wait()
    bulk_wait(total.at[pl.ds(0, 15 * PIECE)], full_ssem)
    bulk_wait(message.at[pl.ds(0, (BATCH - 1) * 4)], slot_ssem)


def call(kernel, outs, ins, scratch, name, collective_id=None):
    params = dict(vmem_limit_bytes=LIMIT)
    if collective_id is not None:
        params.update(collective_id=collective_id, has_side_effects=True)
    return pl.pallas_call(
        kernel,
        out_shape=[jax.ShapeDtypeStruct(shape, dtype) for shape, dtype in outs],
        in_specs=[VMEM] * ins,
        out_specs=[VMEM] * len(outs),
        scratch_shapes=scratch,
        compiler_params=pltpu.CompilerParams(**params),
        name=name,
    )


def on_device(
    tables, dense, dense_weight, expert_in, expert_out, gate_weight, tower_weight, head_weight, slots, requests, pred_cot
):
    i32 = jnp.int32
    dma = pltpu.SemaphoreType.DMA
    req = requests[0].T
    tab = tables.transpose(0, 2, 1).reshape(EMBED, ROWS)
    win = expert_in.transpose(1, 2, 0).reshape(EXPERTS * UNITS, WIDTH)
    wout = expert_out.reshape(EXPERTS * UNITS, OUT)
    gate = gate_weight.transpose(0, 2, 1).reshape(TASKS * EXPERTS, WIDTH)
    tower = tower_weight.transpose(0, 2, 1).reshape(TASKS * TOWER, OUT)
    rows, ids, win_all, wout_all, cot_all = call(
        fetch_kernel,
        [
            ((512, 128), f32), ((8, 128), i32), ((HIDDEN, 512, WIDTH), f32), ((HIDDEN, 512, OUT), f32),
            ((HIDDEN, TASKS, 128), f32),
        ],
        5,
        [
            pltpu.VMEM((128, 128), i32), pltpu.VMEM((32, 128), i32), pltpu.VMEM((32, 128), i32),
            pltpu.VMEM((128, 128), f32), pltpu.VMEM((2 * EMBED, ROWS), bf16),
            dma((3, 2)), dma((3, 2)), dma((3, 2)), dma((3, 2)), dma((3,)), dma((3,)), dma, dma, dma, dma, dma((3,)),
        ],
        "fetch",
        0,
    )(req, tab, win, wout, pred_cot.T)
    units = EXPERTS, 256, EXAMPLES
    outputs = EXPERTS, OUT, EXAMPLES
    predictions, dense_grad, sums, message = call(
        model_kernel,
        [((TASKS, 128), f32), ((DENSE, EXAMPLES), f32), ((SUMMED, 128), f32), ((128, 128), f32)],
        10,
        [
            pltpu.VMEM((EXPERTS, 256, WIDTH), bf16), pltpu.VMEM((EXPERTS, 256, WIDTH), bf16),
            pltpu.VMEM((EXPERTS, WIDTH, 256), bf16), pltpu.VMEM((EXPERTS, WIDTH, 256), bf16),
            pltpu.VMEM((EXPERTS, 256, OUT), bf16), pltpu.VMEM((EXPERTS, 256, OUT), bf16),
            pltpu.VMEM((EXPERTS, OUT, 256), bf16), pltpu.VMEM((EXPERTS, OUT, 256), bf16),
            pltpu.VMEM((256, 512), bf16), pltpu.VMEM((WIDTH, EXAMPLES), bf16), pltpu.VMEM((WIDTH, EXAMPLES), bf16),
            pltpu.VMEM((128, EXAMPLES), f32), pltpu.VMEM((128, 128), f32), pltpu.VMEM((128, 128), f32),
            pltpu.VMEM(units, bf16), pltpu.VMEM(units, bf16), pltpu.VMEM(units, f32),
            pltpu.VMEM(units, bf16), pltpu.VMEM(units, bf16),
            pltpu.VMEM(outputs, f32), pltpu.VMEM(outputs, f32), pltpu.VMEM(outputs, bf16), pltpu.VMEM(outputs, bf16),
            pltpu.VMEM((16, EXAMPLES), f32), pltpu.VMEM((16, EXAMPLES), f32),
            pltpu.VMEM((TASKS, OUT, EXAMPLES), f32), pltpu.VMEM((TASKS, OUT, EXAMPLES), f32),
            pltpu.VMEM((WIDTH, EXAMPLES), f32), pltpu.VMEM((512, 256), f32), pltpu.VMEM((512, 128), f32),
        ],
        "model",
    )(rows, slots.T, dense.T, dense_weight, win_all, wout_all, gate, tower, head_weight, cot_all)
    table_grad, total = call(
        sum_kernel,
        [((EMBED, ROWS), f32), ((SUMMED, 128), f32)],
        3,
        [
            pltpu.VMEM((128, 128), f32), pltpu.VMEM((HALF, 128), f32), pltpu.VMEM((HALF, 128), f32),
            pltpu.VMEM((HALF, 128), f32),
            dma((2,)), dma((2,)), dma, dma, dma, dma, dma, dma,
        ],
        "sum",
        1,
    )(sums, message, ids)
    in_grad = total[:IN_ROWS].reshape(4, EXPERTS, UNITS, 128).transpose(0, 3, 1, 2).reshape(WIDTH, EXPERTS, UNITS)
    out_grad = total[OUT_AT:GATE_AT].reshape(EXPERTS, UNITS, OUT)
    gate_grad = total[GATE_AT:TOWER_AT].reshape(4, TASKS, EXPERTS, 128).transpose(1, 0, 3, 2)
    tower_grad = total[TOWER_AT:DENSE_AT].reshape(TASKS, TOWER, OUT).transpose(0, 2, 1)
    return (
        predictions.T,
        dense_grad.T,
        table_grad.reshape(TABLES, ENTRY, ROWS).transpose(0, 2, 1),
        total[DENSE_AT : DENSE_AT + DENSE, :PROJ],
        in_grad,
        out_grad,
        gate_grad.reshape(TASKS, WIDTH, EXPERTS),
        tower_grad,
        total[HEAD_AT].reshape(TASKS, TOWER),
    )


def solution(mesh):
    placed = (
        P(None, ("batch", "hidden"), None),
        P("batch", None),
        P(),
        P(None, None, "hidden"),
        P(None, "hidden", None),
        P(),
        P(),
        P(),
        P("batch", None),
        P("batch", None, None),
        P(("batch", "hidden"), None),
    )
    return jax.shard_map(
        on_device,
        mesh=mesh,
        in_specs=placed,
        out_specs=(
            P(("batch", "hidden"), None),
            P("batch", None),
            P(None, ("batch", "hidden"), None),
            P(),
            P(None, None, "hidden"),
            P(None, "hidden", None),
            P(),
            P(),
            P(),
        ),
        check_vma=False,
    )
```

```python
import jax
import jax.numpy as jnp
from jax import lax
from jax.experimental import pallas as pl
from jax.experimental.pallas import tpu as pltpu
from jax.sharding import PartitionSpec as P

f32 = jnp.float32
bf16 = jnp.bfloat16
MESH = pl.DeviceIdType.MESH
VMEM = pl.BlockSpec(memory_space=pltpu.VMEM)
LIMIT = 56 * 2**20

TABLES, ROWS, ENTRY = 26, 1024, 16
BATCH, HIDDEN = 32, 4
DEVICES = BATCH * HIDDEN
EXPERTS, UNITS, OUT, WIDTH = 8, 64, 128, 512
TASKS, TOWER, DENSE, PROJ = 2, 64, 13, 96
EXAMPLES = 512
EMBED = TABLES * ENTRY

IN_ROWS, OUT_ROWS, GATE_ROWS, TOWER_ROWS = 2048, 512, 64, 128
OUT_AT = IN_ROWS
GATE_AT = OUT_AT + OUT_ROWS
TOWER_AT = GATE_AT + GATE_ROWS
DENSE_AT = TOWER_AT + TOWER_ROWS
HEAD_AT = DENSE_AT + 16
PIECE = 88
HALF = 16 * PIECE
SUMMED = 2 * HALF


def split(value):
    high = value.astype(bf16)
    return high, (value - high.astype(f32)).astype(bf16)


def dot_nn(a, b):
    return lax.dot_general(a, b, (((1,), (0,)), ((), ())), preferred_element_type=f32)


def dot_nt(a, b):
    return lax.dot_general(a, b, (((1,), (1,)), ((), ())), preferred_element_type=f32)


def dot3_nn(a, b):
    (ah, al), (bh, bl) = a, b
    return dot_nn(jnp.concatenate([ah, al, ah], 1), jnp.concatenate([bh, bh, bl], 0))


def dot3_nt(a, b):
    (ah, al), (bh, bl) = a, b
    return dot_nt(jnp.concatenate([ah, al, ah], 1), jnp.concatenate([bh, bh, bl], 1))


def sigmoid(value):
    return 0.5 * jnp.tanh(0.5 * value) + 0.5


def silu_both(value):
    sigma = sigmoid(value)
    result = value * sigma
    return result, sigma + result * (1.0 - sigma)


def iota(shape, axis):
    return lax.broadcasted_iota(jnp.int32, shape, axis)


def place():
    b, h = lax.axis_index("batch"), lax.axis_index("hidden")
    return b, h, lax.rem(b, 2)


def target(b, h):
    return {"batch": b, "hidden": h}


def remote(src, dst, send, recv, b, h):
    return pltpu.make_async_remote_copy(src, dst, send, recv, device_id=target(b, h), device_id_type=MESH)


def bulk_wait(ref, sem):
    pltpu.make_async_copy(ref, ref, sem).wait()


def ids_by_query(received):
    turned = jnp.concatenate([received] * 4, 0).T
    lane = iota((8, 128), 1) // 32
    out = jnp.zeros((8, 128), jnp.int32)
    for q in range(4):
        out = jnp.where(lane == q, turned[q * 8 : q * 8 + 8, :], out)
    return out


def hot_of(code, count):
    rows = iota((count, code.shape[1]), 0).astype(jnp.int16)
    return jnp.where(rows == code.astype(jnp.int16), bf16(1.0), bf16(0.0))


def model_kernel(
    req, tab, win, wout, cot, slots, dense, dense_weight, gate_weight, tower_weight, head,
    pred_out, dense_grad_out, table_out, total,
    id_turned, id_send, id_recv, row_send, rows, tab_value, tab_split, win_all, wout_all, cot_all,
    wh, wl, wth, wtl, oh, ol, oth, otl,
    lists, feat_h, feat_l, dense_pad, weight_pad, head_pad,
    inner_h, inner_l, slope, ig_h, ig_l, eo, eslope, ep_h, ep_l, gates, gate_slope, mixed, mixed_grad, pred, fg, slot_sum,
    sums, message, got, from_core, reduced, pieces, table_grad,
    y_send, y_recv, p_send, p_recv, c_send, c_recv, wo_send, wo_recv, woc_send, woc_recv, cot_send, cot_recv,
    id_ssem, id_rsem, row_ssem, row_rsem, local_sem, swap_send, swap_recv, slot_ssem, slot_rsem,
    piece_ssem, piece_rsem, full_ssem, full_recv, last_ssem, last_rsem,
):
    b, h, core = place()
    x, z = lax.rem(b // 2, 4), b // 8
    chip = b // 2
    sibling = b + 1 - 2 * core
    me = b * HIDDEN + h
    locals_in = (
        pltpu.make_async_copy(tab, tab_value, local_sem.at[0]),
        pltpu.make_async_copy(win, win_all.at[h], local_sem.at[1]),
        pltpu.make_async_copy(wout, wout_all.at[h], local_sem.at[2]),
    )
    for copy in locals_in:
        copy.start()
    barrier = pltpu.get_barrier_semaphore()

    def greet(i, carry):
        pl.semaphore_signal(barrier, inc=1, device_id=target(lax.rem(b + i, BATCH), h), device_id_type=MESH)
        return carry

    lax.fori_loop(1, BATCH, greet, 0)
    for i in range(1, HIDDEN):
        pl.semaphore_signal(barrier, inc=1, device_id=target(b, lax.rem(h + i, HIDDEN)), device_id_type=MESH)
    id_turned[...] = jnp.concatenate([req[...]] * 4, 0).T
    id_send[...] = id_turned[pl.ds(h, BATCH, stride=HIDDEN), :]
    pl.semaphore_wait(barrier, BATCH - 1 + HIDDEN - 1)

    def send_ids(i, carry):
        other = lax.rem(b + i, BATCH)
        remote(id_send.at[pl.ds(other, 1)], id_recv.at[pl.ds(b, 1)], id_ssem, id_rsem, other, h).start()
        return carry

    lax.fori_loop(1, BATCH, send_ids, 0)
    spots = (
        pl.ds(pl.multiple_of(core * 128 + x * 32, 32), 32),
        pl.ds(pl.multiple_of(256 + core * 128 + z * 32, 32), 32),
    )
    spans = (pl.ds(pl.multiple_of(core * 128, 128), 128), pl.ds(pl.multiple_of(256 + core * 128, 128), 128))
    half = pl.ds(pl.multiple_of(core * 256, 256), 256)
    order = (1, 3, 2)
    y_copies, wo_copies, cot_copies = {}, {}, {}
    for i in order:
        other = lax.rem(h + i, HIDDEN)
        y_copies[i] = [
            remote(win.at[spots[p]], win_all.at[h, spots[p]], y_send.at[i - 1, p], y_recv.at[i - 1, p], b, other)
            for p in range(2)
        ]
        wo_copies[i] = remote(wout.at[half], wout_all.at[h, half], wo_send.at[i - 1], wo_recv.at[i - 1], b, other)
        cot_copies[i] = remote(cot, cot_all.at[h], cot_send.at[i - 1], cot_recv.at[i - 1], b, other)
    for i in order:
        for copy in y_copies[i]:
            copy.start()
    for i in order:
        cot_copies[i].start()
        wo_copies[i].start()
    cot_all[pl.ds(h, 1)] = cot[...].reshape(1, TASKS, 128)
    p_copies = {}

    def spread(i):
        source = lax.rem(h - i + HIDDEN, HIDDEN)
        p_copies[i] = []
        for p in range(2):
            y_copies[i][p].wait_recv()
            block = win_all.at[source, spots[p]]
            for j in range(1, 4):
                if p == 0:
                    other = z * 8 + lax.rem(x + j, 4) * 2 + core
                else:
                    other = lax.rem(z + j, 4) * 8 + x * 2 + core
                copy = remote(block, block, p_send.at[i - 1, p, j - 1], p_recv.at[i - 1, p, j - 1], other, h)
                copy.start()
                p_copies[i].append(copy)

    c_copies = {}

    def to_core(i):
        source = lax.rem(h - i + HIDDEN, HIDDEN)
        for copy in p_copies[i]:
            copy.wait_recv()
        c_copies[i] = []
        for p in range(2):
            block = win_all.at[source, spans[p]]
            copy = remote(block, block, c_send.at[i - 1, p], c_recv.at[i - 1, p], sibling, h)
            copy.start()
            c_copies[i].append(copy)

    woc_copies = {}

    def out_to_core(i):
        source = lax.rem(h - i + HIDDEN, HIDDEN)
        wo_copies[i].wait_recv()
        block = wout_all.at[source, half]
        woc_copies[i] = remote(block, block, woc_send.at[i - 1], woc_recv.at[i - 1], sibling, h)
        woc_copies[i].start()

    locals_in[0].wait()
    high, low = split(tab_value[...])
    tab_split[0:EMBED, :] = high
    tab_split[EMBED : 2 * EMBED, :] = low
    id_recv[pl.ds(b, 1), :] = id_send[pl.ds(b, 1), :]
    bulk_wait(id_recv.at[pl.ds(0, BATCH - 1)], id_rsem)
    spread(1)
    ids = ids_by_query(id_recv[...])
    table, row = ids // ROWS, lax.rem(ids, ROWS)
    found = []
    for pair in range(4):
        hot = jnp.concatenate([hot_of(row[j : j + 1, :], ROWS) for j in (2 * pair, 2 * pair + 1)], 1)
        value = dot_nn(tab_split[...], hot)
        for part in range(2):
            wanted = table[2 * pair + part : 2 * pair + part + 1, :]
            entry = jnp.zeros((ENTRY, 128), f32)
            for t in range(TABLES):
                block = value[t * ENTRY : (t + 1) * ENTRY, part * 128 : part * 128 + 128]
                rest = value[EMBED + t * ENTRY : EMBED + (t + 1) * ENTRY, part * 128 : part * 128 + 128]
                entry = jnp.where(wanted == t, block + rest, entry)
            found.append(entry)
    turned = jnp.concatenate(found, 0).T
    for q in range(4):
        row_send[pl.ds(q, BATCH, stride=4), :] = turned[q * 32 : q * 32 + 32, :]
    mine = pl.ds(me * 4, 4)

    def send_rows(i, carry):
        other = lax.rem(me + i, DEVICES)
        group = other // HIDDEN
        remote(
            row_send.at[pl.ds(group * 4, 4)], rows.at[mine], row_ssem, row_rsem, group, lax.rem(other, HIDDEN)
        ).start()
        return carry

    lax.fori_loop(1, DEVICES, send_rows, 0)
    rows[mine, :] = row_send[pl.ds(b * 4, 4), :]
    spread(3)
    spread(2)
    locals_in[1].wait()
    locals_in[2].wait()
    dense_pad[...] = jnp.zeros_like(dense_pad)
    dense_pad[0:DENSE, :] = dense[...]
    weight_pad[...] = jnp.zeros_like(weight_pad)
    weight_pad[0:DENSE, 0:PROJ] = dense_weight[...]
    head_pad[...] = jnp.zeros_like(head_pad)
    head_pad[0:TASKS, 0:TOWER] = head[...]
    dense_split = split(dense_pad[...])
    projected = dot3_nn(split(weight_pad[...].T), dense_split)
    high, low = split(projected[0:PROJ, :])
    feat_h[EMBED:WIDTH, :] = high
    feat_l[EMBED:WIDTH, :] = low
    head_turned = head_pad[...].T
    tower_turned = split(tower_weight[...].T)
    gate_split = split(gate_weight[...])
    wh[h], wl[h] = split(win_all[h])
    to_core(1)
    bulk_wait(rows.at[pl.ds(0, (DEVICES - 1) * 4)], row_rsem)
    for q in range(4):
        high, low = split(rows[pl.ds(q, DEVICES, stride=4), :].T)
        lists[0:128, q * 128 : q * 128 + 128] = high
        lists[128:256, q * 128 : q * 128 + 128] = low

    def gather(t, carry):
        slot = slots[pl.ds(t, 1), :]
        low = lax.rem(slot, 8)
        value = dot_nn(lists[...], hot_of(lax.rem(slot, 32) // 8 * 128 + slot // 32, 512))
        high_sum = jnp.zeros((ENTRY, EXAMPLES), f32)
        low_sum = jnp.zeros((ENTRY, EXAMPLES), f32)
        for j in range(8):
            high_sum = jnp.where(low == j, value[j * 16 : j * 16 + 16, :], high_sum)
            low_sum = jnp.where(low == j, value[128 + j * 16 : 128 + j * 16 + 16, :], low_sum)
        at = pl.ds(pl.multiple_of(t * ENTRY, ENTRY), ENTRY)
        feat_h[at, :] = high_sum.astype(bf16)
        feat_l[at, :] = low_sum.astype(bf16)
        return carry

    lax.fori_loop(0, TABLES, gather, 0, unroll=2)
    to_core(3)
    to_core(2)
    for i in order:
        out_to_core(i)
    feat = (feat_h[...], feat_l[...])
    logits = dot3_nn(gate_split, feat)
    for k in range(TASKS):
        part = logits[k * 8 : k * 8 + 8, :]
        raised = jnp.exp(part - jnp.max(part, axis=0, keepdims=True))
        gates[k * 8 : k * 8 + 8, :] = raised / jnp.sum(raised, axis=0, keepdims=True)

    def first_layer(s):
        inner, slope[s] = silu_both(dot3_nn((wh[s], wl[s]), (feat_h[...], feat_l[...])))
        inner_h[s], inner_l[s] = split(inner)

    first_layer(h)
    for i in order:
        source = lax.rem(h - i + HIDDEN, HIDDEN)
        for copy in c_copies[i]:
            copy.wait_recv()
        wh[source], wl[source] = split(win_all[source])
        first_layer(source)
    for i in order:
        woc_copies[i].wait_recv()
        cot_copies[i].wait_recv()
    for e in range(EXPERTS):
        at = pl.ds(e * UNITS, UNITS)
        value = jnp.concatenate([wout_all[s, at, :] for s in range(HIDDEN)], 0)
        oh[e], ol[e] = split(value)
        oth[e], otl[e] = split(value.T)
    mixed[...] = jnp.zeros_like(mixed)
    for e in range(EXPERTS):
        at = pl.ds(e * UNITS, UNITS)
        inner = tuple(jnp.concatenate([ref[s, at, :] for s in range(HIDDEN)], 0) for ref in (inner_h, inner_l))
        outputs, eslope[e] = silu_both(dot3_nn((oth[e], otl[e]), inner))
        eo[e] = outputs
        for k in range(TASKS):
            mixed[k] = mixed[k] + gates[k * 8 + e : k * 8 + e + 1, :] * outputs
    tower_grads, score_grads, tower_list = [], [], []
    for k in range(TASKS):
        at = slice(k * TOWER, (k + 1) * TOWER)
        mixed_split = split(mixed[k])
        towers, tower_slope = silu_both(dot3_nn(split(tower_weight[at, :]), mixed_split))
        column = jnp.broadcast_to(head_turned[0:TOWER, k : k + 1], (TOWER, EXAMPLES))
        predicted = sigmoid(jnp.sum(towers * column, axis=0, keepdims=True))
        pred[k : k + 1, :] = predicted
        pred_out[k : k + 1, :] = pred[k : k + 1, pl.ds(pl.multiple_of(h * 128, 128), 128)]
        cotangent = jnp.concatenate([cot_all[i, k : k + 1, :] for i in range(HIDDEN)], 1)
        score = cotangent * predicted * (1.0 - predicted)
        pre_grad = score * column * tower_slope
        sums[TOWER_AT + k * TOWER : TOWER_AT + (k + 1) * TOWER, :] = dot3_nt(split(pre_grad), mixed_split)
        tower_grads.append(pre_grad)
        score_grads.append(score)
        tower_list.append(towers)
    nothing = jnp.zeros((TOWER, EXAMPLES), f32)
    mixed_grad[0] = dot3_nn(tower_turned, split(jnp.concatenate([tower_grads[0], nothing], 0)))
    mixed_grad[1] = dot3_nn(tower_turned, split(jnp.concatenate([nothing, tower_grads[1]], 0)))
    scores = jnp.concatenate(score_grads + [jnp.zeros((14, EXAMPLES), f32)], 0)
    head_rows = dot3_nt(split(scores), split(jnp.concatenate(tower_list, 0)))
    sums[HEAD_AT:SUMMED, :] = jnp.zeros((SUMMED - HEAD_AT, 128), f32)
    sums[HEAD_AT : HEAD_AT + 1, :] = jnp.where(iota((1, 128), 1) < TOWER, head_rows[0:1, :], head_rows[1:2, :])
    for e in range(EXPERTS):
        at = pl.ds(e * UNITS, UNITS)
        outputs = eo[e]
        grad = jnp.zeros((OUT, EXAMPLES), f32)
        for k in range(TASKS):
            gate_slope[k * 8 + e : k * 8 + e + 1, :] = jnp.sum(mixed_grad[k] * outputs, axis=0, keepdims=True)
            grad = grad + gates[k * 8 + e : k * 8 + e + 1, :] * mixed_grad[k]
        out_split = split(grad * eslope[e])
        ep_h[e], ep_l[e] = out_split
        inner_grad = dot3_nn((oh[e], ol[e]), out_split)
        for s in range(HIDDEN):
            ig_h[s, at, :], ig_l[s, at, :] = split(inner_grad[s * UNITS : (s + 1) * UNITS, :] * slope[s, at, :])
    in_grad = dot3_nt((ig_h[h], ig_l[h]), feat)
    for q in range(4):
        sums[q * 512 : (q + 1) * 512, :] = in_grad[:, q * 128 : (q + 1) * 128]
    for e in range(EXPERTS):
        at = pl.ds(e * UNITS, UNITS)
        sums[OUT_AT + e * UNITS : OUT_AT + (e + 1) * UNITS, :] = dot3_nt(
            (inner_h[h, at, :], inner_l[h, at, :]), (ep_h[e], ep_l[e])
        )
    logit_grads = []
    for k in range(TASKS):
        gate, slopes = gates[k * 8 : k * 8 + 8, :], gate_slope[k * 8 : k * 8 + 8, :]
        logit_grads.append(gate * (slopes - jnp.sum(gate * slopes, axis=0, keepdims=True)))
    lgh, lgl = split(jnp.concatenate(logit_grads, 0))
    gate_grad = dot3_nt((lgh, lgl), feat)
    for q in range(4):
        sums[GATE_AT + q * 16 : GATE_AT + q * 16 + 16, :] = gate_grad[:, q * 128 : (q + 1) * 128]
    for s in range(HIDDEN):
        wth[s], wtl[s] = split(win_all[s].T)
    turned_h = jnp.concatenate([wth[s] for s in range(HIDDEN)], 1)
    turned_l = jnp.concatenate([wtl[s] for s in range(HIDDEN)], 1)
    ig_split = tuple(jnp.concatenate([ref[s] for s in range(HIDDEN)], 0) for ref in (ig_h, ig_l))
    fg[...] = dot3_nn((turned_h, turned_l), ig_split)
    gh, gl = (part.astype(f32) for part in gate_split)
    stacked = jnp.concatenate([gh, gl, gh, jnp.zeros((80, WIDTH), f32)], 0).T.astype(bf16)
    fg[...] += dot_nn(stacked, jnp.concatenate([lgh, lgh, lgl, jnp.zeros((80, EXAMPLES), bf16)], 0))
    projected_grad = split(jnp.concatenate([fg[EMBED:WIDTH, :], jnp.zeros((32, EXAMPLES), f32)], 0))
    dense_grad_out[...] = dot3_nn(split(weight_pad[...]), projected_grad)[0:DENSE, :]
    sums[DENSE_AT : DENSE_AT + 16, :] = dot3_nt(dense_split, projected_grad)[0:16, :]
    own_half = pl.ds(pl.multiple_of(core * HALF, HALF), HALF)
    other_half = pl.ds(pl.multiple_of((1 - core) * HALF, HALF), HALF)
    swap = remote(sums.at[other_half], from_core, swap_send, swap_recv, sibling, h)
    swap.start()
    swap.wait()
    reduced[...] = sums[own_half, :] + from_core[...]

    def send_pieces(i, carry):
        other = lax.rem(chip + i, 16)
        remote(
            reduced.at[pl.ds(pl.multiple_of(other * PIECE, 8), PIECE)],
            pieces.at[pl.ds(pl.multiple_of(chip * PIECE, 8), PIECE)],
            piece_ssem, piece_rsem, other * 2 + core, h,
        ).start()
        return carry

    lax.fori_loop(1, 16, send_pieces, 0)
    own = pl.ds(pl.multiple_of(chip * PIECE, 8), PIECE)
    pieces[own, :] = reduced[own, :]
    slot_sum[...] = jnp.zeros_like(slot_sum)

    def scatter(pair, carry):
        hots, spreads = [], []
        for part in range(2):
            t = 2 * pair + part
            slot = slots[pl.ds(t, 1), :]
            owner, low = slot // 32, lax.rem(slot, 8)
            code = jnp.where(lax.rem(owner, HIDDEN) == h, lax.rem(slot, 32) // 8 * 32 + owner // HIDDEN, -1)
            hots.append(hot_of(code, 128))
            grad = fg[pl.ds(pl.multiple_of(t * ENTRY, ENTRY), ENTRY), :]
            high = grad.astype(bf16).astype(f32)
            rest = grad - high
            chosen = [jnp.where(low == j, value, 0.0) for value in (high, rest) for j in range(8)]
            spreads.append(jnp.concatenate(chosen, 0).astype(bf16))
        slot_sum[...] += dot_nt(jnp.concatenate(hots, 1), jnp.concatenate(spreads, 1))
        return carry

    lax.fori_loop(0, TABLES // 2, scatter, 0)
    for q in range(4):
        at = slice(q * 32, q * 32 + 32)
        message[pl.ds(q, BATCH, stride=4), :] = slot_sum[at, 0:128] + slot_sum[at, 128:256]

    def send_slots(i, carry):
        other = lax.rem(b + i, BATCH)
        remote(message.at[pl.ds(other * 4, 4)], got.at[pl.ds(b * 4, 4)], slot_ssem, slot_rsem, other, h).start()
        return carry

    lax.fori_loop(1, BATCH, send_slots, 0)
    got[pl.ds(b * 4, 4), :] = message[pl.ds(b * 4, 4), :]
    bulk_wait(pieces.at[pl.ds(0, 15 * PIECE)], piece_rsem)
    value = pieces[0:PIECE, :]
    for i in range(1, 16):
        value = value + pieces[i * PIECE : (i + 1) * PIECE, :]
    place_of = pl.ds(pl.multiple_of(core * HALF + chip * PIECE, 8), PIECE)
    total[place_of, :] = value

    def send_full(i, carry):
        other = lax.rem(chip + i, 16)
        remote(total.at[place_of], total.at[place_of], full_ssem, full_recv.at[i], other * 2 + core, h).start()
        return carry

    lax.fori_loop(1, 16, send_full, 0)
    remote(total.at[place_of], total.at[place_of], last_ssem, last_rsem, sibling, h).start()
    bulk_wait(got.at[pl.ds(0, (BATCH - 1) * 4)], slot_rsem)
    turned = jnp.concatenate([got[pl.ds(q, BATCH, stride=4), :] for q in range(4)], 0).T
    high = turned.astype(bf16).astype(f32)
    rest = turned - high
    spreads = []
    for j in range(8):
        chosen = [
            jnp.where(table[j : j + 1, :] == t, value[j * 16 : j * 16 + 16, :], 0.0)
            for value in (high, rest)
            for t in range(TABLES)
        ]
        spreads.append(jnp.concatenate(chosen, 0).astype(bf16))
    spreads = jnp.concatenate(spreads, 1)
    hots = jnp.concatenate([hot_of(row[j : j + 1, :], ROWS) for j in range(8)], 1)
    for part in range(4):
        both = dot_nt(spreads, hots[part * 256 : (part + 1) * 256, :])
        table_grad[:, part * 256 : (part + 1) * 256] = both[0:EMBED, :] + both[EMBED : 2 * EMBED, :]
    store = pltpu.make_async_copy(table_grad, table_out, local_sem.at[3])
    store.start()

    def hand_on(i, carry):
        source = lax.rem(chip - i + 16, 16)
        at = pl.ds(pl.multiple_of(core * HALF + source * PIECE, 8), PIECE)
        pltpu.make_async_copy(total.at[at], total.at[at], full_recv.at[i]).wait()
        remote(total.at[at], total.at[at], last_ssem, last_rsem, sibling, h).start()
        return carry

    lax.fori_loop(1, 16, hand_on, 0)
    bulk_wait(total.at[pl.ds(0, HALF)], last_rsem)
    bulk_wait(total.at[pl.ds(0, HALF)], last_ssem)
    bulk_wait(total.at[pl.ds(0, 15 * PIECE)], full_ssem)
    bulk_wait(pieces.at[pl.ds(0, 15 * PIECE)], piece_ssem)
    bulk_wait(message.at[pl.ds(0, (BATCH - 1) * 4)], slot_ssem)
    bulk_wait(rows.at[pl.ds(0, (DEVICES - 1) * 4)], row_ssem)
    bulk_wait(id_send.at[pl.ds(0, BATCH - 1)], id_ssem)
    for i in order:
        for copy in (*y_copies[i], *p_copies[i], *c_copies[i], wo_copies[i], woc_copies[i], cot_copies[i]):
            copy.wait_send()
    store.wait()


def write_kernel(table, total, pred, dense_grad, *outs):
    table_out, in_out, out_out, gate_out, tower_out, weight_out, head_out, pred_out, dense_out = outs
    table_out[...] = table[...]
    pred_out[...] = pred[...]
    dense_out[...] = dense_grad[...]
    for q in range(4):
        at = slice(q * 128, q * 128 + 128)
        in_out[:, at] = total[q * 512 : q * 512 + 512, :]
        gate_out[:, at] = total[GATE_AT + q * 16 : GATE_AT + q * 16 + 16, :]
    out_out[...] = total[OUT_AT:GATE_AT, :]
    tower_out[...] = total[TOWER_AT:DENSE_AT, :]
    weight_out[...] = total[DENSE_AT : DENSE_AT + DENSE, 0:PROJ]
    head_out[0:1, :] = total[HEAD_AT : HEAD_AT + 1, 0:TOWER]
    head_out[1:2, :] = total[HEAD_AT : HEAD_AT + 1, TOWER : 2 * TOWER]


def on_device(
    tables, dense, dense_weight, expert_in, expert_out, gate_weight, tower_weight, head_weight, slots, requests, pred_cot
):
    i32 = jnp.int32
    dma = pltpu.SemaphoreType.DMA
    vmem = pltpu.VMEM
    anywhere = pl.BlockSpec(memory_space=pl.ANY)
    arrays = (
        requests[0].T,
        tables.transpose(0, 2, 1).reshape(EMBED, ROWS),
        expert_in.transpose(1, 2, 0).reshape(EXPERTS * UNITS, WIDTH),
        expert_out.reshape(EXPERTS * UNITS, OUT),
        pred_cot.T,
        slots.T,
        dense.T,
        dense_weight,
        gate_weight.transpose(0, 2, 1).reshape(TASKS * EXPERTS, WIDTH),
        tower_weight.transpose(0, 2, 1).reshape(TASKS * TOWER, OUT),
        head_weight,
    )
    shape = lambda *dims: jax.ShapeDtypeStruct(dims, f32)
    units = HIDDEN, 512, EXAMPLES
    outputs = EXPERTS, OUT, EXAMPLES
    pred, dense_grad, table_grad, total = pl.pallas_call(
        model_kernel,
        out_shape=[shape(TASKS, 128), shape(DENSE, EXAMPLES), shape(EMBED, ROWS), shape(SUMMED, 128)],
        in_specs=[VMEM, anywhere, anywhere, anywhere] + [VMEM] * 7,
        out_specs=[VMEM, VMEM, anywhere, VMEM],
        scratch_shapes=[
            vmem((128, 128), i32), vmem((32, 128), i32), vmem((32, 128), i32), vmem((128, 128), f32),
            vmem((512, 128), f32), vmem((EMBED, ROWS), f32), vmem((2 * EMBED, ROWS), bf16),
            vmem((HIDDEN, 512, WIDTH), f32), vmem((HIDDEN, 512, OUT), f32), vmem((HIDDEN, TASKS, 128), f32),
            vmem((HIDDEN, 512, WIDTH), bf16), vmem((HIDDEN, 512, WIDTH), bf16),
            vmem((HIDDEN, WIDTH, 512), bf16), vmem((HIDDEN, WIDTH, 512), bf16),
            vmem((EXPERTS, 256, OUT), bf16), vmem((EXPERTS, 256, OUT), bf16),
            vmem((EXPERTS, OUT, 256), bf16), vmem((EXPERTS, OUT, 256), bf16),
            vmem((256, 512), bf16), vmem((WIDTH, EXAMPLES), bf16), vmem((WIDTH, EXAMPLES), bf16),
            vmem((128, EXAMPLES), f32), vmem((128, 128), f32), vmem((128, 128), f32),
            vmem(units, bf16), vmem(units, bf16), vmem(units, f32), vmem(units, bf16), vmem(units, bf16),
            vmem(outputs, f32), vmem(outputs, f32), vmem(outputs, bf16), vmem(outputs, bf16),
            vmem((16, EXAMPLES), f32), vmem((16, EXAMPLES), f32),
            vmem((TASKS, OUT, EXAMPLES), f32), vmem((TASKS, OUT, EXAMPLES), f32), vmem((TASKS, EXAMPLES), f32),
            vmem((WIDTH, EXAMPLES), f32), vmem((128, 256), f32),
            vmem((SUMMED, 128), f32), vmem((128, 128), f32), vmem((128, 128), f32),
            vmem((HALF, 128), f32), vmem((HALF, 128), f32), vmem((HALF, 128), f32), vmem((EMBED, ROWS), f32),
            dma((3, 2)), dma((3, 2)), dma((3, 2, 3)), dma((3, 2, 3)), dma((3, 2)), dma((3, 2)),
            dma((3,)), dma((3,)), dma((3,)), dma((3,)), dma((3,)), dma((3,)),
            dma, dma, dma, dma, dma((4,)), dma, dma, dma, dma, dma, dma, dma, dma((16,)), dma, dma,
        ],
        compiler_params=pltpu.CompilerParams(vmem_limit_bytes=LIMIT, collective_id=0, has_side_effects=True),
        name="model",
    )(*arrays)
    table_grad, in_grad, out_grad, gate_grad, tower_grad, weight_grad, head_grad, pred, dense_grad = pl.pallas_call(
        write_kernel,
        out_shape=[
            shape(EMBED, ROWS), shape(512, WIDTH), shape(512, OUT), shape(TASKS * EXPERTS, WIDTH),
            shape(TASKS * TOWER, OUT), shape(DENSE, PROJ), shape(TASKS, TOWER), shape(TASKS, 128),
            shape(DENSE, EXAMPLES),
        ],
        in_specs=[VMEM] * 4,
        out_specs=[VMEM] * 9,
        compiler_params=pltpu.CompilerParams(vmem_limit_bytes=LIMIT),
        name="write",
    )(table_grad, total, pred, dense_grad)
    return (
        pred.T,
        dense_grad.T,
        table_grad.reshape(TABLES, ENTRY, ROWS).transpose(0, 2, 1),
        weight_grad,
        in_grad.reshape(EXPERTS, UNITS, WIDTH).transpose(2, 0, 1),
        out_grad.reshape(EXPERTS, UNITS, OUT),
        gate_grad.reshape(TASKS, EXPERTS, WIDTH).transpose(0, 2, 1),
        tower_grad.reshape(TASKS, TOWER, OUT).transpose(0, 2, 1),
        head_grad,
    )


def solution(mesh):
    placed = (
        P(None, ("batch", "hidden"), None),
        P("batch", None),
        P(),
        P(None, None, "hidden"),
        P(None, "hidden", None),
        P(),
        P(),
        P(),
        P("batch", None),
        P("batch", None, None),
        P(("batch", "hidden"), None),
    )
    return jax.shard_map(
        on_device,
        mesh=mesh,
        in_specs=placed,
        out_specs=(
            P(("batch", "hidden"), None),
            P("batch", None),
            P(None, ("batch", "hidden"), None),
            P(),
            P(None, None, "hidden"),
            P(None, "hidden", None),
            P(),
            P(),
            P(),
        ),
        check_vma=False,
    )
```

```python
import jax
import jax.numpy as jnp
from jax import lax
from jax.experimental import pallas as pl
from jax.experimental.pallas import tpu as pltpu
from jax.sharding import PartitionSpec as P

f32 = jnp.float32
bf16 = jnp.bfloat16
MESH = pl.DeviceIdType.MESH
VMEM = pl.BlockSpec(memory_space=pltpu.VMEM)
LIMIT = 56 * 2**20

TABLES, ROWS, ENTRY = 26, 1024, 16
BATCH, HIDDEN = 32, 4
DEVICES = BATCH * HIDDEN
EXPERTS, UNITS, OUT, WIDTH = 8, 64, 128, 512
TASKS, TOWER, DENSE, PROJ = 2, 64, 13, 96
EXAMPLES = 512
EMBED = TABLES * ENTRY

IN_ROWS, IN_PIECE = 2048, 64
OUT_AT, GATE_AT, TOWER_AT, HEAD_AT = 0, 512, 576, 704
REST_ROWS, REST_PIECE = 768, 24


def split(value):
    high = value.astype(bf16)
    return high, (value - high.astype(f32)).astype(bf16)


def dot_nn(a, b):
    return lax.dot_general(a, b, (((1,), (0,)), ((), ())), preferred_element_type=f32)


def dot_nt(a, b):
    return lax.dot_general(a, b, (((1,), (1,)), ((), ())), preferred_element_type=f32)


def dot3_nn(a, b):
    (ah, al), (bh, bl) = a, b
    return dot_nn(jnp.concatenate([ah, al, ah], 1), jnp.concatenate([bh, bh, bl], 0))


def dot3_nt(a, b):
    (ah, al), (bh, bl) = a, b
    return dot_nt(jnp.concatenate([ah, al, ah], 1), jnp.concatenate([bh, bh, bl], 1))


def sigmoid(value):
    return 0.5 * jnp.tanh(0.5 * value) + 0.5


def silu_both(value):
    sigma = sigmoid(value)
    result = value * sigma
    return result, sigma + result * (1.0 - sigma)


def iota(shape, axis):
    return lax.broadcasted_iota(jnp.int32, shape, axis)


def hops(offset):
    return min(offset, 4 - offset)


PLANE = sorted(
    ((dz, dx, dc) for dz in range(4) for dx in range(4) for dc in range(2) if dz or dx or dc),
    key=lambda d: -(2 * hops(d[0]) + 2 * hops(d[1]) + d[2]),
)
EVERYWHERE = sorted(
    ((dz, dx, dc, dy) for dz in range(4) for dx in range(4) for dc in range(2) for dy in range(4) if dz or dx or dc or dy),
    key=lambda d: -(2 * hops(d[0]) + 2 * hops(d[1]) + d[2] + 2 * hops(d[3])),
)
CHIPS = [(dz, dx) for dz, dx, dc in PLANE if not dc and (dz or dx)]


def target(b, h):
    return {"batch": b, "hidden": h}


def remote(src, dst, send, recv, b, h):
    return pltpu.make_async_remote_copy(src, dst, send, recv, device_id=target(b, h), device_id_type=MESH)


def bulk_wait(ref, sem):
    pltpu.make_async_copy(ref, ref, sem).wait()


def ids_by_query(received):
    turned = jnp.concatenate([received] * 4, 0).T
    lane = iota((8, 128), 1) // 32
    out = jnp.zeros((8, 128), jnp.int32)
    for q in range(4):
        out = jnp.where(lane == q, turned[q * 8 : q * 8 + 8, :], out)
    return out


def hot_of(code, count):
    rows = iota((count, code.shape[1]), 0).astype(jnp.int16)
    return jnp.where(rows == code.astype(jnp.int16), bf16(1.0), bf16(0.0))


def model_kernel(
    req_in, tab_in, win, wout, cot_in, slots_in, dense_in, dense_weight_in, gate_weight_in, tower_weight_in, head_in,
    pred_out, dense_grad_out, table_out, in_total, rest_total, weight_grad_out, head_grad_out,
    req, tab, cot, slots, dense, dense_weight, gate_weight, tower_weight, head,
    id_turned, id_send, id_recv, row_send, rows, tab_split, win_all, wout_all, cot_all,
    wh, wl, wth, wtl, oh, ol, oth, otl,
    lists, feat_h, feat_l, dense_pad, weight_pad, head_pad,
    inner_h, inner_l, slope, ig_h, ig_l, eo, eslope, ep_h, ep_l, gates, gate_slope, mixed, mixed_grad, pred, fg, slot_sum,
    in_sums, rest_sums, in_swap, rest_swap, in_pieces, rest_pieces, message, got, weight_part, weight_got,
    local_sem, y_send, y_recv, p_send, p_recv, c_send, c_recv, wo_send, wo_recv, woc_send, woc_recv, cot_send, cot_recv,
    id_ssem, id_rsem, row_ssem, row_rsem, slot_ssem, slot_rsem, weight_ssem, weight_rsem,
    swap_send, swap_recv, piece_ssem, piece_rsem, full_ssem, full_recv, last_ssem, last_rsem,
):
    b, h = lax.axis_index("batch"), lax.axis_index("hidden")
    core, x, z, chip = lax.rem(b, 2), lax.rem(b // 2, 4), b // 8, b // 2
    me = b * HIDDEN + h
    sibling = b + 1 - 2 * core
    zs = [lax.rem(z + d, 4) * 8 for d in range(4)]
    xs = [lax.rem(x + d, 4) * 2 for d in range(4)]
    cores = [core, 1 - core]
    hs = [lax.rem(h + d, HIDDEN) for d in range(HIDDEN)]
    chips = [(zs[dz] + xs[dx]) // 2 for dz, dx in CHIPS]
    plane = [zs[dz] + xs[dx] + cores[dc] for dz, dx, dc in PLANE]
    order = (1, 3, 2)

    def bring(source, home, i):
        copy = pltpu.make_async_copy(source, home, local_sem.at[i])
        copy.start()
        return copy

    req_copy = bring(req_in, req, 0)
    barrier = pltpu.get_barrier_semaphore()
    for other in plane:
        pl.semaphore_signal(barrier, inc=1, device_id=target(other, h), device_id_type=MESH)
    for i in (2, 1, 3):
        pl.semaphore_signal(barrier, inc=1, device_id=target(b, hs[i]), device_id_type=MESH)
    tab_copy = bring(tab_in, tab, 1)
    win_copy = bring(win, win_all.at[h], 2)
    wout_copy = bring(wout, wout_all.at[h], 3)
    small = ((cot_in, cot), (slots_in, slots), (dense_in, dense), (dense_weight_in, dense_weight),
             (gate_weight_in, gate_weight), (tower_weight_in, tower_weight), (head_in, head))
    small_copies = [bring(source, home, 4 + i) for i, (source, home) in enumerate(small)]
    req_copy.wait()
    id_turned[...] = jnp.concatenate([req[...]] * 4, 0).T
    id_send[...] = id_turned[pl.ds(h, BATCH, stride=HIDDEN), :]
    pl.semaphore_wait(barrier, BATCH - 1 + HIDDEN - 1)

    for other in plane:
        remote(id_send.at[pl.ds(other, 1)], id_recv.at[pl.ds(b, 1)], id_ssem, id_rsem, other, h).start()
    spots = (
        pl.ds(pl.multiple_of(core * 128 + x * 32, 32), 32),
        pl.ds(pl.multiple_of(256 + core * 128 + z * 32, 32), 32),
    )
    spans = (pl.ds(pl.multiple_of(core * 128, 128), 128), pl.ds(pl.multiple_of(256 + core * 128, 128), 128))
    half = pl.ds(pl.multiple_of(core * 256, 256), 256)
    source_of = [lax.rem(h - i + HIDDEN, HIDDEN) for i in range(HIDDEN)]
    y_copies, p_copies, c_copies, wo_copies, woc_copies, cot_copies = {}, {}, {}, {}, {}, {}
    for i in order:
        y_copies[i] = [
            remote(win.at[spots[p]], win_all.at[h, spots[p]], y_send.at[i - 1, p], y_recv.at[i - 1, p], b, hs[i])
            for p in range(2)
        ]
        for copy in y_copies[i]:
            copy.start()

    def spread(i):
        p_copies[i] = []
        for p in range(2):
            y_copies[i][p].wait_recv()
        for j in (2, 1, 3):
            for p in range(2):
                block = win_all.at[source_of[i], spots[p]]
                other = z * 8 + xs[j] + core if p == 0 else zs[j] + x * 2 + core
                copy = remote(block, block, p_send.at[i - 1, p, j - 1], p_recv.at[i - 1, p, j - 1], other, h)
                copy.start()
                p_copies[i].append(copy)

    def to_core(i):
        for copy in p_copies[i]:
            copy.wait_recv()
        c_copies[i] = []
        for p in range(2):
            block = win_all.at[source_of[i], spans[p]]
            copy = remote(block, block, c_send.at[i - 1, p], c_recv.at[i - 1, p], sibling, h)
            copy.start()
            c_copies[i].append(copy)

    def out_to_core(i):
        wo_copies[i].wait_recv()
        block = wout_all.at[source_of[i], half]
        woc_copies[i] = remote(block, block, woc_send.at[i - 1], woc_recv.at[i - 1], sibling, h)
        woc_copies[i].start()

    tab_copy.wait()
    high, low = split(tab[...])
    tab_split[0:EMBED, :] = high
    tab_split[EMBED : 2 * EMBED, :] = low
    id_recv[pl.ds(b, 1), :] = id_send[pl.ds(b, 1), :]
    bulk_wait(id_recv.at[pl.ds(0, BATCH - 1)], id_rsem)
    ids = ids_by_query(id_recv[...])
    table, row = ids // ROWS, lax.rem(ids, ROWS)
    found = []
    for pair in range(4):
        hot = jnp.concatenate([hot_of(row[j : j + 1, :], ROWS) for j in (2 * pair, 2 * pair + 1)], 1)
        value = dot_nn(tab_split[...], hot)
        for part in range(2):
            wanted = table[2 * pair + part : 2 * pair + part + 1, :]
            entry = jnp.zeros((ENTRY, 128), f32)
            for t in range(TABLES):
                block = value[t * ENTRY : (t + 1) * ENTRY, part * 128 : part * 128 + 128]
                rest = value[EMBED + t * ENTRY : EMBED + (t + 1) * ENTRY, part * 128 : part * 128 + 128]
                entry = jnp.where(wanted == t, block + rest, entry)
            found.append(entry)
    turned = jnp.concatenate(found, 0).T
    for q in range(4):
        row_send[pl.ds(q, BATCH, stride=4), :] = turned[q * 32 : q * 32 + 32, :]
    mine = pl.ds(me * 4, 4)
    for dz, dx, dc, dy in EVERYWHERE:
        group = zs[dz] + xs[dx] + cores[dc]
        remote(row_send.at[pl.ds(group * 4, 4)], rows.at[mine], row_ssem, row_rsem, group, hs[dy]).start()
    rows[mine, :] = row_send[pl.ds(b * 4, 4), :]
    for i in order:
        spread(i)
    for copy in small_copies:
        copy.wait()
    wout_copy.wait()
    for i in order:
        cot_copies[i] = remote(cot, cot_all.at[h], cot_send.at[i - 1], cot_recv.at[i - 1], b, hs[i])
        cot_copies[i].start()
        wo_copies[i] = remote(
            wout_all.at[h, half], wout_all.at[h, half], wo_send.at[i - 1], wo_recv.at[i - 1], b, hs[i]
        )
        wo_copies[i].start()
    cot_all[pl.ds(h, 1)] = cot[...].reshape(1, TASKS, 128)
    dense_pad[...] = jnp.zeros_like(dense_pad)
    dense_pad[0:DENSE, :] = dense[...]
    weight_pad[...] = jnp.zeros_like(weight_pad)
    weight_pad[0:DENSE, 0:PROJ] = dense_weight[...]
    head_pad[...] = jnp.zeros_like(head_pad)
    head_pad[0:TASKS, 0:TOWER] = head[...]
    dense_split = split(dense_pad[...])
    projected = dot3_nn(split(weight_pad[...].T), dense_split)
    high, low = split(projected[0:PROJ, :])
    feat_h[EMBED:WIDTH, :] = high
    feat_l[EMBED:WIDTH, :] = low
    head_turned = head_pad[...].T
    tower_turned = split(tower_weight[...].T)
    gate_split = split(gate_weight[...])
    win_copy.wait()
    wh[h], wl[h] = split(win_all[h])
    wth[h], wtl[h] = split(win_all[h].T)
    bulk_wait(rows.at[pl.ds(0, (DEVICES - 1) * 4)], row_rsem)
    for q in range(4):
        high, low = split(rows[pl.ds(q, DEVICES, stride=4), :].T)
        lists[0:128, q * 128 : q * 128 + 128] = high
        lists[128:256, q * 128 : q * 128 + 128] = low

    def gather(t):
        slot = slots[t : t + 1, :]
        low = lax.rem(slot, 8)
        value = dot_nn(lists[...], hot_of(lax.rem(slot, 32) // 8 * 128 + slot // 32, 512))
        high_sum = jnp.zeros((ENTRY, EXAMPLES), f32)
        low_sum = jnp.zeros((ENTRY, EXAMPLES), f32)
        for j in range(8):
            high_sum = jnp.where(low == j, value[j * 16 : j * 16 + 16, :], high_sum)
            low_sum = jnp.where(low == j, value[128 + j * 16 : 128 + j * 16 + 16, :], low_sum)
        feat_h[t * ENTRY : (t + 1) * ENTRY, :] = high_sum.astype(bf16)
        feat_l[t * ENTRY : (t + 1) * ENTRY, :] = low_sum.astype(bf16)

    for t in range(TABLES // 2):
        gather(t)
    to_core(1)
    for t in range(TABLES // 2, TABLES):
        gather(t)
    to_core(3)

    def first_layer(s):
        inner, slope[s] = silu_both(dot3_nn((wh[s], wl[s]), (feat_h[...], feat_l[...])))
        inner_h[s], inner_l[s] = split(inner)

    def next_layer(i):
        s = source_of[i]
        for copy in c_copies[i]:
            copy.wait_recv()
        wh[s], wl[s] = split(win_all[s])
        first_layer(s)

    first_layer(h)
    to_core(2)
    next_layer(1)
    for i in order:
        out_to_core(i)
    next_layer(3)
    next_layer(2)
    feat = (feat_h[...], feat_l[...])
    logits = dot3_nn(gate_split, feat)
    for k in range(TASKS):
        part = logits[k * 8 : k * 8 + 8, :]
        raised = jnp.exp(part - jnp.max(part, axis=0, keepdims=True))
        gates[k * 8 : k * 8 + 8, :] = raised / jnp.sum(raised, axis=0, keepdims=True)
    for i in order:
        woc_copies[i].wait_recv()
        cot_copies[i].wait_recv()
    for e in range(EXPERTS):
        at = pl.ds(e * UNITS, UNITS)
        value = jnp.concatenate([wout_all[s, at, :] for s in range(HIDDEN)], 0)
        oh[e], ol[e] = split(value)
        oth[e], otl[e] = split(value.T)
    mixed[...] = jnp.zeros_like(mixed)
    for e in range(EXPERTS):
        at = pl.ds(e * UNITS, UNITS)
        inner = tuple(jnp.concatenate([ref[s, at, :] for s in range(HIDDEN)], 0) for ref in (inner_h, inner_l))
        outputs, eslope[e] = silu_both(dot3_nn((oth[e], otl[e]), inner))
        eo[e] = outputs
        for k in range(TASKS):
            mixed[k] = mixed[k] + gates[k * 8 + e : k * 8 + e + 1, :] * outputs
    pre_grads, scores, tower_list = [], [], []
    for k in range(TASKS):
        at = slice(k * TOWER, (k + 1) * TOWER)
        towers, tower_slope = silu_both(dot3_nn(split(tower_weight[at, :]), split(mixed[k])))
        column = jnp.broadcast_to(head_turned[0:TOWER, k : k + 1], (TOWER, EXAMPLES))
        predicted = sigmoid(jnp.sum(towers * column, axis=0, keepdims=True))
        pred[k : k + 1, :] = predicted
        cotangent = jnp.concatenate([cot_all[i, k : k + 1, :] for i in range(HIDDEN)], 1)
        score = cotangent * predicted * (1.0 - predicted)
        pre_grads.append(score * column * tower_slope)
        scores.append(score)
        tower_list.append(towers)
    nothing = jnp.zeros((TOWER, EXAMPLES), f32)
    mixed_grad[0] = dot3_nn(tower_turned, split(jnp.concatenate([pre_grads[0], nothing], 0)))
    mixed_grad[1] = dot3_nn(tower_turned, split(jnp.concatenate([nothing, pre_grads[1]], 0)))
    for e in range(EXPERTS):
        at = pl.ds(e * UNITS, UNITS)
        outputs = eo[e]
        grad = jnp.zeros((OUT, EXAMPLES), f32)
        for k in range(TASKS):
            gate_slope[k * 8 + e : k * 8 + e + 1, :] = jnp.sum(mixed_grad[k] * outputs, axis=0, keepdims=True)
            grad = grad + gates[k * 8 + e : k * 8 + e + 1, :] * mixed_grad[k]
        out_split = split(grad * eslope[e])
        ep_h[e], ep_l[e] = out_split
        inner_grad = dot3_nn((oh[e], ol[e]), out_split)
        for s in range(HIDDEN):
            ig_h[s, at, :], ig_l[s, at, :] = split(inner_grad[s * UNITS : (s + 1) * UNITS, :] * slope[s, at, :])
    in_grad = dot3_nt((ig_h[h], ig_l[h]), feat)
    for q in range(4):
        in_sums[q * 512 : (q + 1) * 512, :] = in_grad[:, q * 128 : (q + 1) * 128]

    parts = ((in_sums, in_swap, in_pieces, in_total, IN_PIECE), (rest_sums, rest_swap, rest_pieces, rest_total, REST_PIECE))

    def swap(n):
        sums, swapped, _, _, piece = parts[n]
        half_rows = 16 * piece
        copy = remote(
            sums.at[pl.ds(pl.multiple_of((1 - core) * half_rows, 8), half_rows)], swapped,
            swap_send.at[n], swap_recv.at[n], sibling, h,
        )
        copy.start()
        return copy

    def send_pieces(n, copy):
        sums, swapped, pieces, _, piece = parts[n]
        half_rows = 16 * piece
        copy.wait_recv()
        swapped[...] += sums[pl.ds(pl.multiple_of(core * half_rows, 8), half_rows), :]
        own = pl.ds(pl.multiple_of(chip * piece, 8), piece)
        for other in chips:
            remote(
                swapped.at[pl.ds(pl.multiple_of(other * piece, 8), piece)], pieces.at[own],
                piece_ssem.at[n], piece_rsem.at[n], other * 2 + core, h,
            ).start()
        pieces[own, :] = swapped[own, :]

    def send_sums(n):
        _, _, pieces, total, piece = parts[n]
        half_rows = 16 * piece
        bulk_wait(pieces.at[pl.ds(0, 15 * piece)], piece_rsem.at[n])
        value = pieces[0:piece, :]
        for i in range(1, 16):
            value = value + pieces[i * piece : (i + 1) * piece, :]
        at = pl.ds(pl.multiple_of(core * half_rows + chip * piece, 8), piece)
        total[at, :] = value
        for i, other in enumerate(chips):
            remote(total.at[at], total.at[at], full_ssem.at[n], full_recv.at[n, i], other * 2 + core, h).start()
        remote(total.at[at], total.at[at], last_ssem.at[n], last_rsem.at[n], sibling, h).start()

    def hand_on(n):
        _, _, _, total, piece = parts[n]
        for i, (dz, dx) in reversed(list(enumerate(CHIPS))):
            source = (zs[(4 - dz) % 4] + xs[(4 - dx) % 4]) // 2
            at = pl.ds(pl.multiple_of(core * 16 * piece + source * piece, 8), piece)
            bulk_wait(total.at[at], full_recv.at[n, i])
            remote(total.at[at], total.at[at], last_ssem.at[n], last_rsem.at[n], sibling, h).start()

    in_copy = swap(0)
    tower_splits = [split(grad) for grad in pre_grads]
    for k in range(TASKS):
        rest_sums[TOWER_AT + k * TOWER : TOWER_AT + (k + 1) * TOWER, :] = dot3_nt(tower_splits[k], split(mixed[k]))
    score_rows = jnp.concatenate(scores + [jnp.zeros((14, EXAMPLES), f32)], 0)
    head_rows = dot3_nt(split(score_rows), split(jnp.concatenate(tower_list, 0)))
    rest_sums[HEAD_AT:REST_ROWS, :] = jnp.zeros((REST_ROWS - HEAD_AT, 128), f32)
    rest_sums[HEAD_AT : HEAD_AT + 1, :] = jnp.where(iota((1, 128), 1) < TOWER, head_rows[0:1, :], head_rows[1:2, :])
    logit_grads = []
    for k in range(TASKS):
        gate, slopes = gates[k * 8 : k * 8 + 8, :], gate_slope[k * 8 : k * 8 + 8, :]
        logit_grads.append(gate * (slopes - jnp.sum(gate * slopes, axis=0, keepdims=True)))
    lgh, lgl = split(jnp.concatenate(logit_grads, 0))
    gate_grad = dot3_nt((lgh, lgl), feat)
    for q in range(4):
        rest_sums[GATE_AT + q * 16 : GATE_AT + q * 16 + 16, :] = gate_grad[:, q * 128 : (q + 1) * 128]
    send_pieces(0, in_copy)
    for e in range(EXPERTS):
        at = pl.ds(e * UNITS, UNITS)
        rest_sums[OUT_AT + e * UNITS : OUT_AT + (e + 1) * UNITS, :] = dot3_nt(
            (inner_h[h, at, :], inner_l[h, at, :]), (ep_h[e], ep_l[e])
        )
    rest_copy = swap(1)
    for k in range(TASKS):
        pred_out[k : k + 1, :] = pred[k : k + 1, pl.ds(pl.multiple_of(h * 128, 128), 128)]
    for i in order:
        s = source_of[i]
        wth[s], wtl[s] = split(win_all[s].T)
    send_pieces(1, rest_copy)
    turned_h = jnp.concatenate([wth[s] for s in range(HIDDEN)], 1)
    turned_l = jnp.concatenate([wtl[s] for s in range(HIDDEN)], 1)
    ig_split = tuple(jnp.concatenate([ref[s] for s in range(HIDDEN)], 0) for ref in (ig_h, ig_l))
    fg[...] = dot3_nn((turned_h, turned_l), ig_split)
    gh, gl = (part.astype(f32) for part in gate_split)
    stacked = jnp.concatenate([gh, gl, gh, jnp.zeros((80, WIDTH), f32)], 0).T.astype(bf16)
    fg[...] += dot_nn(stacked, jnp.concatenate([lgh, lgh, lgl, jnp.zeros((80, EXAMPLES), bf16)], 0))
    slot_sum[...] = jnp.zeros_like(slot_sum)

    def scatter(pair, carry):
        hots, spreads = [], []
        for part in range(2):
            t = 2 * pair + part
            slot = slots[pl.ds(t, 1), :]
            owner, low = slot // 32, lax.rem(slot, 8)
            code = jnp.where(lax.rem(owner, HIDDEN) == h, lax.rem(slot, 32) // 8 * 32 + owner // HIDDEN, -1)
            hots.append(hot_of(code, 128))
            grad = fg[pl.ds(pl.multiple_of(t * ENTRY, ENTRY), ENTRY), :]
            high = grad.astype(bf16).astype(f32)
            rest = grad - high
            chosen = [jnp.where(low == j, value, 0.0) for value in (high, rest) for j in range(8)]
            spreads.append(jnp.concatenate(chosen, 0).astype(bf16))
        slot_sum[...] += dot_nt(jnp.concatenate(hots, 1), jnp.concatenate(spreads, 1))
        return carry

    lax.fori_loop(0, TABLES // 2, scatter, 0)
    for q in range(4):
        at = slice(q * 32, q * 32 + 32)
        message[pl.ds(q, BATCH, stride=4), :] = slot_sum[at, 0:128] + slot_sum[at, 128:256]
    for other in plane:
        remote(message.at[pl.ds(other * 4, 4)], got.at[pl.ds(b * 4, 4)], slot_ssem, slot_rsem, other, h).start()
    got[pl.ds(b * 4, 4), :] = message[pl.ds(b * 4, 4), :]
    send_sums(0)
    projected_grad = split(jnp.concatenate([fg[EMBED:WIDTH, :], jnp.zeros((32, EXAMPLES), f32)], 0))
    dense_grad_out[...] = dot3_nn(split(weight_pad[...]), projected_grad)[0:DENSE, :]
    weight_part[...] = dot3_nt(dense_split, projected_grad)[0:16, :]
    weight_at = pl.ds(pl.multiple_of(b * 16, 16), 16)
    for other in plane:
        remote(weight_part, weight_got.at[weight_at], weight_ssem, weight_rsem, other, h).start()
    weight_got[weight_at, :] = weight_part[...]
    send_sums(1)
    bulk_wait(got.at[pl.ds(0, (BATCH - 1) * 4)], slot_rsem)
    turned = jnp.concatenate([got[pl.ds(q, BATCH, stride=4), :] for q in range(4)], 0).T
    high = turned.astype(bf16).astype(f32)
    rest = turned - high
    spreads = []
    for j in range(8):
        chosen = [
            jnp.where(table[j : j + 1, :] == t, value[j * 16 : j * 16 + 16, :], 0.0)
            for value in (high, rest)
            for t in range(TABLES)
        ]
        spreads.append(jnp.concatenate(chosen, 0).astype(bf16))
    spreads = jnp.concatenate(spreads, 1)
    hots = jnp.concatenate([hot_of(row[j : j + 1, :], ROWS) for j in range(8)], 1)
    for part in range(4):
        both = dot_nt(spreads, hots[part * 256 : (part + 1) * 256, :])
        table_out[:, part * 256 : (part + 1) * 256] = both[0:EMBED, :] + both[EMBED : 2 * EMBED, :]
    bulk_wait(weight_got.at[pl.ds(0, (BATCH - 1) * 16)], weight_rsem)
    value = weight_got[0:16, :]
    for i in range(1, BATCH):
        value = value + weight_got[i * 16 : i * 16 + 16, :]
    weight_grad_out[...] = value[0:DENSE, 0:PROJ]
    hand_on(1)
    hand_on(0)
    for n, (_, _, pieces, total, piece) in enumerate(parts):
        bulk_wait(total.at[pl.ds(0, 16 * piece)], last_rsem.at[n])
        if n == 1:
            head_grad_out[0:1, :] = total[HEAD_AT : HEAD_AT + 1, 0:TOWER]
            head_grad_out[1:2, :] = total[HEAD_AT : HEAD_AT + 1, TOWER : 2 * TOWER]
        bulk_wait(total.at[pl.ds(0, 16 * piece)], last_ssem.at[n])
        bulk_wait(total.at[pl.ds(0, 15 * piece)], full_ssem.at[n])
        bulk_wait(pieces.at[pl.ds(0, 15 * piece)], piece_ssem.at[n])
    in_copy.wait_send()
    rest_copy.wait_send()
    bulk_wait(weight_got.at[pl.ds(0, (BATCH - 1) * 16)], weight_ssem)
    bulk_wait(message.at[pl.ds(0, (BATCH - 1) * 4)], slot_ssem)
    bulk_wait(rows.at[pl.ds(0, (DEVICES - 1) * 4)], row_ssem)
    bulk_wait(id_send.at[pl.ds(0, BATCH - 1)], id_ssem)
    for i in order:
        for copy in (*y_copies[i], *p_copies[i], *c_copies[i], wo_copies[i], woc_copies[i], cot_copies[i]):
            copy.wait_send()


def write_kernel(
    table, in_total, rest_total, weight_grad, head_grad, pred, dense_grad,
    table_out, in_out, out_out, tower_out, gate_out, weight_out, head_out, pred_out, dense_out, sems,
):
    copies = [(table, table_out), (rest_total.at[OUT_AT:GATE_AT], out_out), (rest_total.at[TOWER_AT:HEAD_AT], tower_out)]
    copies += [(in_total.at[q * 512 : q * 512 + 512], in_out.at[:, q * 128 : q * 128 + 128]) for q in range(4)]
    copies += [
        (rest_total.at[GATE_AT + q * 16 : GATE_AT + q * 16 + 16], gate_out.at[:, q * 128 : q * 128 + 128])
        for q in range(4)
    ]
    copies += [(weight_grad, weight_out), (head_grad, head_out), (pred, pred_out), (dense_grad, dense_out)]
    copies = [pltpu.make_async_copy(source, home, sems.at[i]) for i, (source, home) in enumerate(copies)]
    for copy in copies:
        copy.start()
    for copy in copies:
        copy.wait()


def on_device(
    tables, dense, dense_weight, expert_in, expert_out, gate_weight, tower_weight, head_weight, slots, requests, pred_cot
):
    i32 = jnp.int32
    dma = pltpu.SemaphoreType.DMA
    vmem = pltpu.VMEM
    anywhere = pl.BlockSpec(memory_space=pl.ANY)
    arrays = (
        requests[0].T,
        tables.transpose(0, 2, 1).reshape(EMBED, ROWS),
        expert_in.transpose(1, 2, 0).reshape(EXPERTS * UNITS, WIDTH),
        expert_out.reshape(EXPERTS * UNITS, OUT),
        pred_cot.T,
        slots.T,
        dense.T,
        dense_weight,
        gate_weight.transpose(0, 2, 1).reshape(TASKS * EXPERTS, WIDTH),
        tower_weight.transpose(0, 2, 1).reshape(TASKS * TOWER, OUT),
        head_weight,
    )
    shape = lambda *dims: jax.ShapeDtypeStruct(dims, f32)
    units = HIDDEN, 512, EXAMPLES
    outputs = EXPERTS, OUT, EXAMPLES
    results = pl.pallas_call(
        model_kernel,
        out_shape=[
            vmem((TASKS, 128), f32), vmem((DENSE, EXAMPLES), f32), vmem((EMBED, ROWS), f32), vmem((IN_ROWS, 128), f32),
            vmem((REST_ROWS, 128), f32), vmem((DENSE, PROJ), f32), vmem((TASKS, TOWER), f32),
        ],
        in_specs=[anywhere] * 11,
        out_specs=[VMEM] * 7,
        scratch_shapes=[
            vmem((32, 128), i32), vmem((EMBED, ROWS), f32), vmem((TASKS, 128), f32), vmem((TABLES, EXAMPLES), i32),
            vmem((DENSE, EXAMPLES), f32), vmem((DENSE, PROJ), f32), vmem((16, WIDTH), f32), vmem((128, OUT), f32),
            vmem((TASKS, TOWER), f32),
            vmem((128, 128), i32), vmem((32, 128), i32), vmem((32, 128), i32), vmem((128, 128), f32),
            vmem((512, 128), f32), vmem((2 * EMBED, ROWS), bf16),
            vmem((HIDDEN, 512, WIDTH), f32), vmem((HIDDEN, 512, OUT), f32), vmem((HIDDEN, TASKS, 128), f32),
            vmem((HIDDEN, 512, WIDTH), bf16), vmem((HIDDEN, 512, WIDTH), bf16),
            vmem((HIDDEN, WIDTH, 512), bf16), vmem((HIDDEN, WIDTH, 512), bf16),
            vmem((EXPERTS, 256, OUT), bf16), vmem((EXPERTS, 256, OUT), bf16),
            vmem((EXPERTS, OUT, 256), bf16), vmem((EXPERTS, OUT, 256), bf16),
            vmem((256, 512), bf16), vmem((WIDTH, EXAMPLES), bf16), vmem((WIDTH, EXAMPLES), bf16),
            vmem((128, EXAMPLES), f32), vmem((128, 128), f32), vmem((128, 128), f32),
            vmem(units, bf16), vmem(units, bf16), vmem(units, f32), vmem(units, bf16), vmem(units, bf16),
            vmem(outputs, f32), vmem(outputs, f32), vmem(outputs, bf16), vmem(outputs, bf16),
            vmem((16, EXAMPLES), f32), vmem((16, EXAMPLES), f32),
            vmem((TASKS, OUT, EXAMPLES), f32), vmem((TASKS, OUT, EXAMPLES), f32), vmem((TASKS, EXAMPLES), f32),
            vmem((WIDTH, EXAMPLES), f32), vmem((128, 256), f32),
            vmem((IN_ROWS, 128), f32), vmem((REST_ROWS, 128), f32), vmem((16 * IN_PIECE, 128), f32),
            vmem((16 * REST_PIECE, 128), f32), vmem((16 * IN_PIECE, 128), f32), vmem((16 * REST_PIECE, 128), f32),
            vmem((128, 128), f32), vmem((128, 128), f32), vmem((16, 128), f32), vmem((BATCH * 16, 128), f32),
            dma((11,)), dma((3, 2)), dma((3, 2)), dma((3, 2, 3)), dma((3, 2, 3)), dma((3, 2)), dma((3, 2)),
            dma((3,)), dma((3,)), dma((3,)), dma((3,)), dma((3,)), dma((3,)),
            dma, dma, dma, dma, dma, dma, dma, dma,
            dma((2,)), dma((2,)), dma((2,)), dma((2,)), dma((2,)), dma((2, 15)), dma((2,)), dma((2,)),
        ],
        compiler_params=pltpu.CompilerParams(vmem_limit_bytes=LIMIT, collective_id=0, has_side_effects=True),
        name="model",
    )(*arrays)
    results = [pltpu.with_memory_space_constraint(result, pltpu.VMEM) for result in results]
    pred, dense_grad, table_grad, in_total, rest_total, weight_grad, head_grad = results
    table_grad, in_grad, out_grad, tower_grad, gate_grad, weight_grad, head_grad, pred, dense_grad = pl.pallas_call(
        write_kernel,
        out_shape=[
            shape(EMBED, ROWS), shape(512, WIDTH), shape(512, OUT), shape(TASKS * TOWER, OUT),
            shape(TASKS * EXPERTS, WIDTH), shape(DENSE, PROJ), shape(TASKS, TOWER), shape(TASKS, 128),
            shape(DENSE, EXAMPLES),
        ],
        in_specs=[anywhere] * 7,
        out_specs=[anywhere] * 9,
        scratch_shapes=[dma((15,))],
        compiler_params=pltpu.CompilerParams(vmem_limit_bytes=LIMIT),
        name="write",
    )(table_grad, in_total, rest_total, weight_grad, head_grad, pred, dense_grad)
    return (
        pred.T,
        dense_grad.T,
        table_grad.reshape(TABLES, ENTRY, ROWS).transpose(0, 2, 1),
        weight_grad,
        in_grad.reshape(EXPERTS, UNITS, WIDTH).transpose(2, 0, 1),
        out_grad.reshape(EXPERTS, UNITS, OUT),
        gate_grad.reshape(TASKS, EXPERTS, WIDTH).transpose(0, 2, 1),
        tower_grad.reshape(TASKS, TOWER, OUT).transpose(0, 2, 1),
        head_grad,
    )


def solution(mesh):
    placed = (
        P(None, ("batch", "hidden"), None),
        P("batch", None),
        P(),
        P(None, None, "hidden"),
        P(None, "hidden", None),
        P(),
        P(),
        P(),
        P("batch", None),
        P("batch", None, None),
        P(("batch", "hidden"), None),
    )
    return jax.shard_map(
        on_device,
        mesh=mesh,
        in_specs=placed,
        out_specs=(
            P(("batch", "hidden"), None),
            P("batch", None),
            P(None, ("batch", "hidden"), None),
            P(),
            P(None, None, "hidden"),
            P(None, "hidden", None),
            P(),
            P(),
            P(),
        ),
        check_vma=False,
    )
```

```python
import jax
import jax.numpy as jnp
from jax import lax
from jax.experimental import pallas as pl
from jax.experimental.pallas import tpu as pltpu
from jax.sharding import PartitionSpec as P

f32 = jnp.float32
bf16 = jnp.bfloat16
MESH = pl.DeviceIdType.MESH
VMEM = pl.BlockSpec(memory_space=pltpu.VMEM)
LIMIT = 56 * 2**20

TABLES, ROWS, ENTRY = 26, 1024, 16
BATCH, HIDDEN = 32, 4
DEVICES = BATCH * HIDDEN
EXPERTS, UNITS, OUT, WIDTH = 8, 64, 128, 512
TASKS, TOWER, DENSE, PROJ = 2, 64, 13, 96
EXAMPLES = 512
EMBED = TABLES * ENTRY

IN_ROWS, IN_PIECE = 1024, 32
OUT_AT, GATE_AT, TOWER_AT, HEAD_AT = 0, 512, 576, 704
REST_ROWS, REST_PIECE = 768, 24


def split(value):
    high = value.astype(bf16)
    return high, (value - high.astype(f32)).astype(bf16)


def dot_nn(a, b):
    return lax.dot_general(a, b, (((1,), (0,)), ((), ())), preferred_element_type=f32)


def dot_nt(a, b):
    return lax.dot_general(a, b, (((1,), (1,)), ((), ())), preferred_element_type=f32)


def dot_tn(a, b):
    return lax.dot_general(a, b, (((0,), (0,)), ((), ())), preferred_element_type=f32)


def dot3_tn(a, b):
    (ah, al), (bh, bl) = a, b
    return dot_tn(ah, bh) + dot_tn(al, bh) + dot_tn(ah, bl)


def dot3_nn(a, b):
    (ah, al), (bh, bl) = a, b
    return dot_nn(jnp.concatenate([ah, al, ah], 1), jnp.concatenate([bh, bh, bl], 0))


def dot3_nt(a, b):
    (ah, al), (bh, bl) = a, b
    return dot_nt(jnp.concatenate([ah, al, ah], 1), jnp.concatenate([bh, bh, bl], 1))


def sigmoid(value):
    return 0.5 * jnp.tanh(0.5 * value) + 0.5


def silu_both(value):
    sigma = sigmoid(value)
    result = value * sigma
    return result, sigma + result * (1.0 - sigma)


def iota(shape, axis):
    return lax.broadcasted_iota(jnp.int32, shape, axis)


def hops(offset):
    return min(offset, 4 - offset)


PLANE = sorted(
    ((dz, dx, dc) for dz in range(4) for dx in range(4) for dc in range(2) if dz or dx or dc),
    key=lambda d: -(2 * hops(d[0]) + 2 * hops(d[1]) + d[2]),
)
EVERYWHERE = sorted(
    ((dz, dx, dc, dy) for dz in range(4) for dx in range(4) for dc in range(2) for dy in range(4) if dz or dx or dc or dy),
    key=lambda d: -(2 * hops(d[0]) + 2 * hops(d[1]) + d[2] + 2 * hops(d[3])),
)
CHIPS = [(dz, dx) for dz, dx, dc in PLANE if not dc and (dz or dx)]


def target(b, h):
    return {"batch": b, "hidden": h}


def remote(src, dst, send, recv, b, h):
    return pltpu.make_async_remote_copy(src, dst, send, recv, device_id=target(b, h), device_id_type=MESH)


def bulk_wait(ref, sem):
    pltpu.make_async_copy(ref, ref, sem).wait()


def ids_by_query(received):
    turned = jnp.concatenate([received] * 4, 0).T
    lane = iota((8, 128), 1) // 32
    out = jnp.zeros((8, 128), jnp.int32)
    for q in range(4):
        out = jnp.where(lane == q, turned[q * 8 : q * 8 + 8, :], out)
    return out


def hot_of(code, count):
    rows = iota((count, code.shape[1]), 0).astype(jnp.int16)
    return jnp.where(rows == code.astype(jnp.int16), bf16(1.0), bf16(0.0))


def model_kernel(
    req_in, tab_in, win, wout, cot_in, slots_in, dense_in, dense_weight_in, gate_weight_in, tower_weight_in, head_in,
    pred_out, dense_grad_out, table_out, in_total, rest_total, weight_grad_out, head_grad_out,
    req, tab, cot, slots, dense, dense_weight, gate_weight, tower_weight, head,
    id_turned, id_send, id_recv, ids, row_send, rows, tab_split, win_all, wout_all, cot_all,
    wh, wl, oh, ol, gate_h, gate_l, tower_h, tower_l, dense_h, dense_l, lists, feat_h, feat_l,
    dense_pad, weight_pad, head_pad,
    inner_h, inner_l, slope, ig_h, ig_l, eo, eslope, ep_h, ep_l, gates, gate_slope, mixed, mixed_grad, pred,
    towers, pre_grads, scores, lgh, lgl, fg, slot_sum,
    in_sums, rest_sums, in_swap, rest_swap, in_pieces, rest_pieces,
    message, got, weight_part, weight_swap, weight_got, weight_total, hot_rows,
    local_sem, y_send, y_recv, p_send, p_recv, c_send, c_recv, wo_send, wo_recv, woc_send, woc_recv, cot_send, cot_recv,
    id_ssem, id_rsem, row_ssem, row_rsem, slot_ssem, slot_rsem, weight_ssem, weight_rsem, weight_send, weight_recv,
    swap_send, swap_recv, piece_ssem, piece_rsem, full_ssem, full_recv, last_ssem, last_rsem,
):
    b, h = lax.axis_index("batch"), lax.axis_index("hidden")
    core, x, z, chip = lax.rem(b, 2), lax.rem(b // 2, 4), b // 8, b // 2
    me = b * HIDDEN + h
    sibling = b + 1 - 2 * core
    zs = [lax.rem(z + d, 4) * 8 for d in range(4)]
    xs = [lax.rem(x + d, 4) * 2 for d in range(4)]
    cores = [core, 1 - core]
    hs = [lax.rem(h + d, HIDDEN) for d in range(HIDDEN)]
    chips = [(zs[dz] + xs[dx]) // 2 for dz, dx in CHIPS]
    plane = [zs[dz] + xs[dx] + cores[dc] for dz, dx, dc in PLANE]
    order = (1, 3, 2)
    block = pl.when(core >= 0)

    def bring(source, home, i):
        copy = pltpu.make_async_copy(source, home, local_sem.at[i])
        copy.start()
        return copy

    def block_of(s):
        return pl.ds(pl.multiple_of(s * 512, 512), 512)

    req_copy = bring(req_in, req, 0)
    barrier = pltpu.get_barrier_semaphore()
    for other in plane:
        pl.semaphore_signal(barrier, inc=1, device_id=target(other, h), device_id_type=MESH)
    for i in (2, 1, 3):
        pl.semaphore_signal(barrier, inc=1, device_id=target(b, hs[i]), device_id_type=MESH)
    tab_copy = bring(tab_in, tab, 1)
    win_copy = bring(win, win_all.at[h], 2)
    wout_copy = bring(wout, wout_all.at[h], 3)
    small = ((cot_in, cot), (slots_in, slots), (dense_in, dense), (dense_weight_in, dense_weight),
             (gate_weight_in, gate_weight), (tower_weight_in, tower_weight), (head_in, head))
    small_copies = [bring(source, home, 4 + i) for i, (source, home) in enumerate(small)]
    req_copy.wait()
    id_turned[...] = jnp.concatenate([req[...]] * 4, 0).T
    id_send[...] = id_turned[pl.ds(h, BATCH, stride=HIDDEN), :]
    pl.semaphore_wait(barrier, BATCH - 1 + HIDDEN - 1)

    for other in plane:
        remote(id_send.at[pl.ds(other, 1)], id_recv.at[pl.ds(b, 1)], id_ssem, id_rsem, other, h).start()
    spots = (
        pl.ds(pl.multiple_of(core * 128 + x * 32, 32), 32),
        pl.ds(pl.multiple_of(256 + core * 128 + z * 32, 32), 32),
    )
    spans = (pl.ds(pl.multiple_of(core * 128, 128), 128), pl.ds(pl.multiple_of(256 + core * 128, 128), 128))
    half = pl.ds(pl.multiple_of(core * 256, 256), 256)
    source_of = [lax.rem(h - i + HIDDEN, HIDDEN) for i in range(HIDDEN)]
    y_copies, p_copies, c_copies, wo_copies, woc_copies, cot_copies = {}, {}, {}, {}, {}, {}
    for i in order:
        y_copies[i] = [
            remote(win.at[spots[p]], win_all.at[h, spots[p]], y_send.at[i - 1, p], y_recv.at[i - 1, p], b, hs[i])
            for p in range(2)
        ]
        for copy in y_copies[i]:
            copy.start()

    def spread(i):
        p_copies[i] = []
        for p in range(2):
            y_copies[i][p].wait_recv()
        for j in (2, 1, 3):
            for p in range(2):
                piece = win_all.at[source_of[i], spots[p]]
                other = z * 8 + xs[j] + core if p == 0 else zs[j] + x * 2 + core
                copy = remote(piece, piece, p_send.at[i - 1, p, j - 1], p_recv.at[i - 1, p, j - 1], other, h)
                copy.start()
                p_copies[i].append(copy)

    def to_core(i):
        for copy in p_copies[i]:
            copy.wait_recv()
        c_copies[i] = []
        for p in range(2):
            piece = win_all.at[source_of[i], spans[p]]
            copy = remote(piece, piece, c_send.at[i - 1, p], c_recv.at[i - 1, p], sibling, h)
            copy.start()
            c_copies[i].append(copy)

    def out_to_core(i):
        wo_copies[i].wait_recv()
        piece = wout_all.at[source_of[i], half]
        woc_copies[i] = remote(piece, piece, woc_send.at[i - 1], woc_recv.at[i - 1], sibling, h)
        woc_copies[i].start()

    tab_copy.wait()

    @block
    def _():
        high, low = split(tab[...])
        tab_split[0:EMBED, :] = high
        tab_split[EMBED : 2 * EMBED, :] = low

    id_recv[pl.ds(b, 1), :] = id_send[pl.ds(b, 1), :]
    bulk_wait(id_recv.at[pl.ds(0, BATCH - 1)], id_rsem)

    @block
    def _():
        found = ids_by_query(id_recv[...])
        ids[...] = found
        table, row = found // ROWS, lax.rem(found, ROWS)
        entries = []
        for pair in range(4):
            hot = jnp.concatenate([hot_of(row[j : j + 1, :], ROWS) for j in (2 * pair, 2 * pair + 1)], 1)
            value = dot_nn(tab_split[...], hot)
            for part in range(2):
                wanted = table[2 * pair + part : 2 * pair + part + 1, :]
                entry = jnp.zeros((ENTRY, 128), f32)
                for t in range(TABLES):
                    high = value[t * ENTRY : (t + 1) * ENTRY, part * 128 : part * 128 + 128]
                    low = value[EMBED + t * ENTRY : EMBED + (t + 1) * ENTRY, part * 128 : part * 128 + 128]
                    entry = jnp.where(wanted == t, high + low, entry)
                entries.append(entry)
        turned = jnp.concatenate(entries, 0).T
        for q in range(4):
            row_send[pl.ds(q, BATCH, stride=4), :] = turned[q * 32 : q * 32 + 32, :]

    mine = pl.ds(me * 4, 4)
    for dz, dx, dc, dy in EVERYWHERE:
        group = zs[dz] + xs[dx] + cores[dc]
        remote(row_send.at[pl.ds(group * 4, 4)], rows.at[mine], row_ssem, row_rsem, group, hs[dy]).start()
    rows[mine, :] = row_send[pl.ds(b * 4, 4), :]
    for i in order:
        spread(i)
    for copy in small_copies:
        copy.wait()
    wout_copy.wait()
    for i in order:
        cot_copies[i] = remote(cot, cot_all.at[h], cot_send.at[i - 1], cot_recv.at[i - 1], b, hs[i])
        cot_copies[i].start()
        wo_copies[i] = remote(
            wout_all.at[h, half], wout_all.at[h, half], wo_send.at[i - 1], wo_recv.at[i - 1], b, hs[i]
        )
        wo_copies[i].start()
    win_copy.wait()

    @block
    def _():
        cot_all[pl.ds(h, 1)] = cot[...].reshape(1, TASKS, 128)
        dense_pad[...] = jnp.zeros_like(dense_pad)
        dense_pad[0:DENSE, :] = dense[...]
        weight_pad[...] = jnp.zeros_like(weight_pad)
        weight_pad[0:DENSE, 0:PROJ] = dense_weight[...]
        head_pad[...] = jnp.zeros_like(head_pad)
        head_pad[0:TASKS, 0:TOWER] = head[...]
        dense_h[...], dense_l[...] = split(dense_pad[...])
        projected = dot3_nn(split(weight_pad[...].T), (dense_h[...], dense_l[...]))
        feat_h[EMBED:WIDTH, :], feat_l[EMBED:WIDTH, :] = split(projected[0:PROJ, :])
        tower_h[...], tower_l[...] = split(tower_weight[...])
        gate_h[...], gate_l[...] = split(gate_weight[...])
        wh[block_of(h), :], wl[block_of(h), :] = split(win_all[h])

    bulk_wait(rows.at[pl.ds(0, (DEVICES - 1) * 4)], row_rsem)

    def gather(first, last):
        for t in range(first, last):
            slot = slots[t : t + 1, :]
            low = lax.rem(slot, 8)
            value = dot_nn(lists[...], hot_of(lax.rem(slot, 32) // 8 * 128 + slot // 32, 512))
            high_sum = jnp.zeros((ENTRY, EXAMPLES), f32)
            low_sum = jnp.zeros((ENTRY, EXAMPLES), f32)
            for j in range(8):
                high_sum = jnp.where(low == j, value[j * 16 : j * 16 + 16, :], high_sum)
                low_sum = jnp.where(low == j, value[128 + j * 16 : 128 + j * 16 + 16, :], low_sum)
            feat_h[t * ENTRY : (t + 1) * ENTRY, :] = high_sum.astype(bf16)
            feat_l[t * ENTRY : (t + 1) * ENTRY, :] = low_sum.astype(bf16)

    @block
    def _():
        for q in range(4):
            at = slice(q * 128, q * 128 + 128)
            lists[0:128, at], lists[128:256, at] = split(rows[pl.ds(q, DEVICES, stride=4), :].T)
        gather(0, 13)

    to_core(1)
    block(lambda: gather(13, TABLES))

    def first_layer(s):
        at = block_of(s)
        inner, slope[at, :] = silu_both(dot3_nn((wh[at, :], wl[at, :]), (feat_h[...], feat_l[...])))
        inner_h[at, :], inner_l[at, :] = split(inner)

    def next_layer(i):
        for copy in c_copies[i]:
            copy.wait_recv()

        @block
        def _():
            s = source_of[i]
            wh[block_of(s), :], wl[block_of(s), :] = split(win_all[s])
            first_layer(s)

    block(lambda: first_layer(h))
    to_core(3)
    next_layer(1)
    to_core(2)
    next_layer(3)
    for i in order:
        out_to_core(i)
    next_layer(2)
    for i in order:
        woc_copies[i].wait_recv()
        cot_copies[i].wait_recv()

    def of_expert(refs, e):
        return tuple(
            jnp.concatenate([ref[s * 512 + e * UNITS : s * 512 + (e + 1) * UNITS, :] for s in range(HIDDEN)], 0)
            for ref in refs
        )

    @block
    def _():
        logits = dot3_nn((gate_h[...], gate_l[...]), (feat_h[...], feat_l[...]))
        for k in range(TASKS):
            part = logits[k * 8 : k * 8 + 8, :]
            raised = jnp.exp(part - jnp.max(part, axis=0, keepdims=True))
            gates[k * 8 : k * 8 + 8, :] = raised / jnp.sum(raised, axis=0, keepdims=True)
        for s in range(HIDDEN):
            at = slice(s * 512, s * 512 + 512)
            oh[at, :], ol[at, :] = split(wout_all[s])

    @block
    def _():
        mixed[...] = jnp.zeros_like(mixed)
        for e in range(EXPERTS):
            outputs, eslope[e] = silu_both(dot3_tn(of_expert((oh, ol), e), of_expert((inner_h, inner_l), e)))
            eo[e] = outputs
            for k in range(TASKS):
                mixed[k] = mixed[k] + gates[k * 8 + e : k * 8 + e + 1, :] * outputs

    @block
    def _():
        head_turned = head_pad[...].T
        scores[...] = jnp.zeros_like(scores)
        for k in range(TASKS):
            at = slice(k * TOWER, (k + 1) * TOWER)
            value, tower_slope = silu_both(dot3_nn((tower_h[at, :], tower_l[at, :]), split(mixed[k])))
            column = jnp.broadcast_to(head_turned[0:TOWER, k : k + 1], (TOWER, EXAMPLES))
            predicted = sigmoid(jnp.sum(value * column, axis=0, keepdims=True))
            pred[k : k + 1, :] = predicted
            cotangent = jnp.concatenate([cot_all[i, k : k + 1, :] for i in range(HIDDEN)], 1)
            score = cotangent * predicted * (1.0 - predicted)
            scores[k : k + 1, :] = score
            towers[at, :] = value
            pre_grad = score * column * tower_slope
            pre_grads[at, :] = pre_grad
            mixed_grad[k] = dot3_tn((tower_h[at, :], tower_l[at, :]), split(pre_grad))

    def expert_grads(first, last):
        for e in range(first, last):
            at = pl.ds(e * UNITS, UNITS)
            outputs = eo[e]
            grad = jnp.zeros((OUT, EXAMPLES), f32)
            for k in range(TASKS):
                gate_slope[k * 8 + e : k * 8 + e + 1, :] = jnp.sum(mixed_grad[k] * outputs, axis=0, keepdims=True)
                grad = grad + gates[k * 8 + e : k * 8 + e + 1, :] * mixed_grad[k]
            out_split = split(grad * eslope[e])
            ep_h[e], ep_l[e] = out_split
            inner_grad = dot3_nn(of_expert((oh, ol), e), out_split)
            for s in range(HIDDEN):
                at = slice(s * 512 + e * UNITS, s * 512 + (e + 1) * UNITS)
                ig_h[at, :], ig_l[at, :] = split(inner_grad[s * UNITS : (s + 1) * UNITS, :] * slope[at, :])

    def first_layer_grad(n):
        at = pl.ds(pl.multiple_of(h * 512 + n * 256, 256), 256)
        in_grad = dot3_nt((ig_h[at, :], ig_l[at, :]), (feat_h[...], feat_l[...]))
        for q in range(4):
            in_sums[n * IN_ROWS + q * 256 : n * IN_ROWS + (q + 1) * 256, :] = in_grad[:, q * 128 : (q + 1) * 128]

    parts = [
        tuple(ref.at[pl.ds(n * size, size)] for ref, size in zip((in_sums, in_swap, in_pieces, in_total), sizes))
        + (IN_PIECE,)
        for n in range(2)
        for sizes in [(IN_ROWS, IN_ROWS // 2, IN_ROWS // 2, IN_ROWS)]
    ] + [(rest_sums, rest_swap, rest_pieces, rest_total, REST_PIECE)]

    def swap(n):
        sums, swapped, _, _, piece = parts[n]
        half_rows = 16 * piece
        copy = remote(
            sums.at[pl.ds(pl.multiple_of((1 - core) * half_rows, 8), half_rows)], swapped,
            swap_send.at[n], swap_recv.at[n], sibling, h,
        )
        copy.start()
        return copy

    def send_pieces(n, copy):
        sums, swapped, pieces, _, piece = parts[n]
        half_rows = 16 * piece
        copy.wait_recv()
        swapped[...] += sums[pl.ds(pl.multiple_of(core * half_rows, 8), half_rows), :]
        own = pl.ds(pl.multiple_of(chip * piece, 8), piece)
        for other in chips:
            remote(
                swapped.at[pl.ds(pl.multiple_of(other * piece, 8), piece)], pieces.at[own],
                piece_ssem.at[n], piece_rsem.at[n], other * 2 + core, h,
            ).start()
        pieces[own, :] = swapped[own, :]

    def send_sums(n):
        _, _, pieces, total, piece = parts[n]
        half_rows = 16 * piece
        bulk_wait(pieces.at[pl.ds(0, 15 * piece)], piece_rsem.at[n])
        value = pieces[0:piece, :]
        for i in range(1, 16):
            value = value + pieces[i * piece : (i + 1) * piece, :]
        at = pl.ds(pl.multiple_of(core * half_rows + chip * piece, 8), piece)
        total[at, :] = value
        for i, other in enumerate(chips):
            remote(total.at[at], total.at[at], full_ssem.at[n], full_recv.at[n, i], other * 2 + core, h).start()
        remote(total.at[at], total.at[at], last_ssem.at[n], last_rsem.at[n], sibling, h).start()

    def hand_on(n):
        _, _, _, total, piece = parts[n]
        for i, (dz, dx) in reversed(list(enumerate(CHIPS))):
            source = (zs[(4 - dz) % 4] + xs[(4 - dx) % 4]) // 2
            at = pl.ds(pl.multiple_of(core * 16 * piece + source * piece, 8), piece)
            bulk_wait(total.at[at], full_recv.at[n, i])
            remote(total.at[at], total.at[at], last_ssem.at[n], last_rsem.at[n], sibling, h).start()

    @block
    def _():
        expert_grads(0, EXPERTS // 2)
        first_layer_grad(0)

    swaps = [swap(0)]
    block(lambda: expert_grads(EXPERTS // 2, EXPERTS))
    send_pieces(0, swaps[0])
    block(lambda: first_layer_grad(1))
    swaps.append(swap(1))

    @block
    def _():
        for k in range(TASKS):
            at = slice(k * TOWER, (k + 1) * TOWER)
            rest_sums[TOWER_AT + k * TOWER : TOWER_AT + (k + 1) * TOWER, :] = dot3_nt(
                split(pre_grads[at, :]), split(mixed[k])
            )
        head_rows = dot3_nt(split(scores[...]), split(towers[...]))
        rest_sums[HEAD_AT:REST_ROWS, :] = jnp.zeros((REST_ROWS - HEAD_AT, 128), f32)
        rest_sums[HEAD_AT : HEAD_AT + 1, :] = jnp.where(
            iota((1, 128), 1) < TOWER, head_rows[0:1, :], head_rows[1:2, :]
        )
        logit_grads = []
        for k in range(TASKS):
            gate, slopes = gates[k * 8 : k * 8 + 8, :], gate_slope[k * 8 : k * 8 + 8, :]
            logit_grads.append(gate * (slopes - jnp.sum(gate * slopes, axis=0, keepdims=True)))
        lgh[...], lgl[...] = split(jnp.concatenate(logit_grads, 0))
        gate_grad = dot3_nt((lgh[...], lgl[...]), (feat_h[...], feat_l[...]))
        for q in range(4):
            rest_sums[GATE_AT + q * 16 : GATE_AT + q * 16 + 16, :] = gate_grad[:, q * 128 : (q + 1) * 128]

    send_pieces(1, swaps[1])

    @block
    def _():
        for e in range(EXPERTS):
            at = pl.ds(pl.multiple_of(h * 512 + e * UNITS, UNITS), UNITS)
            rest_sums[OUT_AT + e * UNITS : OUT_AT + (e + 1) * UNITS, :] = dot3_nt(
                (inner_h[at, :], inner_l[at, :]), (ep_h[e], ep_l[e])
            )

    swaps.append(swap(2))

    def feature_grad(low, high):
        at = slice(low, high)
        fg[at, :] = dot3_tn((wh[:, at], wl[:, at]), (ig_h[...], ig_l[...])) + dot3_tn(
            (gate_h[:, at], gate_l[:, at]), (lgh[...], lgl[...])
        )

    def scatter(first, last):
        hots, spreads = [], []
        for t in range(first, last):
            slot = slots[t : t + 1, :]
            owner, low = slot // 32, lax.rem(slot, 8)
            code = jnp.where(lax.rem(owner, HIDDEN) == h, lax.rem(slot, 32) // 8 * 32 + owner // HIDDEN, -1)
            hots.append(hot_of(code, 128))
            high, rest = split(fg[t * ENTRY : (t + 1) * ENTRY, :])
            where = jnp.broadcast_to(low, (ENTRY, EXAMPLES)).astype(jnp.int16)
            nothing = jnp.zeros((ENTRY, EXAMPLES), bf16)
            spreads.append(
                jnp.concatenate([jnp.where(where == j, value, nothing) for value in (high, rest) for j in range(8)], 0)
            )
        return dot_nt(jnp.concatenate(spreads, 1), jnp.concatenate(hots, 1))

    block(lambda: feature_grad(256, WIDTH))
    send_pieces(2, swaps[2])

    @block
    def _():
        projected_grad = split(jnp.concatenate([fg[EMBED:WIDTH, :], jnp.zeros((32, EXAMPLES), f32)], 0))
        weight_part[...] = dot3_nt((dense_h[...], dense_l[...]), projected_grad)[0:16, :]
        dense_grad_out[...] = dot3_nn(split(weight_pad[...]), projected_grad)[0:DENSE, :]

    weight_copies = [
        remote(
            weight_part.at[pl.ds(pl.multiple_of((1 - core) * 8, 8), 8)], weight_swap,
            weight_send.at[0], weight_recv.at[0], sibling, h,
        )
    ]
    weight_copies[0].start()

    @block
    def _():
        slot_sum[...] = scatter(16, TABLES)

    weight_copies[0].wait_recv()
    weight_swap[...] += weight_part[pl.ds(pl.multiple_of(core * 8, 8), 8), :]
    weight_at = pl.ds(pl.multiple_of(chip * 8, 8), 8)
    for other in chips:
        remote(weight_swap, weight_got.at[weight_at], weight_ssem, weight_rsem, other * 2 + core, h).start()
    weight_got[weight_at, :] = weight_swap[...]
    block(lambda: feature_grad(0, 256))
    send_sums(0)

    @block
    def _():
        slot_turned = slot_sum[...] + scatter(0, 16)
        slot_turned = (slot_turned[0:128, :] + slot_turned[128:256, :]).T
        for q in range(4):
            message[pl.ds(q, BATCH, stride=4), :] = slot_turned[q * 32 : q * 32 + 32, :]

    for other in plane:
        remote(message.at[pl.ds(other * 4, 4)], got.at[pl.ds(b * 4, 4)], slot_ssem, slot_rsem, other, h).start()
    got[pl.ds(b * 4, 4), :] = message[pl.ds(b * 4, 4), :]
    send_sums(1)
    send_sums(2)
    bulk_wait(weight_got.at[pl.ds(0, 15 * 8)], weight_rsem)
    value = weight_got[0:8, :]
    for i in range(1, 16):
        value = value + weight_got[i * 8 : i * 8 + 8, :]
    weight_at = pl.ds(pl.multiple_of(core * 8, 8), 8)
    weight_total[weight_at, :] = value
    weight_copies.append(
        remote(
            weight_total.at[weight_at], weight_total.at[weight_at], weight_send.at[1], weight_recv.at[1], sibling, h
        )
    )
    weight_copies[1].start()
    for k in range(TASKS):
        pred_out[k : k + 1, :] = pred[k : k + 1, pl.ds(pl.multiple_of(h * 128, 128), 128)]

    @block
    def _():
        row = lax.rem(ids[...], ROWS)
        for j in range(8):
            hot_rows[:, j * 128 : (j + 1) * 128] = hot_of(row[j : j + 1, :], ROWS)

    bulk_wait(got.at[pl.ds(0, (BATCH - 1) * 4)], slot_rsem)

    @block
    def _():
        high, rest = split(jnp.concatenate([got[pl.ds(q, BATCH, stride=4), :] for q in range(4)], 0).T)
        table = ids[...] // ROWS
        spreads = []
        for j in range(8):
            where = jnp.broadcast_to(table[j : j + 1, :], (ENTRY, 128)).astype(jnp.int16)
            nothing = jnp.zeros((ENTRY, 128), bf16)
            chosen = [
                jnp.where(where == t, value[j * 16 : j * 16 + 16, :], nothing)
                for value in (high, rest)
                for t in range(TABLES)
            ]
            spreads.append(jnp.concatenate(chosen, 0))
        both = dot_nt(jnp.concatenate(spreads, 1), hot_rows[...])
        table_out[...] = both[0:EMBED, :] + both[EMBED : 2 * EMBED, :]

    weight_copies[1].wait_recv()
    weight_grad_out[...] = weight_total[0:DENSE, 0:PROJ]
    for n in range(3):
        hand_on(n)
    for n, (_, _, pieces, total, piece) in enumerate(parts):
        bulk_wait(total.at[pl.ds(0, 16 * piece)], last_rsem.at[n])
        if n == 2:
            head_grad_out[0:1, :] = total[HEAD_AT : HEAD_AT + 1, 0:TOWER]
            head_grad_out[1:2, :] = total[HEAD_AT : HEAD_AT + 1, TOWER : 2 * TOWER]
        bulk_wait(total.at[pl.ds(0, 16 * piece)], last_ssem.at[n])
        bulk_wait(total.at[pl.ds(0, 15 * piece)], full_ssem.at[n])
        bulk_wait(pieces.at[pl.ds(0, 15 * piece)], piece_ssem.at[n])
    for copy in swaps:
        copy.wait_send()
    for copy in weight_copies:
        copy.wait_send()
    bulk_wait(weight_got.at[pl.ds(0, 15 * 8)], weight_ssem)
    bulk_wait(message.at[pl.ds(0, (BATCH - 1) * 4)], slot_ssem)
    bulk_wait(rows.at[pl.ds(0, (DEVICES - 1) * 4)], row_ssem)
    bulk_wait(id_send.at[pl.ds(0, BATCH - 1)], id_ssem)
    for i in order:
        for copy in (*y_copies[i], *p_copies[i], *c_copies[i], wo_copies[i], woc_copies[i], cot_copies[i]):
            copy.wait_send()


def write_kernel(
    table, in_total, rest_total, weight_grad, head_grad, pred, dense_grad,
    table_out, in_out, out_out, tower_out, gate_out, weight_out, head_out, pred_out, dense_out, sems,
):
    copies = [(table, table_out), (rest_total.at[OUT_AT:GATE_AT], out_out), (rest_total.at[TOWER_AT:HEAD_AT], tower_out)]
    copies += [
        (
            in_total.at[n * IN_ROWS + q * 256 : n * IN_ROWS + (q + 1) * 256],
            in_out.at[n * 256 : (n + 1) * 256, q * 128 : (q + 1) * 128],
        )
        for n in range(2)
        for q in range(4)
    ]
    copies += [
        (rest_total.at[GATE_AT + q * 16 : GATE_AT + q * 16 + 16], gate_out.at[:, q * 128 : q * 128 + 128])
        for q in range(4)
    ]
    copies += [(weight_grad, weight_out), (head_grad, head_out), (pred, pred_out), (dense_grad, dense_out)]
    copies = [pltpu.make_async_copy(source, home, sems.at[i]) for i, (source, home) in enumerate(copies)]
    for copy in copies:
        copy.start()
    for copy in copies:
        copy.wait()


def on_device(
    tables, dense, dense_weight, expert_in, expert_out, gate_weight, tower_weight, head_weight, slots, requests, pred_cot
):
    i32 = jnp.int32
    dma = pltpu.SemaphoreType.DMA
    vmem = pltpu.VMEM
    anywhere = pl.BlockSpec(memory_space=pl.ANY)
    arrays = (
        requests[0].T,
        tables.transpose(0, 2, 1).reshape(EMBED, ROWS),
        expert_in.transpose(1, 2, 0).reshape(EXPERTS * UNITS, WIDTH),
        expert_out.reshape(EXPERTS * UNITS, OUT),
        pred_cot.T,
        slots.T,
        dense.T,
        dense_weight,
        gate_weight.transpose(0, 2, 1).reshape(TASKS * EXPERTS, WIDTH),
        tower_weight.transpose(0, 2, 1).reshape(TASKS * TOWER, OUT),
        head_weight,
    )
    shape = lambda *dims: jax.ShapeDtypeStruct(dims, f32)
    units = HIDDEN * 512, EXAMPLES
    outputs = EXPERTS, OUT, EXAMPLES
    results = pl.pallas_call(
        model_kernel,
        out_shape=[
            vmem((TASKS, 128), f32), vmem((DENSE, EXAMPLES), f32), vmem((EMBED, ROWS), f32), vmem((2 * IN_ROWS, 128), f32),
            vmem((REST_ROWS, 128), f32), vmem((DENSE, PROJ), f32), vmem((TASKS, TOWER), f32),
        ],
        in_specs=[anywhere] * 11,
        out_specs=[VMEM] * 7,
        scratch_shapes=[
            vmem((32, 128), i32), vmem((EMBED, ROWS), f32), vmem((TASKS, 128), f32), vmem((TABLES, EXAMPLES), i32),
            vmem((DENSE, EXAMPLES), f32), vmem((DENSE, PROJ), f32), vmem((16, WIDTH), f32), vmem((128, OUT), f32),
            vmem((TASKS, TOWER), f32),
            vmem((128, 128), i32), vmem((32, 128), i32), vmem((32, 128), i32), vmem((8, 128), i32), vmem((128, 128), f32),
            vmem((512, 128), f32), vmem((2 * EMBED, ROWS), bf16),
            vmem((HIDDEN, 512, WIDTH), f32), vmem((HIDDEN, 512, OUT), f32), vmem((HIDDEN, TASKS, 128), f32),
            vmem((2048, WIDTH), bf16), vmem((2048, WIDTH), bf16), vmem((2048, OUT), bf16), vmem((2048, OUT), bf16),
            vmem((16, WIDTH), bf16), vmem((16, WIDTH), bf16), vmem((128, OUT), bf16), vmem((128, OUT), bf16),
            vmem((128, EXAMPLES), bf16), vmem((128, EXAMPLES), bf16),
            vmem((256, 512), bf16), vmem((WIDTH, EXAMPLES), bf16), vmem((WIDTH, EXAMPLES), bf16),
            vmem((128, EXAMPLES), f32), vmem((128, 128), f32), vmem((128, 128), f32),
            vmem(units, bf16), vmem(units, bf16), vmem(units, f32), vmem(units, bf16), vmem(units, bf16),
            vmem(outputs, f32), vmem(outputs, f32), vmem(outputs, bf16), vmem(outputs, bf16),
            vmem((16, EXAMPLES), f32), vmem((16, EXAMPLES), f32),
            vmem((TASKS, OUT, EXAMPLES), f32), vmem((TASKS, OUT, EXAMPLES), f32), vmem((TASKS, EXAMPLES), f32),
            vmem((128, EXAMPLES), f32), vmem((128, EXAMPLES), f32), vmem((16, EXAMPLES), f32),
            vmem((16, EXAMPLES), bf16), vmem((16, EXAMPLES), bf16),
            vmem((WIDTH, EXAMPLES), f32), vmem((256, 128), f32),
            vmem((2 * IN_ROWS, 128), f32), vmem((REST_ROWS, 128), f32), vmem((IN_ROWS, 128), f32),
            vmem((16 * REST_PIECE, 128), f32), vmem((IN_ROWS, 128), f32), vmem((16 * REST_PIECE, 128), f32),
            vmem((128, 128), f32), vmem((128, 128), f32), vmem((16, 128), f32), vmem((8, 128), f32),
            vmem((128, 128), f32), vmem((16, 128), f32), vmem((ROWS, ROWS), bf16),
            dma((11,)), dma((3, 2)), dma((3, 2)), dma((3, 2, 3)), dma((3, 2, 3)), dma((3, 2)), dma((3, 2)),
            dma((3,)), dma((3,)), dma((3,)), dma((3,)), dma((3,)), dma((3,)),
            dma, dma, dma, dma, dma, dma, dma, dma, dma((2,)), dma((2,)),
            dma((3,)), dma((3,)), dma((3,)), dma((3,)), dma((3,)), dma((3, 15)), dma((3,)), dma((3,)),
        ],
        compiler_params=pltpu.CompilerParams(vmem_limit_bytes=LIMIT, collective_id=0, has_side_effects=True),
        name="model",
    )(*arrays)
    results = [pltpu.with_memory_space_constraint(result, pltpu.VMEM) for result in results]
    pred, dense_grad, table_grad, in_total, rest_total, weight_grad, head_grad = results
    table_grad, in_grad, out_grad, tower_grad, gate_grad, weight_grad, head_grad, pred, dense_grad = pl.pallas_call(
        write_kernel,
        out_shape=[
            shape(EMBED, ROWS), shape(512, WIDTH), shape(512, OUT), shape(TASKS * TOWER, OUT),
            shape(TASKS * EXPERTS, WIDTH), shape(DENSE, PROJ), shape(TASKS, TOWER), shape(TASKS, 128),
            shape(DENSE, EXAMPLES),
        ],
        in_specs=[anywhere] * 7,
        out_specs=[anywhere] * 9,
        scratch_shapes=[dma((19,))],
        compiler_params=pltpu.CompilerParams(vmem_limit_bytes=LIMIT),
        name="write",
    )(table_grad, in_total, rest_total, weight_grad, head_grad, pred, dense_grad)
    return (
        pred.T,
        dense_grad.T,
        table_grad.reshape(TABLES, ENTRY, ROWS).transpose(0, 2, 1),
        weight_grad,
        in_grad.reshape(EXPERTS, UNITS, WIDTH).transpose(2, 0, 1),
        out_grad.reshape(EXPERTS, UNITS, OUT),
        gate_grad.reshape(TASKS, EXPERTS, WIDTH).transpose(0, 2, 1),
        tower_grad.reshape(TASKS, TOWER, OUT).transpose(0, 2, 1),
        head_grad,
    )


def solution(mesh):
    placed = (
        P(None, ("batch", "hidden"), None),
        P("batch", None),
        P(),
        P(None, None, "hidden"),
        P(None, "hidden", None),
        P(),
        P(),
        P(),
        P("batch", None),
        P("batch", None, None),
        P(("batch", "hidden"), None),
    )
    return jax.shard_map(
        on_device,
        mesh=mesh,
        in_specs=placed,
        out_specs=(
            P(("batch", "hidden"), None),
            P("batch", None),
            P(None, ("batch", "hidden"), None),
            P(),
            P(None, None, "hidden"),
            P(None, "hidden", None),
            P(),
            P(),
            P(),
        ),
        check_vma=False,
    )
```

```python
import jax
import jax.numpy as jnp
from jax import lax
from jax.experimental import pallas as pl
from jax.experimental.pallas import tpu as pltpu
from jax.sharding import PartitionSpec as P

f32 = jnp.float32
bf16 = jnp.bfloat16
MESH = pl.DeviceIdType.MESH
VMEM = pl.BlockSpec(memory_space=pltpu.VMEM)
LIMIT = 56 * 2**20

TABLES, ROWS, ENTRY = 26, 1024, 16
BATCH, HIDDEN = 32, 4
DEVICES = BATCH * HIDDEN
EXPERTS, UNITS, OUT, WIDTH = 8, 64, 128, 512
TASKS, TOWER, DENSE, PROJ = 2, 64, 13, 96
EXAMPLES = 512
EMBED = TABLES * ENTRY

IN_PARTS = ((0, 3), (3, 6), (6, 8))
IN_ROWS = 2048
OUT_AT, GATE_AT, TOWER_AT, HEAD_AT = 0, 512, 576, 704
REST_ROWS, REST_PIECE = 768, 24


def split(value):
    high = value.astype(bf16)
    return high, (value - high.astype(f32)).astype(bf16)


def dot_nn(a, b):
    return lax.dot_general(a, b, (((1,), (0,)), ((), ())), preferred_element_type=f32)


def dot_nt(a, b):
    return lax.dot_general(a, b, (((1,), (1,)), ((), ())), preferred_element_type=f32)


def dot_tn(a, b):
    return lax.dot_general(a, b, (((0,), (0,)), ((), ())), preferred_element_type=f32)


def dot3_tn(a, b):
    (ah, al), (bh, bl) = a, b
    return dot_tn(ah, bh) + dot_tn(al, bh) + dot_tn(ah, bl)


def dot3_nn(a, b):
    (ah, al), (bh, bl) = a, b
    return dot_nn(jnp.concatenate([ah, al, ah], 1), jnp.concatenate([bh, bh, bl], 0))


def dot3_nt(a, b):
    (ah, al), (bh, bl) = a, b
    return dot_nt(jnp.concatenate([ah, al, ah], 1), jnp.concatenate([bh, bh, bl], 1))


def sigmoid(value):
    return 0.5 * jnp.tanh(0.5 * value) + 0.5


def silu_both(value):
    sigma = sigmoid(value)
    result = value * sigma
    return result, sigma + result * (1.0 - sigma)


def iota(shape, axis):
    return lax.broadcasted_iota(jnp.int32, shape, axis)


def hops(offset):
    return min(offset, 4 - offset)


PLANE = sorted(
    ((dz, dx, dc) for dz in range(4) for dx in range(4) for dc in range(2) if dz or dx or dc),
    key=lambda d: -(2 * hops(d[0]) + 2 * hops(d[1]) + d[2]),
)
EVERYWHERE = sorted(
    ((dz, dx, dc, dy) for dz in range(4) for dx in range(4) for dc in range(2) for dy in range(4) if dz or dx or dc or dy),
    key=lambda d: -(2 * hops(d[0]) + 2 * hops(d[1]) + d[2] + 2 * hops(d[3])),
)
CHIPS = [(dz, dx) for dz, dx, dc in PLANE if not dc and (dz or dx)]


def target(b, h):
    return {"batch": b, "hidden": h}


def remote(src, dst, send, recv, b, h):
    return pltpu.make_async_remote_copy(src, dst, send, recv, device_id=target(b, h), device_id_type=MESH)


def bulk_wait(ref, sem):
    pltpu.make_async_copy(ref, ref, sem).wait()


def ids_by_query(received):
    turned = jnp.concatenate([received] * 4, 0).T
    lane = iota((8, 128), 1) // 32
    out = jnp.zeros((8, 128), jnp.int32)
    for q in range(4):
        out = jnp.where(lane == q, turned[q * 8 : q * 8 + 8, :], out)
    return out


def hot_of(code, count):
    rows = iota((count, code.shape[1]), 0).astype(jnp.int16)
    return jnp.where(rows == code.astype(jnp.int16), bf16(1.0), bf16(0.0))


def model_kernel(
    req_in, tab_in, win, wout, cot_in, slots_in, dense_in, dense_weight_in, gate_weight_in, tower_weight_in, head_in,
    pred_out, dense_grad_out, table_out, in_total, rest_total, weight_grad_out, head_grad_out,
    req, tab, cot, slots, dense, dense_weight, gate_weight, tower_weight, head,
    id_turned, id_send, id_recv, ids, row_send, rows, tab_split, win_all, wout_all, cot_all,
    wh, wl, oh, ol, gate_h, gate_l, tower_h, tower_l, dense_h, dense_l, lists, feat_h, feat_l,
    dense_pad, weight_pad, head_pad,
    inner_h, inner_l, slope, ig_h, ig_l, eo, eslope, ep_h, ep_l, gates, gate_slope, mixed, mixed_grad, pred,
    towers, pre_grads, scores, lgh, lgl, fg, slot_sum,
    in_sums, rest_sums, in_swap, rest_swap, in_pieces, rest_pieces,
    message, got, weight_part, weight_swap, weight_got, weight_total, hot_rows, hot_slots,
    local_sem, y_ssem, y_rsem, p_ssem, p_rsem, c_ssem, c_rsem, wo_ssem, wo_rsem, woc_ssem, woc_rsem, cot_ssem, cot_rsem,
    id_ssem, id_rsem, row_ssem, row_rsem, slot_ssem, slot_rsem, weight_ssem, weight_rsem, weight_send, weight_recv,
    swap_ssem, swap_rsem, piece_ssem, piece_rsem, full_ssem, full_rsem, last_ssem, last_rsem,
):
    b, h = lax.axis_index("batch"), lax.axis_index("hidden")
    core, x, z, chip = lax.rem(b, 2), lax.rem(b // 2, 4), b // 8, b // 2
    me = b * HIDDEN + h
    sibling = b + 1 - 2 * core
    zs = [lax.rem(z + d, 4) * 8 for d in range(4)]
    xs = [lax.rem(x + d, 4) * 2 for d in range(4)]
    cores = [core, 1 - core]
    hs = [lax.rem(h + d, HIDDEN) for d in range(HIDDEN)]
    chips = [(zs[dz] + xs[dx]) // 2 for dz, dx in CHIPS]
    plane = [zs[dz] + xs[dx] + cores[dc] for dz, dx, dc in PLANE]
    order = (1, 3, 2)
    block = pl.when(core >= 0)

    def bring(source, home, i):
        copy = pltpu.make_async_copy(source, home, local_sem.at[i])
        copy.start()
        return copy

    def units_of(s, e):
        return pl.ds(pl.multiple_of(s * 512 + e * UNITS, UNITS), UNITS)

    def block_of(s):
        return pl.ds(pl.multiple_of(s * 512, 512), 512)

    req_copy = bring(req_in, req, 0)
    barrier = pltpu.get_barrier_semaphore()
    for other in plane:
        pl.semaphore_signal(barrier, inc=1, device_id=target(other, h), device_id_type=MESH)
    for i in (2, 1, 3):
        pl.semaphore_signal(barrier, inc=1, device_id=target(b, hs[i]), device_id_type=MESH)
    tab_copy = bring(tab_in, tab, 1)
    win_copy = bring(win, win_all.at[h], 2)
    wout_copy = bring(wout, wout_all.at[h], 3)
    small = ((cot_in, cot), (slots_in, slots), (dense_in, dense), (dense_weight_in, dense_weight),
             (gate_weight_in, gate_weight), (tower_weight_in, tower_weight), (head_in, head))
    small_copies = [bring(source, home, 4 + i) for i, (source, home) in enumerate(small)]
    req_copy.wait()
    id_turned[...] = jnp.concatenate([req[...]] * 4, 0).T
    id_send[...] = id_turned[pl.ds(h, BATCH, stride=HIDDEN), :]
    pl.semaphore_wait(barrier, BATCH - 1 + HIDDEN - 1)

    for other in plane:
        remote(id_send.at[pl.ds(other, 1)], id_recv.at[pl.ds(b, 1)], id_ssem, id_rsem, other, h).start()
    spots = (
        pl.ds(pl.multiple_of(core * 128 + x * 32, 32), 32),
        pl.ds(pl.multiple_of(256 + core * 128 + z * 32, 32), 32),
    )
    spans = (pl.ds(pl.multiple_of(core * 128, 128), 128), pl.ds(pl.multiple_of(256 + core * 128, 128), 128))
    half = pl.ds(pl.multiple_of(core * 256, 256), 256)
    source_of = [lax.rem(h - i + HIDDEN, HIDDEN) for i in range(HIDDEN)]
    for i in order:
        for spot in spots:
            remote(win.at[spot], win_all.at[h, spot], y_ssem, y_rsem.at[i - 1], b, hs[i]).start()

    def spread(i):
        source = source_of[i]
        bulk_wait(win_all.at[source, pl.ds(0, 64)], y_rsem.at[i - 1])
        for j in (2, 1, 3):
            for spot, other in ((spots[0], z * 8 + xs[j] + core), (spots[1], zs[j] + x * 2 + core)):
                piece = win_all.at[source, spot]
                remote(piece, piece, p_ssem, p_rsem.at[i - 1], other, h).start()

    def to_core(i):
        source = source_of[i]
        bulk_wait(win_all.at[source, pl.ds(0, 192)], p_rsem.at[i - 1])
        for span in spans:
            piece = win_all.at[source, span]
            remote(piece, piece, c_ssem, c_rsem.at[i - 1], sibling, h).start()

    def out_to_core(i):
        bulk_wait(wout_all.at[source_of[i], half], wo_rsem.at[i - 1])
        piece = wout_all.at[source_of[i], half]
        remote(piece, piece, woc_ssem, woc_rsem, sibling, h).start()

    tab_copy.wait()

    @block
    def _():
        high, low = split(tab[...])
        tab_split[0:EMBED, :] = high
        tab_split[EMBED : 2 * EMBED, :] = low

    id_recv[pl.ds(b, 1), :] = id_send[pl.ds(b, 1), :]
    bulk_wait(id_recv.at[pl.ds(0, BATCH - 1)], id_rsem)

    @block
    def _():
        found = ids_by_query(id_recv[...])
        ids[...] = found
        table, row = found // ROWS, lax.rem(found, ROWS)
        entries = []
        for pair in range(4):
            hot = jnp.concatenate([hot_of(row[j : j + 1, :], ROWS) for j in (2 * pair, 2 * pair + 1)], 1)
            value = dot_nn(tab_split[...], hot)
            for part in range(2):
                wanted = table[2 * pair + part : 2 * pair + part + 1, :]
                entry = jnp.zeros((ENTRY, 128), f32)
                for t in range(TABLES):
                    high = value[t * ENTRY : (t + 1) * ENTRY, part * 128 : part * 128 + 128]
                    low = value[EMBED + t * ENTRY : EMBED + (t + 1) * ENTRY, part * 128 : part * 128 + 128]
                    entry = jnp.where(wanted == t, high + low, entry)
                entries.append(entry)
        turned = jnp.concatenate(entries, 0).T
        for q in range(4):
            row_send[pl.ds(q, BATCH, stride=4), :] = turned[q * 32 : q * 32 + 32, :]

    mine = pl.ds(me * 4, 4)
    for dz, dx, dc, dy in EVERYWHERE:
        group = zs[dz] + xs[dx] + cores[dc]
        remote(row_send.at[pl.ds(group * 4, 4)], rows.at[mine], row_ssem, row_rsem, group, hs[dy]).start()
    rows[mine, :] = row_send[pl.ds(b * 4, 4), :]
    for i in order:
        spread(i)
    for copy in small_copies:
        copy.wait()
    wout_copy.wait()
    for i in order:
        remote(cot, cot_all.at[h], cot_ssem, cot_rsem, b, hs[i]).start()
        piece = wout_all.at[h, half]
        remote(piece, piece, wo_ssem, wo_rsem.at[i - 1], b, hs[i]).start()
    win_copy.wait()

    @block
    def _():
        cot_all[pl.ds(h, 1)] = cot[...].reshape(1, TASKS, 128)
        dense_pad[...] = jnp.zeros_like(dense_pad)
        dense_pad[0:DENSE, :] = dense[...]
        weight_pad[...] = jnp.zeros_like(weight_pad)
        weight_pad[0:DENSE, 0:PROJ] = dense_weight[...]
        head_pad[...] = jnp.zeros_like(head_pad)
        head_pad[0:TASKS, 0:TOWER] = head[...]
        dense_h[...], dense_l[...] = split(dense_pad[...])
        projected = dot3_nn(split(weight_pad[...].T), (dense_h[...], dense_l[...]))
        feat_h[EMBED:WIDTH, :], feat_l[EMBED:WIDTH, :] = split(projected[0:PROJ, :])
        tower_h[...], tower_l[...] = split(tower_weight[...])
        gate_h[...], gate_l[...] = split(gate_weight[...])
        wh[block_of(h), :], wl[block_of(h), :] = split(win_all[h])

    @block
    def _():
        row = lax.rem(ids[...], ROWS)
        for j in range(8):
            hot_rows[:, j * 128 : (j + 1) * 128] = hot_of(row[j : j + 1, :], ROWS)

    @block
    def _():
        for t in range(TABLES):
            slot = slots[t : t + 1, :]
            owner = slot // 32
            code = jnp.where(lax.rem(owner, HIDDEN) == h, lax.rem(slot, 32) // 8 * 32 + owner // HIDDEN, -1)
            hot_slots[:, t * EXAMPLES : (t + 1) * EXAMPLES] = hot_of(code, 128)

    bulk_wait(rows.at[pl.ds(0, (DEVICES - 1) * 4)], row_rsem)

    def gather(first, last):
        for t in range(first, last):
            slot = slots[t : t + 1, :]
            low = lax.rem(slot, 8)
            value = dot_nn(lists[...], hot_of(lax.rem(slot, 32) // 8 * 128 + slot // 32, 512))
            high_sum = jnp.zeros((ENTRY, EXAMPLES), f32)
            low_sum = jnp.zeros((ENTRY, EXAMPLES), f32)
            for j in range(8):
                high_sum = jnp.where(low == j, value[j * 16 : j * 16 + 16, :], high_sum)
                low_sum = jnp.where(low == j, value[128 + j * 16 : 128 + j * 16 + 16, :], low_sum)
            feat_h[t * ENTRY : (t + 1) * ENTRY, :] = high_sum.astype(bf16)
            feat_l[t * ENTRY : (t + 1) * ENTRY, :] = low_sum.astype(bf16)

    @block
    def _():
        for q in range(4):
            at = slice(q * 128, q * 128 + 128)
            lists[0:128, at], lists[128:256, at] = split(rows[pl.ds(q, DEVICES, stride=4), :].T)
        gather(0, 13)

    to_core(1)
    block(lambda: gather(13, TABLES))

    def first_layer(s):
        at = block_of(s)
        inner, slope[at, :] = silu_both(dot3_nn((wh[at, :], wl[at, :]), (feat_h[...], feat_l[...])))
        inner_h[at, :], inner_l[at, :] = split(inner)

    def next_layer(*which):
        for i in which:
            bulk_wait(win_all.at[source_of[i], pl.ds(0, 256)], c_rsem.at[i - 1])

        @block
        def _():
            for i in which:
                s = source_of[i]
                wh[block_of(s), :], wl[block_of(s), :] = split(win_all[s])
                first_layer(s)

    @block
    def _():
        first_layer(h)
        logits = dot3_nn((gate_h[...], gate_l[...]), (feat_h[...], feat_l[...]))
        for k in range(TASKS):
            part = logits[k * 8 : k * 8 + 8, :]
            raised = jnp.exp(part - jnp.max(part, axis=0, keepdims=True))
            gates[k * 8 : k * 8 + 8, :] = raised / jnp.sum(raised, axis=0, keepdims=True)

    to_core(3)
    next_layer(1)
    to_core(2)
    next_layer(3)
    for i in order:
        out_to_core(i)
    next_layer(2)
    bulk_wait(wout_all.at[pl.ds(0, 3), pl.ds(0, 256)], woc_rsem)
    bulk_wait(cot_all.at[pl.ds(0, 3)], cot_rsem)

    def of_expert(refs, e):
        return tuple(
            jnp.concatenate([ref[s * 512 + e * UNITS : s * 512 + (e + 1) * UNITS, :] for s in range(HIDDEN)], 0)
            for ref in refs
        )

    @block
    def _():
        mixed[...] = jnp.zeros_like(mixed)
        for s in range(HIDDEN):
            at = slice(s * 512, s * 512 + 512)
            oh[at, :], ol[at, :] = split(wout_all[s])
        for e in range(EXPERTS):
            outputs, eslope[e] = silu_both(dot3_tn(of_expert((oh, ol), e), of_expert((inner_h, inner_l), e)))
            eo[e] = outputs
            for k in range(TASKS):
                mixed[k] = mixed[k] + gates[k * 8 + e : k * 8 + e + 1, :] * outputs

    @block
    def _():
        head_turned = head_pad[...].T
        scores[...] = jnp.zeros_like(scores)
        for k in range(TASKS):
            at = slice(k * TOWER, (k + 1) * TOWER)
            value, tower_slope = silu_both(dot3_nn((tower_h[at, :], tower_l[at, :]), split(mixed[k])))
            column = jnp.broadcast_to(head_turned[0:TOWER, k : k + 1], (TOWER, EXAMPLES))
            predicted = sigmoid(jnp.sum(value * column, axis=0, keepdims=True))
            pred[k : k + 1, :] = predicted
            cotangent = jnp.concatenate([cot_all[i, k : k + 1, :] for i in range(HIDDEN)], 1)
            score = cotangent * predicted * (1.0 - predicted)
            scores[k : k + 1, :] = score
            towers[at, :] = value
            pre_grad = score * column * tower_slope
            pre_grads[at, :] = pre_grad
            mixed_grad[k] = dot3_tn((tower_h[at, :], tower_l[at, :]), split(pre_grad))

    def expert_grads(first, last):
        for e in range(first, last):
            outputs = eo[e]
            grad = jnp.zeros((OUT, EXAMPLES), f32)
            for k in range(TASKS):
                gate_slope[k * 8 + e : k * 8 + e + 1, :] = jnp.sum(mixed_grad[k] * outputs, axis=0, keepdims=True)
                grad = grad + gates[k * 8 + e : k * 8 + e + 1, :] * mixed_grad[k]
            out_split = split(grad * eslope[e])
            ep_h[e], ep_l[e] = out_split
            at = units_of(h, e)
            ig_h[at, :], ig_l[at, :] = split(dot3_nn((oh[at, :], ol[at, :]), out_split) * slope[at, :])

    def other_grads():
        for e in range(EXPERTS):
            places = [units_of(source_of[i], e) for i in order]
            side = tuple(jnp.concatenate([ref[at, :] for at in places], 0) for ref in (oh, ol))
            inner_grad = dot3_nn(side, (ep_h[e], ep_l[e]))
            for n, at in enumerate(places):
                ig_h[at, :], ig_l[at, :] = split(inner_grad[n * UNITS : (n + 1) * UNITS, :] * slope[at, :])

    def first_layer_grad(first, last):
        count = (last - first) * UNITS
        at = pl.ds(pl.multiple_of(h * 512 + first * UNITS, UNITS), count)
        ig, ig_low = ig_h[at, :], ig_l[at, :]
        in_grad = dot_nt(jnp.concatenate([ig, ig_low], 0), feat_h[...])
        in_grad = in_grad[0:count, :] + in_grad[count : 2 * count, :] + dot_nt(ig, feat_l[...])
        for q in range(4):
            start = 4 * first * UNITS + q * count
            in_sums[start : start + count, :] = in_grad[:, q * 128 : (q + 1) * 128]

    parts = []
    for first, last in IN_PARTS:
        start, size = 4 * first * UNITS, 4 * (last - first) * UNITS
        whole, halves = pl.ds(start, size), pl.ds(start // 2, size // 2)
        parts.append((in_sums.at[whole], in_swap.at[halves], in_pieces.at[halves], in_total.at[whole], size // 32))
    parts.append((rest_sums, rest_swap, rest_pieces, rest_total, REST_PIECE))

    def swap(n):
        sums, swapped, _, _, piece = parts[n]
        half_rows = 16 * piece
        theirs = sums.at[pl.ds(pl.multiple_of((1 - core) * half_rows, 8), half_rows)]
        remote(theirs, swapped, swap_ssem, swap_rsem.at[n], sibling, h).start()

    def send_pieces(n):
        sums, swapped, pieces, _, piece = parts[n]
        half_rows = 16 * piece
        bulk_wait(swapped, swap_rsem.at[n])
        swapped[...] += sums[pl.ds(pl.multiple_of(core * half_rows, 8), half_rows), :]
        own = pl.ds(pl.multiple_of(chip * piece, 8), piece)
        for other in chips:
            remote(
                swapped.at[pl.ds(pl.multiple_of(other * piece, 8), piece)], pieces.at[own],
                piece_ssem, piece_rsem.at[n], other * 2 + core, h,
            ).start()
        pieces[own, :] = swapped[own, :]

    def send_sums(n):
        _, _, pieces, total, piece = parts[n]
        half_rows = 16 * piece
        bulk_wait(pieces.at[pl.ds(0, 15 * piece)], piece_rsem.at[n])
        value = pieces[0:piece, :]
        for i in range(1, 16):
            value = value + pieces[i * piece : (i + 1) * piece, :]
        at = pl.ds(pl.multiple_of(core * half_rows + chip * piece, 8), piece)
        total[at, :] = value
        for other in chips:
            remote(total.at[at], total.at[at], full_ssem, full_rsem.at[n], other * 2 + core, h).start()

    def hand_on(n):
        _, _, _, total, piece = parts[n]
        bulk_wait(total.at[pl.ds(0, 15 * piece)], full_rsem.at[n])
        ours = total.at[pl.ds(pl.multiple_of(core * 16 * piece, 8), 16 * piece)]
        remote(ours, ours, last_ssem, last_rsem, sibling, h).start()

    for n, (first, last) in enumerate(IN_PARTS):

        @block
        def _():
            expert_grads(first, last)
            first_layer_grad(first, last)

        swap(n)
        if n:
            send_pieces(n - 1)

    @block
    def _():
        for k in range(TASKS):
            at = slice(k * TOWER, (k + 1) * TOWER)
            rest_sums[TOWER_AT + k * TOWER : TOWER_AT + (k + 1) * TOWER, :] = dot3_nt(
                split(pre_grads[at, :]), split(mixed[k])
            )
        head_rows = dot3_nt(split(scores[...]), split(towers[...]))
        rest_sums[HEAD_AT:REST_ROWS, :] = jnp.zeros((REST_ROWS - HEAD_AT, 128), f32)
        rest_sums[HEAD_AT : HEAD_AT + 1, :] = jnp.where(
            iota((1, 128), 1) < TOWER, head_rows[0:1, :], head_rows[1:2, :]
        )
        logit_grads = []
        for k in range(TASKS):
            gate, slopes = gates[k * 8 : k * 8 + 8, :], gate_slope[k * 8 : k * 8 + 8, :]
            logit_grads.append(gate * (slopes - jnp.sum(gate * slopes, axis=0, keepdims=True)))
        lgh[...], lgl[...] = split(jnp.concatenate(logit_grads, 0))
        gate_grad = dot3_nt((lgh[...], lgl[...]), (feat_h[...], feat_l[...]))
        for q in range(4):
            rest_sums[GATE_AT + q * 16 : GATE_AT + q * 16 + 16, :] = gate_grad[:, q * 128 : (q + 1) * 128]

    send_pieces(2)

    @block
    def _():
        for e in range(EXPERTS):
            at = units_of(h, e)
            rest_sums[OUT_AT + e * UNITS : OUT_AT + (e + 1) * UNITS, :] = dot3_nt(
                (inner_h[at, :], inner_l[at, :]), (ep_h[e], ep_l[e])
            )

    swap(3)

    def feature_grad(low, high):
        at = slice(low, high)
        fg[at, :] = dot3_tn((wh[:, at], wl[:, at]), (ig_h[...], ig_l[...])) + dot3_tn(
            (gate_h[:, at], gate_l[:, at]), (lgh[...], lgl[...])
        )

    def scatter(first, last):
        spreads = []
        for t in range(first, last):
            low = lax.rem(slots[t : t + 1, :], 8)
            high, rest = split(fg[t * ENTRY : (t + 1) * ENTRY, :])
            where = jnp.broadcast_to(low, (ENTRY, EXAMPLES)).astype(jnp.int16)
            nothing = jnp.zeros((ENTRY, EXAMPLES), bf16)
            spreads.append(
                jnp.concatenate([jnp.where(where == j, value, nothing) for value in (high, rest) for j in range(8)], 0)
            )
        return dot_nt(jnp.concatenate(spreads, 1), hot_slots[:, first * EXAMPLES : last * EXAMPLES])

    block(other_grads)
    send_pieces(3)
    block(lambda: feature_grad(256, WIDTH))
    send_sums(0)

    @block
    def _():
        projected_grad = split(jnp.concatenate([fg[EMBED:WIDTH, :], jnp.zeros((32, EXAMPLES), f32)], 0))
        weight_part[...] = dot3_nt((dense_h[...], dense_l[...]), projected_grad)[0:16, :]
        dense_grad_out[...] = dot3_nn(split(weight_pad[...]), projected_grad)[0:DENSE, :]

    weight_copies = [
        remote(
            weight_part.at[pl.ds(pl.multiple_of((1 - core) * 8, 8), 8)], weight_swap,
            weight_send.at[0], weight_recv.at[0], sibling, h,
        )
    ]
    weight_copies[0].start()

    @block
    def _():
        slot_sum[...] = scatter(16, TABLES)

    weight_copies[0].wait_recv()
    weight_swap[...] += weight_part[pl.ds(pl.multiple_of(core * 8, 8), 8), :]
    weight_at = pl.ds(pl.multiple_of(chip * 8, 8), 8)
    for other in chips:
        remote(weight_swap, weight_got.at[weight_at], weight_ssem, weight_rsem, other * 2 + core, h).start()
    weight_got[weight_at, :] = weight_swap[...]
    send_sums(1)
    block(lambda: feature_grad(0, 256))

    @block
    def _():
        slot_turned = slot_sum[...] + scatter(0, 16)
        slot_turned = (slot_turned[0:128, :] + slot_turned[128:256, :]).T
        for q in range(4):
            message[pl.ds(q, BATCH, stride=4), :] = slot_turned[q * 32 : q * 32 + 32, :]

    for other in plane:
        remote(message.at[pl.ds(other * 4, 4)], got.at[pl.ds(b * 4, 4)], slot_ssem, slot_rsem, other, h).start()
    got[pl.ds(b * 4, 4), :] = message[pl.ds(b * 4, 4), :]
    send_sums(2)
    send_sums(3)
    bulk_wait(weight_got.at[pl.ds(0, 15 * 8)], weight_rsem)
    value = weight_got[0:8, :]
    for i in range(1, 16):
        value = value + weight_got[i * 8 : i * 8 + 8, :]
    weight_at = pl.ds(pl.multiple_of(core * 8, 8), 8)
    weight_total[weight_at, :] = value
    weight_copies.append(
        remote(
            weight_total.at[weight_at], weight_total.at[weight_at], weight_send.at[1], weight_recv.at[1], sibling, h
        )
    )
    weight_copies[1].start()
    for k in range(TASKS):
        pred_out[k : k + 1, :] = pred[k : k + 1, pl.ds(pl.multiple_of(h * 128, 128), 128)]

    hand_on(0)
    hand_on(1)
    bulk_wait(got.at[pl.ds(0, (BATCH - 1) * 4)], slot_rsem)

    @block
    def _():
        high, rest = split(jnp.concatenate([got[pl.ds(q, BATCH, stride=4), :] for q in range(4)], 0).T)
        table = ids[...] // ROWS
        spreads = []
        for j in range(8):
            where = jnp.broadcast_to(table[j : j + 1, :], (ENTRY, 128)).astype(jnp.int16)
            nothing = jnp.zeros((ENTRY, 128), bf16)
            chosen = [
                jnp.where(where == t, value[j * 16 : j * 16 + 16, :], nothing)
                for value in (high, rest)
                for t in range(TABLES)
            ]
            spreads.append(jnp.concatenate(chosen, 0))
        both = dot_nt(jnp.concatenate(spreads, 1), hot_rows[...])
        table_out[...] = both[0:EMBED, :] + both[EMBED : 2 * EMBED, :]

    weight_copies[1].wait_recv()
    weight_grad_out[...] = weight_total[0:DENSE, 0:PROJ]
    hand_on(2)
    hand_on(3)
    whole = in_total.at[pl.ds(0, IN_ROWS // 2 + 16 * REST_PIECE)]
    bulk_wait(whole, last_rsem)
    head_grad_out[0:1, :] = rest_total[HEAD_AT : HEAD_AT + 1, 0:TOWER]
    head_grad_out[1:2, :] = rest_total[HEAD_AT : HEAD_AT + 1, TOWER : 2 * TOWER]
    most = in_total.at[pl.ds(0, 15 * (IN_ROWS // 32 + REST_PIECE))]
    bulk_wait(most, full_ssem)
    bulk_wait(most, piece_ssem)
    bulk_wait(whole, swap_ssem)
    bulk_wait(whole, last_ssem)
    for copy in weight_copies:
        copy.wait_send()
    bulk_wait(weight_got.at[pl.ds(0, 15 * 8)], weight_ssem)
    bulk_wait(message.at[pl.ds(0, (BATCH - 1) * 4)], slot_ssem)
    bulk_wait(rows.at[pl.ds(0, (DEVICES - 1) * 4)], row_ssem)
    bulk_wait(id_send.at[pl.ds(0, BATCH - 1)], id_ssem)
    bulk_wait(win_all.at[0, pl.ds(0, 192)], y_ssem)
    bulk_wait(win_all.at[pl.ds(0, 3), pl.ds(0, 192)], p_ssem)
    bulk_wait(win_all.at[pl.ds(0, 3), pl.ds(0, 256)], c_ssem)
    bulk_wait(wout_all.at[pl.ds(0, 3), pl.ds(0, 256)], wo_ssem)
    bulk_wait(wout_all.at[pl.ds(0, 3), pl.ds(0, 256)], woc_ssem)
    bulk_wait(cot_all.at[pl.ds(0, 3)], cot_ssem)


def write_kernel(
    table, in_total, rest_total, weight_grad, head_grad, pred, dense_grad,
    table_out, in_out, out_out, tower_out, gate_out, weight_out, head_out, pred_out, dense_out, sems,
):
    copies = [(table, table_out), (rest_total.at[OUT_AT:GATE_AT], out_out), (rest_total.at[TOWER_AT:HEAD_AT], tower_out)]
    copies += [
        (
            in_total.at[pl.ds((4 * first + q * (last - first)) * UNITS, (last - first) * UNITS)],
            in_out.at[first * UNITS : last * UNITS, q * 128 : (q + 1) * 128],
        )
        for first, last in IN_PARTS
        for q in range(4)
    ]
    copies += [
        (rest_total.at[GATE_AT + q * 16 : GATE_AT + q * 16 + 16], gate_out.at[:, q * 128 : q * 128 + 128])
        for q in range(4)
    ]
    copies += [(weight_grad, weight_out), (head_grad, head_out), (pred, pred_out), (dense_grad, dense_out)]
    copies = [pltpu.make_async_copy(source, home, sems.at[i]) for i, (source, home) in enumerate(copies)]
    for copy in copies:
        copy.start()
    for copy in copies:
        copy.wait()


def on_device(
    tables, dense, dense_weight, expert_in, expert_out, gate_weight, tower_weight, head_weight, slots, requests, pred_cot
):
    i32 = jnp.int32
    dma = pltpu.SemaphoreType.DMA
    vmem = pltpu.VMEM
    anywhere = pl.BlockSpec(memory_space=pl.ANY)
    arrays = (
        requests[0].T,
        tables.transpose(0, 2, 1).reshape(EMBED, ROWS),
        expert_in.transpose(1, 2, 0).reshape(EXPERTS * UNITS, WIDTH),
        expert_out.reshape(EXPERTS * UNITS, OUT),
        pred_cot.T,
        slots.T,
        dense.T,
        dense_weight,
        gate_weight.transpose(0, 2, 1).reshape(TASKS * EXPERTS, WIDTH),
        tower_weight.transpose(0, 2, 1).reshape(TASKS * TOWER, OUT),
        head_weight,
    )
    shape = lambda *dims: jax.ShapeDtypeStruct(dims, f32)
    units = HIDDEN * 512, EXAMPLES
    outputs = EXPERTS, OUT, EXAMPLES
    results = pl.pallas_call(
        model_kernel,
        out_shape=[
            vmem((TASKS, 128), f32), vmem((DENSE, EXAMPLES), f32), vmem((EMBED, ROWS), f32), vmem((IN_ROWS, 128), f32),
            vmem((REST_ROWS, 128), f32), vmem((DENSE, PROJ), f32), vmem((TASKS, TOWER), f32),
        ],
        in_specs=[anywhere] * 11,
        out_specs=[VMEM] * 7,
        scratch_shapes=[
            vmem((32, 128), i32), vmem((EMBED, ROWS), f32), vmem((TASKS, 128), f32), vmem((TABLES, EXAMPLES), i32),
            vmem((DENSE, EXAMPLES), f32), vmem((DENSE, PROJ), f32), vmem((16, WIDTH), f32), vmem((128, OUT), f32),
            vmem((TASKS, TOWER), f32),
            vmem((128, 128), i32), vmem((32, 128), i32), vmem((32, 128), i32), vmem((8, 128), i32), vmem((128, 128), f32),
            vmem((512, 128), f32), vmem((2 * EMBED, ROWS), bf16),
            vmem((HIDDEN, 512, WIDTH), f32), vmem((HIDDEN, 512, OUT), f32), vmem((HIDDEN, TASKS, 128), f32),
            vmem((2048, WIDTH), bf16), vmem((2048, WIDTH), bf16), vmem((2048, OUT), bf16), vmem((2048, OUT), bf16),
            vmem((16, WIDTH), bf16), vmem((16, WIDTH), bf16), vmem((128, OUT), bf16), vmem((128, OUT), bf16),
            vmem((128, EXAMPLES), bf16), vmem((128, EXAMPLES), bf16),
            vmem((256, 512), bf16), vmem((WIDTH, EXAMPLES), bf16), vmem((WIDTH, EXAMPLES), bf16),
            vmem((128, EXAMPLES), f32), vmem((128, 128), f32), vmem((128, 128), f32),
            vmem(units, bf16), vmem(units, bf16), vmem(units, f32), vmem(units, bf16), vmem(units, bf16),
            vmem(outputs, f32), vmem(outputs, f32), vmem(outputs, bf16), vmem(outputs, bf16),
            vmem((16, EXAMPLES), f32), vmem((16, EXAMPLES), f32),
            vmem((TASKS, OUT, EXAMPLES), f32), vmem((TASKS, OUT, EXAMPLES), f32), vmem((TASKS, EXAMPLES), f32),
            vmem((128, EXAMPLES), f32), vmem((128, EXAMPLES), f32), vmem((16, EXAMPLES), f32),
            vmem((16, EXAMPLES), bf16), vmem((16, EXAMPLES), bf16),
            vmem((WIDTH, EXAMPLES), f32), vmem((256, 128), f32),
            vmem((IN_ROWS, 128), f32), vmem((REST_ROWS, 128), f32), vmem((IN_ROWS // 2, 128), f32),
            vmem((16 * REST_PIECE, 128), f32), vmem((IN_ROWS // 2, 128), f32), vmem((16 * REST_PIECE, 128), f32),
            vmem((128, 128), f32), vmem((128, 128), f32), vmem((16, 128), f32), vmem((8, 128), f32),
            vmem((128, 128), f32), vmem((16, 128), f32), vmem((ROWS, ROWS), bf16),
            vmem((128, TABLES * EXAMPLES), bf16),
            dma((11,)), dma, dma((3,)), dma, dma((3,)), dma, dma((3,)), dma, dma((3,)), dma, dma, dma, dma,
            dma, dma, dma, dma, dma, dma, dma, dma, dma((2,)), dma((2,)),
            dma, dma((4,)), dma, dma((4,)), dma, dma((4,)), dma, dma,
        ],
        compiler_params=pltpu.CompilerParams(vmem_limit_bytes=LIMIT, collective_id=0, has_side_effects=True),
        name="model",
    )(*arrays)
    results = [pltpu.with_memory_space_constraint(result, pltpu.VMEM) for result in results]
    pred, dense_grad, table_grad, in_total, rest_total, weight_grad, head_grad = results
    table_grad, in_grad, out_grad, tower_grad, gate_grad, weight_grad, head_grad, pred, dense_grad = pl.pallas_call(
        write_kernel,
        out_shape=[
            shape(EMBED, ROWS), shape(512, WIDTH), shape(512, OUT), shape(TASKS * TOWER, OUT),
            shape(TASKS * EXPERTS, WIDTH), shape(DENSE, PROJ), shape(TASKS, TOWER), shape(TASKS, 128),
            shape(DENSE, EXAMPLES),
        ],
        in_specs=[anywhere] * 7,
        out_specs=[anywhere] * 9,
        scratch_shapes=[dma((23,))],
        compiler_params=pltpu.CompilerParams(vmem_limit_bytes=LIMIT),
        name="write",
    )(table_grad, in_total, rest_total, weight_grad, head_grad, pred, dense_grad)
    return (
        pred.T,
        dense_grad.T,
        table_grad.reshape(TABLES, ENTRY, ROWS).transpose(0, 2, 1),
        weight_grad,
        in_grad.reshape(EXPERTS, UNITS, WIDTH).transpose(2, 0, 1),
        out_grad.reshape(EXPERTS, UNITS, OUT),
        gate_grad.reshape(TASKS, EXPERTS, WIDTH).transpose(0, 2, 1),
        tower_grad.reshape(TASKS, TOWER, OUT).transpose(0, 2, 1),
        head_grad,
    )


def solution(mesh):
    placed = (
        P(None, ("batch", "hidden"), None),
        P("batch", None),
        P(),
        P(None, None, "hidden"),
        P(None, "hidden", None),
        P(),
        P(),
        P(),
        P("batch", None),
        P("batch", None, None),
        P(("batch", "hidden"), None),
    )
    return jax.shard_map(
        on_device,
        mesh=mesh,
        in_specs=placed,
        out_specs=(
            P(("batch", "hidden"), None),
            P("batch", None),
            P(None, ("batch", "hidden"), None),
            P(),
            P(None, None, "hidden"),
            P(None, "hidden", None),
            P(),
            P(),
            P(),
        ),
        check_vma=False,
    )
```

```python
import jax
import jax.numpy as jnp
from jax import lax
from jax.experimental import pallas as pl
from jax.experimental.pallas import tpu as pltpu
from jax.sharding import PartitionSpec as P

f32 = jnp.float32
bf16 = jnp.bfloat16
MESH = pl.DeviceIdType.MESH
VMEM = pl.BlockSpec(memory_space=pltpu.VMEM)
LIMIT = 56 * 2**20

TABLES, ROWS, ENTRY = 26, 1024, 16
BATCH, HIDDEN = 32, 4
DEVICES = BATCH * HIDDEN
EXPERTS, UNITS, OUT, WIDTH = 8, 64, 128, 512
TASKS, TOWER, DENSE, PROJ = 2, 64, 13, 96
EXAMPLES = 512
EMBED = TABLES * ENTRY

IN_PARTS = ((0, 3), (3, 6), (6, 8))
IN_ROWS = 2048
OUT_AT, GATE_AT, TOWER_AT, HEAD_AT = 0, 512, 576, 704
REST_ROWS, REST_PIECE = 768, 24


def split(value):
    high = value.astype(bf16)
    return high, (value - high.astype(f32)).astype(bf16)


def dot_nn(a, b):
    return lax.dot_general(a, b, (((1,), (0,)), ((), ())), preferred_element_type=f32)


def dot_nt(a, b):
    return lax.dot_general(a, b, (((1,), (1,)), ((), ())), preferred_element_type=f32)


def dot_tn(a, b):
    return lax.dot_general(a, b, (((0,), (0,)), ((), ())), preferred_element_type=f32)


def dot3_tn(a, b):
    (ah, al), (bh, bl) = a, b
    return dot_tn(ah, bh) + dot_tn(al, bh) + dot_tn(ah, bl)


def dot3_nn(a, b):
    (ah, al), (bh, bl) = a, b
    return dot_nn(jnp.concatenate([ah, al, ah], 1), jnp.concatenate([bh, bh, bl], 0))


def dot3_nt(a, b):
    (ah, al), (bh, bl) = a, b
    count = ah.shape[0]
    both = dot_nt(jnp.concatenate([ah, al], 0), bh)
    return both[0:count, :] + both[count : 2 * count, :] + dot_nt(ah, bl)


def sigmoid(value):
    return 0.5 * jnp.tanh(0.5 * value) + 0.5


def silu_both(value):
    sigma = sigmoid(value)
    result = value * sigma
    return result, sigma + result * (1.0 - sigma)


def iota(shape, axis):
    return lax.broadcasted_iota(jnp.int32, shape, axis)


def hops(offset):
    return min(offset, 4 - offset)


PLANE = sorted(
    ((dz, dx, dc) for dz in range(4) for dx in range(4) for dc in range(2) if dz or dx or dc),
    key=lambda d: -(2 * hops(d[0]) + 2 * hops(d[1]) + d[2]),
)
EVERYWHERE = sorted(
    ((dz, dx, dc, dy) for dz in range(4) for dx in range(4) for dc in range(2) for dy in range(4) if dz or dx or dc or dy),
    key=lambda d: -(2 * hops(d[0]) + 2 * hops(d[1]) + d[2] + 2 * hops(d[3])),
)
CHIPS = [(dz, dx) for dz, dx, dc in PLANE if not dc and (dz or dx)]


def target(b, h):
    return {"batch": b, "hidden": h}


def remote(src, dst, send, recv, b, h):
    return pltpu.make_async_remote_copy(src, dst, send, recv, device_id=target(b, h), device_id_type=MESH)


def bulk_wait(ref, sem):
    pltpu.make_async_copy(ref, ref, sem).wait()


def ids_by_query(received):
    turned = jnp.concatenate([received] * 4, 0).T
    lane = iota((8, 128), 1) // 32
    out = jnp.zeros((8, 128), jnp.int32)
    for q in range(4):
        out = jnp.where(lane == q, turned[q * 8 : q * 8 + 8, :], out)
    return out


def hot_of(code, count):
    rows = iota((count, code.shape[1]), 0).astype(jnp.int16)
    return jnp.where(rows == code.astype(jnp.int16), bf16(1.0), bf16(0.0))


def model_kernel(
    req_in, tab_in, win, wout, cot_in, slots_in, dense_in, dense_weight_in, gate_weight_in, tower_weight_in, head_in,
    pred_out, dense_grad_out, table_out, in_total, rest_total, weight_grad_out, head_grad_out,
    req, tab, cot, slots, dense, dense_weight, gate_weight, tower_weight, head,
    id_turned, id_send, id_recv, ids, row_send, rows, tab_split, win_all, wout_all, cot_all,
    wh, wl, oh, ol, gate_h, gate_l, tower_h, tower_l, dense_h, dense_l, lists, feat_h, feat_l,
    dense_pad, weight_pad, head_pad,
    inner_h, inner_l, slope, ig_h, ig_l, eo, eslope, ep_h, ep_l, gates, gate_slope, mixed, mixed_grad, pred,
    towers, pre_grads, scores, lgh, lgl, fg, slot_sum,
    in_sums, rest_sums, in_swap, rest_swap, in_pieces, rest_pieces,
    message, got, weight_part, weight_swap, weight_got, weight_total, hot_rows, hot_slots,
    local_sem, y_ssem, y_rsem, p_ssem, p_rsem, c_ssem, c_rsem, wo_ssem, wo_rsem, woc_ssem, woc_rsem, cot_ssem, cot_rsem,
    id_ssem, id_rsem, row_ssem, row_rsem, slot_ssem, slot_rsem, weight_ssem, weight_rsem, weight_send, weight_recv,
    swap_ssem, swap_rsem, piece_ssem, piece_rsem, full_ssem, full_rsem, last_ssem, last_rsem,
):
    b, h = lax.axis_index("batch"), lax.axis_index("hidden")
    core, x, z, chip = lax.rem(b, 2), lax.rem(b // 2, 4), b // 8, b // 2
    me = b * HIDDEN + h
    sibling = b + 1 - 2 * core
    zs = [lax.rem(z + d, 4) * 8 for d in range(4)]
    xs = [lax.rem(x + d, 4) * 2 for d in range(4)]
    cores = [core, 1 - core]
    hs = [lax.rem(h + d, HIDDEN) for d in range(HIDDEN)]
    chips = [(zs[dz] + xs[dx]) // 2 for dz, dx in CHIPS]
    plane = [zs[dz] + xs[dx] + cores[dc] for dz, dx, dc in PLANE]
    order = (1, 3, 2)
    block = pl.when(core >= 0)

    def bring(source, home, i):
        copy = pltpu.make_async_copy(source, home, local_sem.at[i])
        copy.start()
        return copy

    def units_of(s, e):
        return pl.ds(pl.multiple_of(s * 512 + e * UNITS, UNITS), UNITS)

    def block_of(s):
        return pl.ds(pl.multiple_of(s * 512, 512), 512)

    req_copy = bring(req_in, req, 0)
    barrier = pltpu.get_barrier_semaphore()
    for other in plane:
        pl.semaphore_signal(barrier, inc=1, device_id=target(other, h), device_id_type=MESH)
    for i in (2, 1, 3):
        pl.semaphore_signal(barrier, inc=1, device_id=target(b, hs[i]), device_id_type=MESH)
    tab_copy = bring(tab_in, tab, 1)
    win_copy = bring(win, win_all.at[h], 2)
    wout_copy = bring(wout, wout_all.at[h], 3)
    small = ((cot_in, cot), (slots_in, slots), (dense_in, dense), (dense_weight_in, dense_weight),
             (gate_weight_in, gate_weight), (tower_weight_in, tower_weight), (head_in, head))
    small_copies = [bring(source, home, 4 + i) for i, (source, home) in enumerate(small)]
    req_copy.wait()
    id_turned[...] = jnp.concatenate([req[...]] * 4, 0).T
    id_send[...] = id_turned[pl.ds(h, BATCH, stride=HIDDEN), :]
    pl.semaphore_wait(barrier, BATCH - 1 + HIDDEN - 1)

    for other in plane:
        remote(id_send.at[pl.ds(other, 1)], id_recv.at[pl.ds(b, 1)], id_ssem, id_rsem, other, h).start()
    spots = (
        pl.ds(pl.multiple_of(core * 128 + x * 32, 32), 32),
        pl.ds(pl.multiple_of(256 + core * 128 + z * 32, 32), 32),
    )
    spans = (pl.ds(pl.multiple_of(core * 128, 128), 128), pl.ds(pl.multiple_of(256 + core * 128, 128), 128))
    half = pl.ds(pl.multiple_of(core * 256, 256), 256)
    source_of = [lax.rem(h - i + HIDDEN, HIDDEN) for i in range(HIDDEN)]
    for i in order:
        for spot in spots:
            remote(win.at[spot], win_all.at[h, spot], y_ssem, y_rsem.at[i - 1], b, hs[i]).start()

    def spread(i):
        source = source_of[i]
        bulk_wait(win_all.at[source, pl.ds(0, 64)], y_rsem.at[i - 1])
        for j in (2, 1, 3):
            for spot, other in ((spots[0], z * 8 + xs[j] + core), (spots[1], zs[j] + x * 2 + core)):
                piece = win_all.at[source, spot]
                remote(piece, piece, p_ssem, p_rsem.at[i - 1], other, h).start()

    def to_core(i):
        source = source_of[i]
        bulk_wait(win_all.at[source, pl.ds(0, 192)], p_rsem.at[i - 1])
        for span in spans:
            piece = win_all.at[source, span]
            remote(piece, piece, c_ssem, c_rsem.at[i - 1], sibling, h).start()

    def out_to_core(i):
        bulk_wait(wout_all.at[source_of[i], half], wo_rsem.at[i - 1])
        piece = wout_all.at[source_of[i], half]
        remote(piece, piece, woc_ssem, woc_rsem, sibling, h).start()

    tab_copy.wait()

    @block
    def _():
        high, low = split(tab[...])
        tab_split[0:EMBED, :] = high
        tab_split[EMBED : 2 * EMBED, :] = low

    id_recv[pl.ds(b, 1), :] = id_send[pl.ds(b, 1), :]
    bulk_wait(id_recv.at[pl.ds(0, BATCH - 1)], id_rsem)

    @block
    def _():
        found = ids_by_query(id_recv[...])
        ids[...] = found
        table, row = found // ROWS, lax.rem(found, ROWS)
        entries = []
        for pair in range(4):
            hot = jnp.concatenate([hot_of(row[j : j + 1, :], ROWS) for j in (2 * pair, 2 * pair + 1)], 1)
            value = dot_nn(tab_split[...], hot)
            for part in range(2):
                wanted = table[2 * pair + part : 2 * pair + part + 1, :]
                entry = jnp.zeros((ENTRY, 128), f32)
                for t in range(TABLES):
                    high = value[t * ENTRY : (t + 1) * ENTRY, part * 128 : part * 128 + 128]
                    low = value[EMBED + t * ENTRY : EMBED + (t + 1) * ENTRY, part * 128 : part * 128 + 128]
                    entry = jnp.where(wanted == t, high + low, entry)
                entries.append(entry)
        turned = jnp.concatenate(entries, 0).T
        for q in range(4):
            row_send[pl.ds(q, BATCH, stride=4), :] = turned[q * 32 : q * 32 + 32, :]

    mine = pl.ds(me * 4, 4)
    for dz, dx, dc, dy in EVERYWHERE:
        group = zs[dz] + xs[dx] + cores[dc]
        remote(row_send.at[pl.ds(group * 4, 4)], rows.at[mine], row_ssem, row_rsem, group, hs[dy]).start()
    rows[mine, :] = row_send[pl.ds(b * 4, 4), :]
    for i in order:
        spread(i)
    for copy in small_copies:
        copy.wait()
    wout_copy.wait()
    for i in order:
        remote(cot, cot_all.at[h], cot_ssem, cot_rsem, b, hs[i]).start()
        piece = wout_all.at[h, half]
        remote(piece, piece, wo_ssem, wo_rsem.at[i - 1], b, hs[i]).start()
    win_copy.wait()

    @block
    def _():
        cot_all[pl.ds(h, 1)] = cot[...].reshape(1, TASKS, 128)
        dense_pad[...] = jnp.zeros_like(dense_pad)
        dense_pad[0:DENSE, :] = dense[...]
        weight_pad[...] = jnp.zeros_like(weight_pad)
        weight_pad[0:DENSE, 0:PROJ] = dense_weight[...]
        head_pad[...] = jnp.zeros_like(head_pad)
        head_pad[0:TASKS, 0:TOWER] = head[...]
        dense_h[...], dense_l[...] = split(dense_pad[...])
        projected = dot3_nn(split(weight_pad[...].T), (dense_h[...], dense_l[...]))
        feat_h[EMBED:WIDTH, :], feat_l[EMBED:WIDTH, :] = split(projected[0:PROJ, :])
        tower_h[...], tower_l[...] = split(tower_weight[...])
        gate_h[...], gate_l[...] = split(gate_weight[...])
        wh[block_of(h), :], wl[block_of(h), :] = split(win_all[h])

    @block
    def _():
        row = lax.rem(ids[...], ROWS)
        for j in range(8):
            hot_rows[:, j * 128 : (j + 1) * 128] = hot_of(row[j : j + 1, :], ROWS)

    @block
    def _():
        for t in range(TABLES):
            slot = slots[t : t + 1, :]
            owner = slot // 32
            code = jnp.where(lax.rem(owner, HIDDEN) == h, lax.rem(slot, 32) // 8 * 32 + owner // HIDDEN, -1)
            hot_slots[:, t * EXAMPLES : (t + 1) * EXAMPLES] = hot_of(code, 128)

    bulk_wait(rows.at[pl.ds(0, (DEVICES - 1) * 4)], row_rsem)

    def gather(first, last):
        for t in range(first, last):
            slot = slots[t : t + 1, :]
            low = lax.rem(slot, 8)
            value = dot_nn(lists[...], hot_of(lax.rem(slot, 32) // 8 * 128 + slot // 32, 512))
            high_sum = jnp.zeros((ENTRY, EXAMPLES), f32)
            low_sum = jnp.zeros((ENTRY, EXAMPLES), f32)
            for j in range(8):
                high_sum = jnp.where(low == j, value[j * 16 : j * 16 + 16, :], high_sum)
                low_sum = jnp.where(low == j, value[128 + j * 16 : 128 + j * 16 + 16, :], low_sum)
            feat_h[t * ENTRY : (t + 1) * ENTRY, :] = high_sum.astype(bf16)
            feat_l[t * ENTRY : (t + 1) * ENTRY, :] = low_sum.astype(bf16)

    @block
    def _():
        for q in range(4):
            at = slice(q * 128, q * 128 + 128)
            lists[0:128, at], lists[128:256, at] = split(rows[pl.ds(q, DEVICES, stride=4), :].T)
        gather(0, 13)

    to_core(1)
    block(lambda: gather(13, TABLES))

    def first_layer(s):
        at = block_of(s)
        inner, slope[at, :] = silu_both(dot3_nn((wh[at, :], wl[at, :]), (feat_h[...], feat_l[...])))
        inner_h[at, :], inner_l[at, :] = split(inner)

    def next_layer(*which):
        for i in which:
            bulk_wait(win_all.at[source_of[i], pl.ds(0, 256)], c_rsem.at[i - 1])

        @block
        def _():
            for i in which:
                s = source_of[i]
                wh[block_of(s), :], wl[block_of(s), :] = split(win_all[s])
                first_layer(s)

    @block
    def _():
        first_layer(h)
        logits = dot3_nn((gate_h[...], gate_l[...]), (feat_h[...], feat_l[...]))
        for k in range(TASKS):
            part = logits[k * 8 : k * 8 + 8, :]
            raised = jnp.exp(part - jnp.max(part, axis=0, keepdims=True))
            gates[k * 8 : k * 8 + 8, :] = raised / jnp.sum(raised, axis=0, keepdims=True)

    to_core(3)
    next_layer(1)
    to_core(2)
    next_layer(3)
    for i in order:
        out_to_core(i)
    next_layer(2)
    bulk_wait(wout_all.at[pl.ds(0, 3), pl.ds(0, 256)], woc_rsem)
    bulk_wait(cot_all.at[pl.ds(0, 3)], cot_rsem)

    def of_expert(refs, e):
        return tuple(
            jnp.concatenate([ref[s * 512 + e * UNITS : s * 512 + (e + 1) * UNITS, :] for s in range(HIDDEN)], 0)
            for ref in refs
        )

    @block
    def _():
        mixed[...] = jnp.zeros_like(mixed)
        for s in range(HIDDEN):
            at = slice(s * 512, s * 512 + 512)
            oh[at, :], ol[at, :] = split(wout_all[s])
        for e in range(EXPERTS):
            outputs, eslope[e] = silu_both(dot3_tn(of_expert((oh, ol), e), of_expert((inner_h, inner_l), e)))
            eo[e] = outputs
            for k in range(TASKS):
                mixed[k] = mixed[k] + gates[k * 8 + e : k * 8 + e + 1, :] * outputs

    @block
    def _():
        head_turned = head_pad[...].T
        scores[...] = jnp.zeros_like(scores)
        for k in range(TASKS):
            at = slice(k * TOWER, (k + 1) * TOWER)
            value, tower_slope = silu_both(dot3_nn((tower_h[at, :], tower_l[at, :]), split(mixed[k])))
            column = jnp.broadcast_to(head_turned[0:TOWER, k : k + 1], (TOWER, EXAMPLES))
            predicted = sigmoid(jnp.sum(value * column, axis=0, keepdims=True))
            pred[k : k + 1, :] = predicted
            cotangent = jnp.concatenate([cot_all[i, k : k + 1, :] for i in range(HIDDEN)], 1)
            score = cotangent * predicted * (1.0 - predicted)
            scores[k : k + 1, :] = score
            towers[at, :] = value
            pre_grad = score * column * tower_slope
            pre_grads[at, :] = pre_grad
            mixed_grad[k] = dot3_tn((tower_h[at, :], tower_l[at, :]), split(pre_grad))

    def expert_grads(first, last):
        for e in range(first, last):
            outputs = eo[e]
            grad = jnp.zeros((OUT, EXAMPLES), f32)
            for k in range(TASKS):
                gate_slope[k * 8 + e : k * 8 + e + 1, :] = jnp.sum(mixed_grad[k] * outputs, axis=0, keepdims=True)
                grad = grad + gates[k * 8 + e : k * 8 + e + 1, :] * mixed_grad[k]
            out_split = split(grad * eslope[e])
            ep_h[e], ep_l[e] = out_split
            at = units_of(h, e)
            ig_h[at, :], ig_l[at, :] = split(dot3_nn((oh[at, :], ol[at, :]), out_split) * slope[at, :])

    def other_grads():
        for e in range(EXPERTS):
            places = [units_of(source_of[i], e) for i in order]
            side = tuple(jnp.concatenate([ref[at, :] for at in places], 0) for ref in (oh, ol))
            inner_grad = dot3_nn(side, (ep_h[e], ep_l[e]))
            for n, at in enumerate(places):
                ig_h[at, :], ig_l[at, :] = split(inner_grad[n * UNITS : (n + 1) * UNITS, :] * slope[at, :])

    def first_layer_grad(first, last):
        count = (last - first) * UNITS
        at = pl.ds(pl.multiple_of(h * 512 + first * UNITS, UNITS), count)
        in_grad = dot3_nt((ig_h[at, :], ig_l[at, :]), (feat_h[...], feat_l[...]))
        for q in range(4):
            start = 4 * first * UNITS + q * count
            in_sums[start : start + count, :] = in_grad[:, q * 128 : (q + 1) * 128]

    parts = []
    for first, last in IN_PARTS:
        start, size = 4 * first * UNITS, 4 * (last - first) * UNITS
        whole, halves = pl.ds(start, size), pl.ds(start // 2, size // 2)
        parts.append((in_sums.at[whole], in_swap.at[halves], in_pieces.at[halves], in_total.at[whole], size // 32))
    parts.append((rest_sums, rest_swap, rest_pieces, rest_total, REST_PIECE))

    def swap(n):
        sums, swapped, _, _, piece = parts[n]
        half_rows = 16 * piece
        theirs = sums.at[pl.ds(pl.multiple_of((1 - core) * half_rows, 8), half_rows)]
        remote(theirs, swapped, swap_ssem, swap_rsem.at[n], sibling, h).start()

    def send_pieces(n):
        sums, swapped, pieces, _, piece = parts[n]
        half_rows = 16 * piece
        bulk_wait(swapped, swap_rsem.at[n])
        swapped[...] += sums[pl.ds(pl.multiple_of(core * half_rows, 8), half_rows), :]
        own = pl.ds(pl.multiple_of(chip * piece, 8), piece)
        for other in chips:
            remote(
                swapped.at[pl.ds(pl.multiple_of(other * piece, 8), piece)], pieces.at[own],
                piece_ssem, piece_rsem.at[n], other * 2 + core, h,
            ).start()
        pieces[own, :] = swapped[own, :]

    def send_sums(n):
        _, _, pieces, total, piece = parts[n]
        half_rows = 16 * piece
        bulk_wait(pieces.at[pl.ds(0, 15 * piece)], piece_rsem.at[n])
        value = pieces[0:piece, :]
        for i in range(1, 16):
            value = value + pieces[i * piece : (i + 1) * piece, :]
        at = pl.ds(pl.multiple_of(core * half_rows + chip * piece, 8), piece)
        total[at, :] = value
        for other in chips:
            remote(total.at[at], total.at[at], full_ssem, full_rsem.at[n], other * 2 + core, h).start()

    def hand_on(n):
        _, _, _, total, piece = parts[n]
        bulk_wait(total.at[pl.ds(0, 15 * piece)], full_rsem.at[n])
        ours = total.at[pl.ds(pl.multiple_of(core * 16 * piece, 8), 16 * piece)]
        remote(ours, ours, last_ssem, last_rsem, sibling, h).start()

    for n, (first, last) in enumerate(IN_PARTS):

        @block
        def _():
            expert_grads(first, last)
            first_layer_grad(first, last)

        swap(n)
        if n:
            send_pieces(n - 1)

    @block
    def _():
        for k in range(TASKS):
            at = slice(k * TOWER, (k + 1) * TOWER)
            rest_sums[TOWER_AT + k * TOWER : TOWER_AT + (k + 1) * TOWER, :] = dot3_nt(
                split(pre_grads[at, :]), split(mixed[k])
            )
        head_rows = dot3_nt(split(scores[...]), split(towers[...]))
        rest_sums[HEAD_AT:REST_ROWS, :] = jnp.zeros((REST_ROWS - HEAD_AT, 128), f32)
        rest_sums[HEAD_AT : HEAD_AT + 1, :] = jnp.where(
            iota((1, 128), 1) < TOWER, head_rows[0:1, :], head_rows[1:2, :]
        )
        logit_grads = []
        for k in range(TASKS):
            gate, slopes = gates[k * 8 : k * 8 + 8, :], gate_slope[k * 8 : k * 8 + 8, :]
            logit_grads.append(gate * (slopes - jnp.sum(gate * slopes, axis=0, keepdims=True)))
        lgh[...], lgl[...] = split(jnp.concatenate(logit_grads, 0))
        gate_grad = dot3_nt((lgh[...], lgl[...]), (feat_h[...], feat_l[...]))
        for q in range(4):
            rest_sums[GATE_AT + q * 16 : GATE_AT + q * 16 + 16, :] = gate_grad[:, q * 128 : (q + 1) * 128]

    send_pieces(2)

    @block
    def _():
        for e in range(EXPERTS):
            at = units_of(h, e)
            rest_sums[OUT_AT + e * UNITS : OUT_AT + (e + 1) * UNITS, :] = dot3_nt(
                (inner_h[at, :], inner_l[at, :]), (ep_h[e], ep_l[e])
            )

    swap(3)

    def feature_grad(low, high):
        at = slice(low, high)
        fg[at, :] = dot3_tn((wh[:, at], wl[:, at]), (ig_h[...], ig_l[...])) + dot3_tn(
            (gate_h[:, at], gate_l[:, at]), (lgh[...], lgl[...])
        )

    def scatter(first, last):
        spreads = []
        for t in range(first, last):
            low = lax.rem(slots[t : t + 1, :], 8)
            high, rest = split(fg[t * ENTRY : (t + 1) * ENTRY, :])
            where = jnp.broadcast_to(low, (ENTRY, EXAMPLES)).astype(jnp.int16)
            nothing = jnp.zeros((ENTRY, EXAMPLES), bf16)
            spreads.append(
                jnp.concatenate([jnp.where(where == j, value, nothing) for value in (high, rest) for j in range(8)], 0)
            )
        return dot_nt(jnp.concatenate(spreads, 1), hot_slots[:, first * EXAMPLES : last * EXAMPLES])

    block(other_grads)
    send_pieces(3)
    block(lambda: feature_grad(256, WIDTH))
    send_sums(0)

    @block
    def _():
        projected_grad = split(jnp.concatenate([fg[EMBED:WIDTH, :], jnp.zeros((32, EXAMPLES), f32)], 0))
        weight_part[...] = dot3_nt((dense_h[...], dense_l[...]), projected_grad)[0:16, :]
        dense_grad_out[...] = dot3_nn(split(weight_pad[...]), projected_grad)[0:DENSE, :]

    weight_copies = [
        remote(
            weight_part.at[pl.ds(pl.multiple_of((1 - core) * 8, 8), 8)], weight_swap,
            weight_send.at[0], weight_recv.at[0], sibling, h,
        )
    ]
    weight_copies[0].start()

    @block
    def _():
        slot_sum[...] = scatter(16, TABLES)

    weight_copies[0].wait_recv()
    weight_swap[...] += weight_part[pl.ds(pl.multiple_of(core * 8, 8), 8), :]
    weight_at = pl.ds(pl.multiple_of(chip * 8, 8), 8)
    for other in chips:
        remote(weight_swap, weight_got.at[weight_at], weight_ssem, weight_rsem, other * 2 + core, h).start()
    weight_got[weight_at, :] = weight_swap[...]
    send_sums(1)
    block(lambda: feature_grad(0, 256))

    @block
    def _():
        slot_turned = slot_sum[...] + scatter(0, 16)
        slot_turned = (slot_turned[0:128, :] + slot_turned[128:256, :]).T
        for q in range(4):
            message[pl.ds(q, BATCH, stride=4), :] = slot_turned[q * 32 : q * 32 + 32, :]

    for other in plane:
        remote(message.at[pl.ds(other * 4, 4)], got.at[pl.ds(b * 4, 4)], slot_ssem, slot_rsem, other, h).start()
    got[pl.ds(b * 4, 4), :] = message[pl.ds(b * 4, 4), :]
    send_sums(2)
    send_sums(3)
    bulk_wait(weight_got.at[pl.ds(0, 15 * 8)], weight_rsem)
    value = weight_got[0:8, :]
    for i in range(1, 16):
        value = value + weight_got[i * 8 : i * 8 + 8, :]
    weight_at = pl.ds(pl.multiple_of(core * 8, 8), 8)
    weight_total[weight_at, :] = value
    weight_copies.append(
        remote(
            weight_total.at[weight_at], weight_total.at[weight_at], weight_send.at[1], weight_recv.at[1], sibling, h
        )
    )
    weight_copies[1].start()
    for k in range(TASKS):
        pred_out[k : k + 1, :] = pred[k : k + 1, pl.ds(pl.multiple_of(h * 128, 128), 128)]

    hand_on(0)
    hand_on(1)
    bulk_wait(got.at[pl.ds(0, (BATCH - 1) * 4)], slot_rsem)

    @block
    def _():
        high, rest = split(jnp.concatenate([got[pl.ds(q, BATCH, stride=4), :] for q in range(4)], 0).T)
        table = ids[...] // ROWS
        spreads = []
        for j in range(8):
            where = jnp.broadcast_to(table[j : j + 1, :], (ENTRY, 128)).astype(jnp.int16)
            nothing = jnp.zeros((ENTRY, 128), bf16)
            chosen = [
                jnp.where(where == t, value[j * 16 : j * 16 + 16, :], nothing)
                for value in (high, rest)
                for t in range(TABLES)
            ]
            spreads.append(jnp.concatenate(chosen, 0))
        both = dot_nt(jnp.concatenate(spreads, 1), hot_rows[...])
        table_out[...] = both[0:EMBED, :] + both[EMBED : 2 * EMBED, :]

    weight_copies[1].wait_recv()
    weight_grad_out[...] = weight_total[0:DENSE, 0:PROJ]
    hand_on(2)
    hand_on(3)
    whole = in_total.at[pl.ds(0, IN_ROWS // 2 + 16 * REST_PIECE)]
    bulk_wait(whole, last_rsem)
    head_grad_out[0:1, :] = rest_total[HEAD_AT : HEAD_AT + 1, 0:TOWER]
    head_grad_out[1:2, :] = rest_total[HEAD_AT : HEAD_AT + 1, TOWER : 2 * TOWER]
    most = in_total.at[pl.ds(0, 15 * (IN_ROWS // 32 + REST_PIECE))]
    bulk_wait(most, full_ssem)
    bulk_wait(most, piece_ssem)
    bulk_wait(whole, swap_ssem)
    bulk_wait(whole, last_ssem)
    for copy in weight_copies:
        copy.wait_send()
    bulk_wait(weight_got.at[pl.ds(0, 15 * 8)], weight_ssem)
    bulk_wait(message.at[pl.ds(0, (BATCH - 1) * 4)], slot_ssem)
    bulk_wait(rows.at[pl.ds(0, (DEVICES - 1) * 4)], row_ssem)
    bulk_wait(id_send.at[pl.ds(0, BATCH - 1)], id_ssem)
    bulk_wait(win_all.at[0, pl.ds(0, 192)], y_ssem)
    bulk_wait(win_all.at[pl.ds(0, 3), pl.ds(0, 192)], p_ssem)
    bulk_wait(win_all.at[pl.ds(0, 3), pl.ds(0, 256)], c_ssem)
    bulk_wait(wout_all.at[pl.ds(0, 3), pl.ds(0, 256)], wo_ssem)
    bulk_wait(wout_all.at[pl.ds(0, 3), pl.ds(0, 256)], woc_ssem)
    bulk_wait(cot_all.at[pl.ds(0, 3)], cot_ssem)


def write_kernel(
    table, in_total, rest_total, weight_grad, head_grad, pred, dense_grad,
    table_out, in_out, out_out, tower_out, gate_out, weight_out, head_out, pred_out, dense_out, sems,
):
    copies = [(table, table_out), (rest_total.at[OUT_AT:GATE_AT], out_out), (rest_total.at[TOWER_AT:HEAD_AT], tower_out)]
    copies += [
        (
            in_total.at[pl.ds((4 * first + q * (last - first)) * UNITS, (last - first) * UNITS)],
            in_out.at[first * UNITS : last * UNITS, q * 128 : (q + 1) * 128],
        )
        for first, last in IN_PARTS
        for q in range(4)
    ]
    copies += [
        (rest_total.at[GATE_AT + q * 16 : GATE_AT + q * 16 + 16], gate_out.at[:, q * 128 : q * 128 + 128])
        for q in range(4)
    ]
    copies += [(weight_grad, weight_out), (head_grad, head_out), (pred, pred_out), (dense_grad, dense_out)]
    copies = [pltpu.make_async_copy(source, home, sems.at[i]) for i, (source, home) in enumerate(copies)]
    for copy in copies:
        copy.start()
    for copy in copies:
        copy.wait()


def on_device(
    tables, dense, dense_weight, expert_in, expert_out, gate_weight, tower_weight, head_weight, slots, requests, pred_cot
):
    i32 = jnp.int32
    dma = pltpu.SemaphoreType.DMA
    vmem = pltpu.VMEM
    anywhere = pl.BlockSpec(memory_space=pl.ANY)
    arrays = (
        requests[0].T,
        tables.transpose(0, 2, 1).reshape(EMBED, ROWS),
        expert_in.transpose(1, 2, 0).reshape(EXPERTS * UNITS, WIDTH),
        expert_out.reshape(EXPERTS * UNITS, OUT),
        pred_cot.T,
        slots.T,
        dense.T,
        dense_weight,
        gate_weight.transpose(0, 2, 1).reshape(TASKS * EXPERTS, WIDTH),
        tower_weight.transpose(0, 2, 1).reshape(TASKS * TOWER, OUT),
        head_weight,
    )
    shape = lambda *dims: jax.ShapeDtypeStruct(dims, f32)
    units = HIDDEN * 512, EXAMPLES
    outputs = EXPERTS, OUT, EXAMPLES
    results = pl.pallas_call(
        model_kernel,
        out_shape=[
            vmem((TASKS, 128), f32), vmem((DENSE, EXAMPLES), f32), vmem((EMBED, ROWS), f32), vmem((IN_ROWS, 128), f32),
            vmem((REST_ROWS, 128), f32), vmem((DENSE, PROJ), f32), vmem((TASKS, TOWER), f32),
        ],
        in_specs=[anywhere] * 11,
        out_specs=[VMEM] * 7,
        scratch_shapes=[
            vmem((32, 128), i32), vmem((EMBED, ROWS), f32), vmem((TASKS, 128), f32), vmem((TABLES, EXAMPLES), i32),
            vmem((DENSE, EXAMPLES), f32), vmem((DENSE, PROJ), f32), vmem((16, WIDTH), f32), vmem((128, OUT), f32),
            vmem((TASKS, TOWER), f32),
            vmem((128, 128), i32), vmem((32, 128), i32), vmem((32, 128), i32), vmem((8, 128), i32), vmem((128, 128), f32),
            vmem((512, 128), f32), vmem((2 * EMBED, ROWS), bf16),
            vmem((HIDDEN, 512, WIDTH), f32), vmem((HIDDEN, 512, OUT), f32), vmem((HIDDEN, TASKS, 128), f32),
            vmem((2048, WIDTH), bf16), vmem((2048, WIDTH), bf16), vmem((2048, OUT), bf16), vmem((2048, OUT), bf16),
            vmem((16, WIDTH), bf16), vmem((16, WIDTH), bf16), vmem((128, OUT), bf16), vmem((128, OUT), bf16),
            vmem((128, EXAMPLES), bf16), vmem((128, EXAMPLES), bf16),
            vmem((256, 512), bf16), vmem((WIDTH, EXAMPLES), bf16), vmem((WIDTH, EXAMPLES), bf16),
            vmem((128, EXAMPLES), f32), vmem((128, 128), f32), vmem((128, 128), f32),
            vmem(units, bf16), vmem(units, bf16), vmem(units, f32), vmem(units, bf16), vmem(units, bf16),
            vmem(outputs, f32), vmem(outputs, f32), vmem(outputs, bf16), vmem(outputs, bf16),
            vmem((16, EXAMPLES), f32), vmem((16, EXAMPLES), f32),
            vmem((TASKS, OUT, EXAMPLES), f32), vmem((TASKS, OUT, EXAMPLES), f32), vmem((TASKS, EXAMPLES), f32),
            vmem((128, EXAMPLES), f32), vmem((128, EXAMPLES), f32), vmem((16, EXAMPLES), f32),
            vmem((16, EXAMPLES), bf16), vmem((16, EXAMPLES), bf16),
            vmem((WIDTH, EXAMPLES), f32), vmem((256, 128), f32),
            vmem((IN_ROWS, 128), f32), vmem((REST_ROWS, 128), f32), vmem((IN_ROWS // 2, 128), f32),
            vmem((16 * REST_PIECE, 128), f32), vmem((IN_ROWS // 2, 128), f32), vmem((16 * REST_PIECE, 128), f32),
            vmem((128, 128), f32), vmem((128, 128), f32), vmem((16, 128), f32), vmem((8, 128), f32),
            vmem((128, 128), f32), vmem((16, 128), f32), vmem((ROWS, ROWS), bf16),
            vmem((128, TABLES * EXAMPLES), bf16),
            dma((11,)), dma, dma((3,)), dma, dma((3,)), dma, dma((3,)), dma, dma((3,)), dma, dma, dma, dma,
            dma, dma, dma, dma, dma, dma, dma, dma, dma((2,)), dma((2,)),
            dma, dma((4,)), dma, dma((4,)), dma, dma((4,)), dma, dma,
        ],
        compiler_params=pltpu.CompilerParams(vmem_limit_bytes=LIMIT, collective_id=0, has_side_effects=True),
        name="model",
    )(*arrays)
    results = [pltpu.with_memory_space_constraint(result, pltpu.VMEM) for result in results]
    pred, dense_grad, table_grad, in_total, rest_total, weight_grad, head_grad = results
    table_grad, in_grad, out_grad, tower_grad, gate_grad, weight_grad, head_grad, pred, dense_grad = pl.pallas_call(
        write_kernel,
        out_shape=[
            shape(EMBED, ROWS), shape(512, WIDTH), shape(512, OUT), shape(TASKS * TOWER, OUT),
            shape(TASKS * EXPERTS, WIDTH), shape(DENSE, PROJ), shape(TASKS, TOWER), shape(TASKS, 128),
            shape(DENSE, EXAMPLES),
        ],
        in_specs=[anywhere] * 7,
        out_specs=[anywhere] * 9,
        scratch_shapes=[dma((23,))],
        compiler_params=pltpu.CompilerParams(vmem_limit_bytes=LIMIT),
        name="write",
    )(table_grad, in_total, rest_total, weight_grad, head_grad, pred, dense_grad)
    return (
        pred.T,
        dense_grad.T,
        table_grad.reshape(TABLES, ENTRY, ROWS).transpose(0, 2, 1),
        weight_grad,
        in_grad.reshape(EXPERTS, UNITS, WIDTH).transpose(2, 0, 1),
        out_grad.reshape(EXPERTS, UNITS, OUT),
        gate_grad.reshape(TASKS, EXPERTS, WIDTH).transpose(0, 2, 1),
        tower_grad.reshape(TASKS, TOWER, OUT).transpose(0, 2, 1),
        head_grad,
    )


def solution(mesh):
    placed = (
        P(None, ("batch", "hidden"), None),
        P("batch", None),
        P(),
        P(None, None, "hidden"),
        P(None, "hidden", None),
        P(),
        P(),
        P(),
        P("batch", None),
        P("batch", None, None),
        P(("batch", "hidden"), None),
    )
    return jax.shard_map(
        on_device,
        mesh=mesh,
        in_specs=placed,
        out_specs=(
            P(("batch", "hidden"), None),
            P("batch", None),
            P(None, ("batch", "hidden"), None),
            P(),
            P(None, None, "hidden"),
            P(None, "hidden", None),
            P(),
            P(),
            P(),
        ),
        check_vma=False,
    )
```

```python
import jax
import jax.numpy as jnp
from jax import lax
from jax.experimental import pallas as pl
from jax.experimental.pallas import tpu as pltpu
from jax.sharding import PartitionSpec as P

f32 = jnp.float32
bf16 = jnp.bfloat16
MESH = pl.DeviceIdType.MESH
VMEM = pl.BlockSpec(memory_space=pltpu.VMEM)
LIMIT = 56 * 2**20

TABLES, ROWS, ENTRY = 26, 1024, 16
BATCH, HIDDEN = 32, 4
DEVICES = BATCH * HIDDEN
EXPERTS, UNITS, OUT, WIDTH = 8, 64, 128, 512
TASKS, TOWER, DENSE, PROJ = 2, 64, 13, 96
EXAMPLES = 512
EMBED = TABLES * ENTRY

IN_PARTS = ((0, 3), (3, 6), (6, 8))
IN_ROWS = 2048
OUT_AT, GATE_AT, TOWER_AT, HEAD_AT = 0, 512, 576, 704
REST_ROWS, REST_PIECE = 768, 24


def split(value):
    high = value.astype(bf16)
    return high, (value - high.astype(f32)).astype(bf16)


def dot_nn(a, b):
    return lax.dot_general(a, b, (((1,), (0,)), ((), ())), preferred_element_type=f32)


def dot_nt(a, b):
    return lax.dot_general(a, b, (((1,), (1,)), ((), ())), preferred_element_type=f32)


def dot_tn(a, b):
    return lax.dot_general(a, b, (((0,), (0,)), ((), ())), preferred_element_type=f32)


def dot3_tn(a, b):
    (ah, al), (bh, bl) = a, b
    return dot_tn(ah, bh) + dot_tn(al, bh) + dot_tn(ah, bl)


def dot3_nn(a, b):
    (ah, al), (bh, bl) = a, b
    return dot_nn(jnp.concatenate([ah, al, ah], 1), jnp.concatenate([bh, bh, bl], 0))


def dot3_nt(a, b):
    (ah, al), (bh, bl) = a, b
    count = ah.shape[0]
    both = dot_nt(jnp.concatenate([ah, al], 0), bh)
    return both[0:count, :] + both[count : 2 * count, :] + dot_nt(ah, bl)


def sigmoid(value):
    return 0.5 * jnp.tanh(0.5 * value) + 0.5


def silu_both(value):
    sigma = sigmoid(value)
    result = value * sigma
    return result, sigma + result * (1.0 - sigma)


def iota(shape, axis):
    return lax.broadcasted_iota(jnp.int32, shape, axis)


def hops(offset):
    return min(offset, 4 - offset)


PLANE = sorted(
    ((dz, dx, dc) for dz in range(4) for dx in range(4) for dc in range(2) if dz or dx or dc),
    key=lambda d: -(2 * hops(d[0]) + 2 * hops(d[1]) + d[2]),
)
EVERYWHERE = sorted(
    ((dz, dx, dc, dy) for dz in range(4) for dx in range(4) for dc in range(2) for dy in range(4) if dz or dx or dc or dy),
    key=lambda d: -(2 * hops(d[0]) + 2 * hops(d[1]) + d[2] + 2 * hops(d[3])),
)
CHIPS = [(dz, dx) for dz, dx, dc in PLANE if not dc and (dz or dx)]


def target(b, h):
    return {"batch": b, "hidden": h}


def remote(src, dst, send, recv, b, h):
    return pltpu.make_async_remote_copy(src, dst, send, recv, device_id=target(b, h), device_id_type=MESH)


def bulk_wait(ref, sem):
    pltpu.make_async_copy(ref, ref, sem).wait()


def ids_by_query(received):
    turned = jnp.concatenate([received] * 4, 0).T
    lane = iota((8, 128), 1) // 32
    out = jnp.zeros((8, 128), jnp.int32)
    for q in range(4):
        out = jnp.where(lane == q, turned[q * 8 : q * 8 + 8, :], out)
    return out


def hot_of(code, count):
    rows = iota((count, code.shape[1]), 0).astype(jnp.int16)
    return jnp.where(rows == code.astype(jnp.int16), bf16(1.0), bf16(0.0))


def model_kernel(
    req_in, tab_in, win, wout, cot_in, slots_in, dense_in, dense_weight_in, gate_weight_in, tower_weight_in, head_in,
    pred_out, dense_grad_out, table_out, in_total, rest_total, weight_grad_out, head_grad_out,
    req, tab, cot, slots, dense, dense_weight, gate_weight, tower_weight, head,
    id_turned, id_send, id_recv, ids, row_send, rows, tab_split, win_all, wout_all, cot_all,
    wh, wl, oh, ol, gate_h, gate_l, tower_h, tower_l, dense_h, dense_l, lists, feat_h, feat_l,
    dense_pad, weight_pad, head_pad,
    inner_h, inner_l, slope, ig_h, ig_l, eo, eslope, ep_h, ep_l, gates, gate_slope, mixed, mixed_grad, pred,
    towers, pre_grads, scores, lgh, lgl, fg, slot_sum,
    in_sums, rest_sums, in_swap, rest_swap, in_pieces, rest_pieces,
    message, got, weight_part, weight_swap, weight_got, weight_total, hot_rows, hot_slots,
    local_sem, y_ssem, y_rsem, p_ssem, p_rsem, c_ssem, c_rsem, wo_ssem, wo_rsem, woc_ssem, woc_rsem, cot_ssem, cot_rsem,
    id_ssem, id_rsem, row_ssem, row_rsem, slot_ssem, slot_rsem, weight_ssem, weight_rsem, weight_send, weight_recv,
    swap_ssem, swap_rsem, piece_ssem, piece_rsem, full_ssem, full_rsem, last_ssem, last_rsem,
):
    b, h = lax.axis_index("batch"), lax.axis_index("hidden")
    core, x, z, chip = lax.rem(b, 2), lax.rem(b // 2, 4), b // 8, b // 2
    me = b * HIDDEN + h
    sibling = b + 1 - 2 * core
    zs = [lax.rem(z + d, 4) * 8 for d in range(4)]
    xs = [lax.rem(x + d, 4) * 2 for d in range(4)]
    cores = [core, 1 - core]
    hs = [lax.rem(h + d, HIDDEN) for d in range(HIDDEN)]
    chips = [(zs[dz] + xs[dx]) // 2 for dz, dx in CHIPS]
    plane = [zs[dz] + xs[dx] + cores[dc] for dz, dx, dc in PLANE]
    order = (1, 3, 2)
    block = pl.when(core >= 0)

    def bring(source, home, i):
        copy = pltpu.make_async_copy(source, home, local_sem.at[i])
        copy.start()
        return copy

    def units_of(s, e):
        return pl.ds(pl.multiple_of(s * 512 + e * UNITS, UNITS), UNITS)

    def block_of(s):
        return pl.ds(pl.multiple_of(s * 512, 512), 512)

    req_copy = bring(req_in, req, 0)
    barrier = pltpu.get_barrier_semaphore()
    for other in plane:
        pl.semaphore_signal(barrier, inc=1, device_id=target(other, h), device_id_type=MESH)
    for i in (2, 1, 3):
        pl.semaphore_signal(barrier, inc=1, device_id=target(b, hs[i]), device_id_type=MESH)
    tab_copy = bring(tab_in, tab, 1)
    win_copy = bring(win, win_all.at[h], 2)
    wout_copy = bring(wout, wout_all.at[h], 3)
    small = ((cot_in, cot), (slots_in, slots), (dense_in, dense), (dense_weight_in, dense_weight),
             (gate_weight_in, gate_weight), (tower_weight_in, tower_weight), (head_in, head))
    small_copies = [bring(source, home, 4 + i) for i, (source, home) in enumerate(small)]
    req_copy.wait()
    id_turned[...] = jnp.concatenate([req[...]] * 4, 0).T
    id_send[...] = id_turned[pl.ds(h, BATCH, stride=HIDDEN), :]
    pl.semaphore_wait(barrier, BATCH - 1 + HIDDEN - 1)

    for other in plane:
        remote(id_send.at[pl.ds(other, 1)], id_recv.at[pl.ds(b, 1)], id_ssem, id_rsem, other, h).start()
    spots = (
        pl.ds(pl.multiple_of(core * 128 + x * 32, 32), 32),
        pl.ds(pl.multiple_of(256 + core * 128 + z * 32, 32), 32),
    )
    spans = (pl.ds(pl.multiple_of(core * 128, 128), 128), pl.ds(pl.multiple_of(256 + core * 128, 128), 128))
    half = pl.ds(pl.multiple_of(core * 256, 256), 256)
    source_of = [lax.rem(h - i + HIDDEN, HIDDEN) for i in range(HIDDEN)]
    for i in order:
        for spot in spots:
            remote(win.at[spot], win_all.at[h, spot], y_ssem, y_rsem.at[i - 1], b, hs[i]).start()

    def spread(i):
        source = source_of[i]
        bulk_wait(win_all.at[source, pl.ds(0, 64)], y_rsem.at[i - 1])
        for j in (2, 1, 3):
            for spot, other in ((spots[0], z * 8 + xs[j] + core), (spots[1], zs[j] + x * 2 + core)):
                piece = win_all.at[source, spot]
                remote(piece, piece, p_ssem, p_rsem.at[i - 1], other, h).start()

    def to_core(i):
        source = source_of[i]
        bulk_wait(win_all.at[source, pl.ds(0, 192)], p_rsem.at[i - 1])
        for span in spans:
            piece = win_all.at[source, span]
            remote(piece, piece, c_ssem, c_rsem.at[i - 1], sibling, h).start()

    def out_to_core(i):
        bulk_wait(wout_all.at[source_of[i], half], wo_rsem.at[i - 1])
        piece = wout_all.at[source_of[i], half]
        remote(piece, piece, woc_ssem, woc_rsem, sibling, h).start()

    tab_copy.wait()

    @block
    def _():
        high, low = split(tab[...])
        tab_split[0:EMBED, :] = high
        tab_split[EMBED : 2 * EMBED, :] = low

    id_recv[pl.ds(b, 1), :] = id_send[pl.ds(b, 1), :]
    bulk_wait(id_recv.at[pl.ds(0, BATCH - 1)], id_rsem)

    @block
    def _():
        found = ids_by_query(id_recv[...])
        ids[...] = found
        table, row = found // ROWS, lax.rem(found, ROWS)
        entries = []
        for pair in range(4):
            hot = jnp.concatenate([hot_of(row[j : j + 1, :], ROWS) for j in (2 * pair, 2 * pair + 1)], 1)
            value = dot_nn(tab_split[...], hot)
            for part in range(2):
                wanted = table[2 * pair + part : 2 * pair + part + 1, :]
                entry = jnp.zeros((ENTRY, 128), f32)
                for t in range(TABLES):
                    high = value[t * ENTRY : (t + 1) * ENTRY, part * 128 : part * 128 + 128]
                    low = value[EMBED + t * ENTRY : EMBED + (t + 1) * ENTRY, part * 128 : part * 128 + 128]
                    entry = jnp.where(wanted == t, high + low, entry)
                entries.append(entry)
        turned = jnp.concatenate(entries, 0).T
        for q in range(4):
            row_send[pl.ds(q, BATCH, stride=4), :] = turned[q * 32 : q * 32 + 32, :]

    mine = pl.ds(me * 4, 4)
    for dz, dx, dc, dy in EVERYWHERE:
        group = zs[dz] + xs[dx] + cores[dc]
        remote(row_send.at[pl.ds(group * 4, 4)], rows.at[mine], row_ssem, row_rsem, group, hs[dy]).start()
    rows[mine, :] = row_send[pl.ds(b * 4, 4), :]
    for i in order:
        spread(i)
    for copy in small_copies:
        copy.wait()
    wout_copy.wait()
    for i in order:
        remote(cot, cot_all.at[h], cot_ssem, cot_rsem, b, hs[i]).start()
        piece = wout_all.at[h, half]
        remote(piece, piece, wo_ssem, wo_rsem.at[i - 1], b, hs[i]).start()
    win_copy.wait()

    @block
    def _():
        cot_all[pl.ds(h, 1)] = cot[...].reshape(1, TASKS, 128)
        dense_pad[...] = jnp.zeros_like(dense_pad)
        dense_pad[0:DENSE, :] = dense[...]
        weight_pad[...] = jnp.zeros_like(weight_pad)
        weight_pad[0:DENSE, 0:PROJ] = dense_weight[...]
        head_pad[...] = jnp.zeros_like(head_pad)
        head_pad[0:TASKS, 0:TOWER] = head[...]
        dense_h[...], dense_l[...] = split(dense_pad[...])
        projected = dot3_nn(split(weight_pad[...].T), (dense_h[...], dense_l[...]))
        feat_h[EMBED:WIDTH, :], feat_l[EMBED:WIDTH, :] = split(projected[0:PROJ, :])
        tower_h[...], tower_l[...] = split(tower_weight[...])
        gate_h[...], gate_l[...] = split(gate_weight[...])
        wh[block_of(h), :], wl[block_of(h), :] = split(win_all[h])

    @block
    def _():
        row = lax.rem(ids[...], ROWS)
        for j in range(8):
            hot_rows[:, j * 128 : (j + 1) * 128] = hot_of(row[j : j + 1, :], ROWS)

    @block
    def _():
        for t in range(TABLES):
            slot = slots[t : t + 1, :]
            owner = slot // 32
            code = jnp.where(lax.rem(owner, HIDDEN) == h, lax.rem(slot, 32) // 8 * 32 + owner // HIDDEN, -1)
            hot_slots[:, t * EXAMPLES : (t + 1) * EXAMPLES] = hot_of(code, 128)

    bulk_wait(rows.at[pl.ds(0, (DEVICES - 1) * 4)], row_rsem)

    def gather(first, last):
        for t in range(first, last):
            slot = slots[t : t + 1, :]
            low = lax.rem(slot, 8)
            value = dot_nn(lists[...], hot_of(lax.rem(slot, 32) // 8 * 128 + slot // 32, 512))
            high_sum = jnp.zeros((ENTRY, EXAMPLES), f32)
            low_sum = jnp.zeros((ENTRY, EXAMPLES), f32)
            for j in range(8):
                high_sum = jnp.where(low == j, value[j * 16 : j * 16 + 16, :], high_sum)
                low_sum = jnp.where(low == j, value[128 + j * 16 : 128 + j * 16 + 16, :], low_sum)
            feat_h[t * ENTRY : (t + 1) * ENTRY, :] = high_sum.astype(bf16)
            feat_l[t * ENTRY : (t + 1) * ENTRY, :] = low_sum.astype(bf16)

    @block
    def _():
        for q in range(4):
            at = slice(q * 128, q * 128 + 128)
            lists[0:128, at], lists[128:256, at] = split(rows[pl.ds(q, DEVICES, stride=4), :].T)
        gather(0, 13)

    to_core(1)
    block(lambda: gather(13, TABLES))

    def first_layer(s):
        at = block_of(s)
        inner, slope[at, :] = silu_both(dot3_nn((wh[at, :], wl[at, :]), (feat_h[...], feat_l[...])))
        inner_h[at, :], inner_l[at, :] = split(inner)

    def next_layer(*which):
        for i in which:
            bulk_wait(win_all.at[source_of[i], pl.ds(0, 256)], c_rsem.at[i - 1])

        @block
        def _():
            for i in which:
                s = source_of[i]
                wh[block_of(s), :], wl[block_of(s), :] = split(win_all[s])
                first_layer(s)

    @block
    def _():
        first_layer(h)
        logits = dot3_nn((gate_h[...], gate_l[...]), (feat_h[...], feat_l[...]))
        for k in range(TASKS):
            part = logits[k * 8 : k * 8 + 8, :]
            raised = jnp.exp(part - jnp.max(part, axis=0, keepdims=True))
            gates[k * 8 : k * 8 + 8, :] = raised / jnp.sum(raised, axis=0, keepdims=True)

    to_core(3)
    next_layer(1)
    to_core(2)
    next_layer(3)
    for i in order:
        out_to_core(i)
    next_layer(2)
    bulk_wait(wout_all.at[pl.ds(0, 3), pl.ds(0, 256)], woc_rsem)
    bulk_wait(cot_all.at[pl.ds(0, 3)], cot_rsem)

    def of_expert(refs, e):
        return tuple(
            jnp.concatenate([ref[s * 512 + e * UNITS : s * 512 + (e + 1) * UNITS, :] for s in range(HIDDEN)], 0)
            for ref in refs
        )

    def second_layer():
        mixed[...] = jnp.zeros_like(mixed)
        for s in range(HIDDEN):
            at = slice(s * 512, s * 512 + 512)
            oh[at, :], ol[at, :] = split(wout_all[s])
        for e in range(EXPERTS):
            outputs, eslope[e] = silu_both(dot3_tn(of_expert((oh, ol), e), of_expert((inner_h, inner_l), e)))
            eo[e] = outputs
            for k in range(TASKS):
                mixed[k] = mixed[k] + gates[k * 8 + e : k * 8 + e + 1, :] * outputs

    def tower_pass():
        head_turned = head_pad[...].T
        scores[...] = jnp.zeros_like(scores)
        for k in range(TASKS):
            at = slice(k * TOWER, (k + 1) * TOWER)
            value, tower_slope = silu_both(dot3_nn((tower_h[at, :], tower_l[at, :]), split(mixed[k])))
            column = jnp.broadcast_to(head_turned[0:TOWER, k : k + 1], (TOWER, EXAMPLES))
            predicted = sigmoid(jnp.sum(value * column, axis=0, keepdims=True))
            pred[k : k + 1, :] = predicted
            cotangent = jnp.concatenate([cot_all[i, k : k + 1, :] for i in range(HIDDEN)], 1)
            score = cotangent * predicted * (1.0 - predicted)
            scores[k : k + 1, :] = score
            towers[at, :] = value
            pre_grad = score * column * tower_slope
            pre_grads[at, :] = pre_grad
            mixed_grad[k] = dot3_tn((tower_h[at, :], tower_l[at, :]), split(pre_grad))

    @block
    def _():
        second_layer()
        tower_pass()

    def expert_grads(first, last):
        for e in range(first, last):
            outputs = eo[e]
            grad = jnp.zeros((OUT, EXAMPLES), f32)
            for k in range(TASKS):
                gate_slope[k * 8 + e : k * 8 + e + 1, :] = jnp.sum(mixed_grad[k] * outputs, axis=0, keepdims=True)
                grad = grad + gates[k * 8 + e : k * 8 + e + 1, :] * mixed_grad[k]
            out_split = split(grad * eslope[e])
            ep_h[e], ep_l[e] = out_split
            at = units_of(h, e)
            ig_h[at, :], ig_l[at, :] = split(dot3_nn((oh[at, :], ol[at, :]), out_split) * slope[at, :])

    def other_grads():
        for e in range(EXPERTS):
            places = [units_of(source_of[i], e) for i in order]
            side = tuple(jnp.concatenate([ref[at, :] for at in places], 0) for ref in (oh, ol))
            inner_grad = dot3_nn(side, (ep_h[e], ep_l[e]))
            for n, at in enumerate(places):
                ig_h[at, :], ig_l[at, :] = split(inner_grad[n * UNITS : (n + 1) * UNITS, :] * slope[at, :])

    def first_layer_grad(first, last):
        count = (last - first) * UNITS
        at = pl.ds(pl.multiple_of(h * 512 + first * UNITS, UNITS), count)
        in_grad = dot3_nt((ig_h[at, :], ig_l[at, :]), (feat_h[...], feat_l[...]))
        for q in range(4):
            start = 4 * first * UNITS + q * count
            in_sums[start : start + count, :] = in_grad[:, q * 128 : (q + 1) * 128]

    parts = []
    for first, last in IN_PARTS:
        start, size = 4 * first * UNITS, 4 * (last - first) * UNITS
        whole, halves = pl.ds(start, size), pl.ds(start // 2, size // 2)
        parts.append((in_sums.at[whole], in_swap.at[halves], in_pieces.at[halves], in_total.at[whole], size // 32))
    parts.append((rest_sums, rest_swap, rest_pieces, rest_total, REST_PIECE))

    def swap(n):
        sums, swapped, _, _, piece = parts[n]
        half_rows = 16 * piece
        theirs = sums.at[pl.ds(pl.multiple_of((1 - core) * half_rows, 8), half_rows)]
        remote(theirs, swapped, swap_ssem, swap_rsem.at[n], sibling, h).start()

    def send_pieces(n):
        sums, swapped, pieces, _, piece = parts[n]
        half_rows = 16 * piece
        bulk_wait(swapped, swap_rsem.at[n])
        swapped[...] += sums[pl.ds(pl.multiple_of(core * half_rows, 8), half_rows), :]
        own = pl.ds(pl.multiple_of(chip * piece, 8), piece)
        for other in chips:
            remote(
                swapped.at[pl.ds(pl.multiple_of(other * piece, 8), piece)], pieces.at[own],
                piece_ssem, piece_rsem.at[n], other * 2 + core, h,
            ).start()
        pieces[own, :] = swapped[own, :]

    def send_sums(n):
        _, _, pieces, total, piece = parts[n]
        half_rows = 16 * piece
        bulk_wait(pieces.at[pl.ds(0, 15 * piece)], piece_rsem.at[n])
        value = pieces[0:piece, :]
        for i in range(1, 16):
            value = value + pieces[i * piece : (i + 1) * piece, :]
        at = pl.ds(pl.multiple_of(core * half_rows + chip * piece, 8), piece)
        total[at, :] = value
        for other in chips:
            remote(total.at[at], total.at[at], full_ssem, full_rsem.at[n], other * 2 + core, h).start()

    def hand_on(n):
        _, _, _, total, piece = parts[n]
        bulk_wait(total.at[pl.ds(0, 15 * piece)], full_rsem.at[n])
        ours = total.at[pl.ds(pl.multiple_of(core * 16 * piece, 8), 16 * piece)]
        remote(ours, ours, last_ssem, last_rsem, sibling, h).start()

    for n, (first, last) in enumerate(IN_PARTS):

        @block
        def _():
            expert_grads(first, last)
            first_layer_grad(first, last)

        swap(n)
        if n:
            send_pieces(n - 1)

    @block
    def _():
        for k in range(TASKS):
            at = slice(k * TOWER, (k + 1) * TOWER)
            rest_sums[TOWER_AT + k * TOWER : TOWER_AT + (k + 1) * TOWER, :] = dot3_nt(
                split(pre_grads[at, :]), split(mixed[k])
            )
        head_rows = dot3_nt(split(scores[...]), split(towers[...]))
        rest_sums[HEAD_AT:REST_ROWS, :] = jnp.zeros((REST_ROWS - HEAD_AT, 128), f32)
        rest_sums[HEAD_AT : HEAD_AT + 1, :] = jnp.where(
            iota((1, 128), 1) < TOWER, head_rows[0:1, :], head_rows[1:2, :]
        )
        logit_grads = []
        for k in range(TASKS):
            gate, slopes = gates[k * 8 : k * 8 + 8, :], gate_slope[k * 8 : k * 8 + 8, :]
            logit_grads.append(gate * (slopes - jnp.sum(gate * slopes, axis=0, keepdims=True)))
        lgh[...], lgl[...] = split(jnp.concatenate(logit_grads, 0))
        gate_grad = dot3_nt((lgh[...], lgl[...]), (feat_h[...], feat_l[...]))
        for q in range(4):
            rest_sums[GATE_AT + q * 16 : GATE_AT + q * 16 + 16, :] = gate_grad[:, q * 128 : (q + 1) * 128]

        for e in range(EXPERTS):
            at = units_of(h, e)
            rest_sums[OUT_AT + e * UNITS : OUT_AT + (e + 1) * UNITS, :] = dot3_nt(
                (inner_h[at, :], inner_l[at, :]), (ep_h[e], ep_l[e])
            )

    swap(3)
    send_pieces(2)

    def feature_grad(low, high):
        at = slice(low, high)
        fg[at, :] = dot3_tn((wh[:, at], wl[:, at]), (ig_h[...], ig_l[...])) + dot3_tn(
            (gate_h[:, at], gate_l[:, at]), (lgh[...], lgl[...])
        )

    def scatter(first, last):
        spreads = []
        for t in range(first, last):
            low = lax.rem(slots[t : t + 1, :], 8)
            high, rest = split(fg[t * ENTRY : (t + 1) * ENTRY, :])
            where = jnp.broadcast_to(low, (ENTRY, EXAMPLES)).astype(jnp.int16)
            nothing = jnp.zeros((ENTRY, EXAMPLES), bf16)
            spreads.append(
                jnp.concatenate([jnp.where(where == j, value, nothing) for value in (high, rest) for j in range(8)], 0)
            )
        return dot_nt(jnp.concatenate(spreads, 1), hot_slots[:, first * EXAMPLES : last * EXAMPLES])

    block(other_grads)
    send_pieces(3)
    block(lambda: feature_grad(256, WIDTH))
    send_sums(0)

    @block
    def _():
        projected_grad = split(jnp.concatenate([fg[EMBED:WIDTH, :], jnp.zeros((32, EXAMPLES), f32)], 0))
        weight_part[...] = dot3_nt((dense_h[...], dense_l[...]), projected_grad)[0:16, :]
        dense_grad_out[...] = dot3_nn(split(weight_pad[...]), projected_grad)[0:DENSE, :]

    weight_copies = [
        remote(
            weight_part.at[pl.ds(pl.multiple_of((1 - core) * 8, 8), 8)], weight_swap,
            weight_send.at[0], weight_recv.at[0], sibling, h,
        )
    ]
    weight_copies[0].start()

    @block
    def _():
        slot_sum[...] = scatter(16, TABLES)

    weight_copies[0].wait_recv()
    weight_swap[...] += weight_part[pl.ds(pl.multiple_of(core * 8, 8), 8), :]
    weight_at = pl.ds(pl.multiple_of(chip * 8, 8), 8)
    for other in chips:
        remote(weight_swap, weight_got.at[weight_at], weight_ssem, weight_rsem, other * 2 + core, h).start()
    weight_got[weight_at, :] = weight_swap[...]
    send_sums(1)

    @block
    def _():
        feature_grad(0, 256)
        slot_turned = slot_sum[...] + scatter(0, 16)
        slot_turned = (slot_turned[0:128, :] + slot_turned[128:256, :]).T
        for q in range(4):
            message[pl.ds(q, BATCH, stride=4), :] = slot_turned[q * 32 : q * 32 + 32, :]

    for other in plane:
        remote(message.at[pl.ds(other * 4, 4)], got.at[pl.ds(b * 4, 4)], slot_ssem, slot_rsem, other, h).start()
    got[pl.ds(b * 4, 4), :] = message[pl.ds(b * 4, 4), :]
    send_sums(2)
    send_sums(3)
    bulk_wait(weight_got.at[pl.ds(0, 15 * 8)], weight_rsem)
    value = weight_got[0:8, :]
    for i in range(1, 16):
        value = value + weight_got[i * 8 : i * 8 + 8, :]
    weight_at = pl.ds(pl.multiple_of(core * 8, 8), 8)
    weight_total[weight_at, :] = value
    weight_copies.append(
        remote(
            weight_total.at[weight_at], weight_total.at[weight_at], weight_send.at[1], weight_recv.at[1], sibling, h
        )
    )
    weight_copies[1].start()
    for k in range(TASKS):
        pred_out[k : k + 1, :] = pred[k : k + 1, pl.ds(pl.multiple_of(h * 128, 128), 128)]

    hand_on(0)
    hand_on(1)
    bulk_wait(got.at[pl.ds(0, (BATCH - 1) * 4)], slot_rsem)

    @block
    def _():
        high, rest = split(jnp.concatenate([got[pl.ds(q, BATCH, stride=4), :] for q in range(4)], 0).T)
        table = ids[...] // ROWS
        spreads = []
        for j in range(8):
            where = jnp.broadcast_to(table[j : j + 1, :], (ENTRY, 128)).astype(jnp.int16)
            nothing = jnp.zeros((ENTRY, 128), bf16)
            chosen = [
                jnp.where(where == t, value[j * 16 : j * 16 + 16, :], nothing)
                for value in (high, rest)
                for t in range(TABLES)
            ]
            spreads.append(jnp.concatenate(chosen, 0))
        both = dot_nt(jnp.concatenate(spreads, 1), hot_rows[...])
        table_out[...] = both[0:EMBED, :] + both[EMBED : 2 * EMBED, :]

    weight_copies[1].wait_recv()
    weight_grad_out[...] = weight_total[0:DENSE, 0:PROJ]
    hand_on(2)
    hand_on(3)
    whole = in_total.at[pl.ds(0, IN_ROWS // 2 + 16 * REST_PIECE)]
    bulk_wait(whole, last_rsem)
    head_grad_out[0:1, :] = rest_total[HEAD_AT : HEAD_AT + 1, 0:TOWER]
    head_grad_out[1:2, :] = rest_total[HEAD_AT : HEAD_AT + 1, TOWER : 2 * TOWER]
    most = in_total.at[pl.ds(0, 15 * (IN_ROWS // 32 + REST_PIECE))]
    bulk_wait(most, full_ssem)
    bulk_wait(most, piece_ssem)
    bulk_wait(whole, swap_ssem)
    bulk_wait(whole, last_ssem)
    for copy in weight_copies:
        copy.wait_send()
    bulk_wait(weight_got.at[pl.ds(0, 15 * 8)], weight_ssem)
    bulk_wait(message.at[pl.ds(0, (BATCH - 1) * 4)], slot_ssem)
    bulk_wait(rows.at[pl.ds(0, (DEVICES - 1) * 4)], row_ssem)
    bulk_wait(id_send.at[pl.ds(0, BATCH - 1)], id_ssem)
    bulk_wait(win_all.at[0, pl.ds(0, 192)], y_ssem)
    bulk_wait(win_all.at[pl.ds(0, 3), pl.ds(0, 192)], p_ssem)
    bulk_wait(win_all.at[pl.ds(0, 3), pl.ds(0, 256)], c_ssem)
    bulk_wait(wout_all.at[pl.ds(0, 3), pl.ds(0, 256)], wo_ssem)
    bulk_wait(wout_all.at[pl.ds(0, 3), pl.ds(0, 256)], woc_ssem)
    bulk_wait(cot_all.at[pl.ds(0, 3)], cot_ssem)


def write_kernel(
    table, in_total, rest_total, weight_grad, head_grad, pred, dense_grad,
    table_out, in_out, out_out, tower_out, gate_out, weight_out, head_out, pred_out, dense_out, sems,
):
    copies = [(table, table_out), (rest_total.at[OUT_AT:GATE_AT], out_out), (rest_total.at[TOWER_AT:HEAD_AT], tower_out)]
    copies += [
        (
            in_total.at[pl.ds((4 * first + q * (last - first)) * UNITS, (last - first) * UNITS)],
            in_out.at[first * UNITS : last * UNITS, q * 128 : (q + 1) * 128],
        )
        for first, last in IN_PARTS
        for q in range(4)
    ]
    copies += [
        (rest_total.at[GATE_AT + q * 16 : GATE_AT + q * 16 + 16], gate_out.at[:, q * 128 : q * 128 + 128])
        for q in range(4)
    ]
    copies += [(weight_grad, weight_out), (head_grad, head_out), (pred, pred_out), (dense_grad, dense_out)]
    copies = [pltpu.make_async_copy(source, home, sems.at[i]) for i, (source, home) in enumerate(copies)]
    for copy in copies:
        copy.start()
    for copy in copies:
        copy.wait()


def on_device(
    tables, dense, dense_weight, expert_in, expert_out, gate_weight, tower_weight, head_weight, slots, requests, pred_cot
):
    i32 = jnp.int32
    dma = pltpu.SemaphoreType.DMA
    vmem = pltpu.VMEM
    anywhere = pl.BlockSpec(memory_space=pl.ANY)
    arrays = (
        requests[0].T,
        tables.transpose(0, 2, 1).reshape(EMBED, ROWS),
        expert_in.transpose(1, 2, 0).reshape(EXPERTS * UNITS, WIDTH),
        expert_out.reshape(EXPERTS * UNITS, OUT),
        pred_cot.T,
        slots.T,
        dense.T,
        dense_weight,
        gate_weight.transpose(0, 2, 1).reshape(TASKS * EXPERTS, WIDTH),
        tower_weight.transpose(0, 2, 1).reshape(TASKS * TOWER, OUT),
        head_weight,
    )
    shape = lambda *dims: jax.ShapeDtypeStruct(dims, f32)
    units = HIDDEN * 512, EXAMPLES
    outputs = EXPERTS, OUT, EXAMPLES
    results = pl.pallas_call(
        model_kernel,
        out_shape=[
            vmem((TASKS, 128), f32), vmem((DENSE, EXAMPLES), f32), vmem((EMBED, ROWS), f32), vmem((IN_ROWS, 128), f32),
            vmem((REST_ROWS, 128), f32), vmem((DENSE, PROJ), f32), vmem((TASKS, TOWER), f32),
        ],
        in_specs=[anywhere] * 11,
        out_specs=[VMEM] * 7,
        scratch_shapes=[
            vmem((32, 128), i32), vmem((EMBED, ROWS), f32), vmem((TASKS, 128), f32), vmem((TABLES, EXAMPLES), i32),
            vmem((DENSE, EXAMPLES), f32), vmem((DENSE, PROJ), f32), vmem((16, WIDTH), f32), vmem((128, OUT), f32),
            vmem((TASKS, TOWER), f32),
            vmem((128, 128), i32), vmem((32, 128), i32), vmem((32, 128), i32), vmem((8, 128), i32), vmem((128, 128), f32),
            vmem((512, 128), f32), vmem((2 * EMBED, ROWS), bf16),
            vmem((HIDDEN, 512, WIDTH), f32), vmem((HIDDEN, 512, OUT), f32), vmem((HIDDEN, TASKS, 128), f32),
            vmem((2048, WIDTH), bf16), vmem((2048, WIDTH), bf16), vmem((2048, OUT), bf16), vmem((2048, OUT), bf16),
            vmem((16, WIDTH), bf16), vmem((16, WIDTH), bf16), vmem((128, OUT), bf16), vmem((128, OUT), bf16),
            vmem((128, EXAMPLES), bf16), vmem((128, EXAMPLES), bf16),
            vmem((256, 512), bf16), vmem((WIDTH, EXAMPLES), bf16), vmem((WIDTH, EXAMPLES), bf16),
            vmem((128, EXAMPLES), f32), vmem((128, 128), f32), vmem((128, 128), f32),
            vmem(units, bf16), vmem(units, bf16), vmem(units, f32), vmem(units, bf16), vmem(units, bf16),
            vmem(outputs, f32), vmem(outputs, f32), vmem(outputs, bf16), vmem(outputs, bf16),
            vmem((16, EXAMPLES), f32), vmem((16, EXAMPLES), f32),
            vmem((TASKS, OUT, EXAMPLES), f32), vmem((TASKS, OUT, EXAMPLES), f32), vmem((TASKS, EXAMPLES), f32),
            vmem((128, EXAMPLES), f32), vmem((128, EXAMPLES), f32), vmem((16, EXAMPLES), f32),
            vmem((16, EXAMPLES), bf16), vmem((16, EXAMPLES), bf16),
            vmem((WIDTH, EXAMPLES), f32), vmem((256, 128), f32),
            vmem((IN_ROWS, 128), f32), vmem((REST_ROWS, 128), f32), vmem((IN_ROWS // 2, 128), f32),
            vmem((16 * REST_PIECE, 128), f32), vmem((IN_ROWS // 2, 128), f32), vmem((16 * REST_PIECE, 128), f32),
            vmem((128, 128), f32), vmem((128, 128), f32), vmem((16, 128), f32), vmem((8, 128), f32),
            vmem((128, 128), f32), vmem((16, 128), f32), vmem((ROWS, ROWS), bf16),
            vmem((128, TABLES * EXAMPLES), bf16),
            dma((11,)), dma, dma((3,)), dma, dma((3,)), dma, dma((3,)), dma, dma((3,)), dma, dma, dma, dma,
            dma, dma, dma, dma, dma, dma, dma, dma, dma((2,)), dma((2,)),
            dma, dma((4,)), dma, dma((4,)), dma, dma((4,)), dma, dma,
        ],
        compiler_params=pltpu.CompilerParams(vmem_limit_bytes=LIMIT, collective_id=0, has_side_effects=True),
        name="model",
    )(*arrays)
    results = [pltpu.with_memory_space_constraint(result, pltpu.VMEM) for result in results]
    pred, dense_grad, table_grad, in_total, rest_total, weight_grad, head_grad = results
    table_grad, in_grad, out_grad, tower_grad, gate_grad, weight_grad, head_grad, pred, dense_grad = pl.pallas_call(
        write_kernel,
        out_shape=[
            shape(EMBED, ROWS), shape(512, WIDTH), shape(512, OUT), shape(TASKS * TOWER, OUT),
            shape(TASKS * EXPERTS, WIDTH), shape(DENSE, PROJ), shape(TASKS, TOWER), shape(TASKS, 128),
            shape(DENSE, EXAMPLES),
        ],
        in_specs=[anywhere] * 7,
        out_specs=[anywhere] * 9,
        scratch_shapes=[dma((23,))],
        compiler_params=pltpu.CompilerParams(vmem_limit_bytes=LIMIT),
        name="write",
    )(table_grad, in_total, rest_total, weight_grad, head_grad, pred, dense_grad)
    return (
        pred.T,
        dense_grad.T,
        table_grad.reshape(TABLES, ENTRY, ROWS).transpose(0, 2, 1),
        weight_grad,
        in_grad.reshape(EXPERTS, UNITS, WIDTH).transpose(2, 0, 1),
        out_grad.reshape(EXPERTS, UNITS, OUT),
        gate_grad.reshape(TASKS, EXPERTS, WIDTH).transpose(0, 2, 1),
        tower_grad.reshape(TASKS, TOWER, OUT).transpose(0, 2, 1),
        head_grad,
    )


def solution(mesh):
    placed = (
        P(None, ("batch", "hidden"), None),
        P("batch", None),
        P(),
        P(None, None, "hidden"),
        P(None, "hidden", None),
        P(),
        P(),
        P(),
        P("batch", None),
        P("batch", None, None),
        P(("batch", "hidden"), None),
    )
    return jax.shard_map(
        on_device,
        mesh=mesh,
        in_specs=placed,
        out_specs=(
            P(("batch", "hidden"), None),
            P("batch", None),
            P(None, ("batch", "hidden"), None),
            P(),
            P(None, None, "hidden"),
            P(None, "hidden", None),
            P(),
            P(),
            P(),
        ),
        check_vma=False,
    )
```

```python
import jax
import jax.numpy as jnp
from jax import lax
from jax.experimental import pallas as pl
from jax.experimental.pallas import tpu as pltpu
from jax.sharding import PartitionSpec as P

f32 = jnp.float32
bf16 = jnp.bfloat16
MESH = pl.DeviceIdType.MESH
VMEM = pl.BlockSpec(memory_space=pltpu.VMEM)
LIMIT = 56 * 2**20

TABLES, ROWS, ENTRY = 26, 1024, 16
BATCH, HIDDEN = 32, 4
DEVICES = BATCH * HIDDEN
EXPERTS, UNITS, OUT, WIDTH = 8, 64, 128, 512
TASKS, TOWER, DENSE, PROJ = 2, 64, 13, 96
EXAMPLES = 512
EMBED = TABLES * ENTRY

IN_PARTS = ((0, 3), (3, 6), (6, 8))
IN_ROWS = 2048
OUT_AT, GATE_AT, TOWER_AT, HEAD_AT = 0, 512, 576, 704
REST_ROWS, REST_PIECE = 768, 24


def split(value):
    high = value.astype(bf16)
    return high, (value - high.astype(f32)).astype(bf16)


def dot_nn(a, b):
    return lax.dot_general(a, b, (((1,), (0,)), ((), ())), preferred_element_type=f32)


def dot_nt(a, b):
    return lax.dot_general(a, b, (((1,), (1,)), ((), ())), preferred_element_type=f32)


def dot_tn(a, b):
    return lax.dot_general(a, b, (((0,), (0,)), ((), ())), preferred_element_type=f32)


def dot3_tn(a, b):
    (ah, al), (bh, bl) = a, b
    return dot_tn(ah, bh) + dot_tn(al, bh) + dot_tn(ah, bl)


def dot3_nn(a, b):
    (ah, al), (bh, bl) = a, b
    return dot_nn(jnp.concatenate([ah, al, ah], 1), jnp.concatenate([bh, bh, bl], 0))


def dot3_nt(a, b):
    (ah, al), (bh, bl) = a, b
    count = ah.shape[0]
    both = dot_nt(jnp.concatenate([ah, al], 0), bh)
    return both[0:count, :] + both[count : 2 * count, :] + dot_nt(ah, bl)


def sigmoid(value):
    return 0.5 * jnp.tanh(0.5 * value) + 0.5


def silu_both(value):
    sigma = sigmoid(value)
    result = value * sigma
    return result, sigma + result * (1.0 - sigma)


def iota(shape, axis):
    return lax.broadcasted_iota(jnp.int32, shape, axis)


def hops(offset):
    return min(offset, 4 - offset)


PLANE = sorted(
    ((dz, dx, dc) for dz in range(4) for dx in range(4) for dc in range(2) if dz or dx or dc),
    key=lambda d: -(2 * hops(d[0]) + 2 * hops(d[1]) + d[2]),
)
EVERYWHERE = sorted(
    ((dz, dx, dc, dy) for dz in range(4) for dx in range(4) for dc in range(2) for dy in range(4) if dz or dx or dc or dy),
    key=lambda d: -(2 * hops(d[0]) + 2 * hops(d[1]) + d[2] + 2 * hops(d[3])),
)
CHIPS = [(dz, dx) for dz, dx, dc in PLANE if not dc and (dz or dx)]


def target(b, h):
    return {"batch": b, "hidden": h}


def remote(src, dst, send, recv, b, h):
    return pltpu.make_async_remote_copy(src, dst, send, recv, device_id=target(b, h), device_id_type=MESH)


def bulk_wait(ref, sem):
    pltpu.make_async_copy(ref, ref, sem).wait()


def ids_by_query(received):
    turned = jnp.concatenate([received] * 4, 0).T
    lane = iota((8, 128), 1) // 32
    out = jnp.zeros((8, 128), jnp.int32)
    for q in range(4):
        out = jnp.where(lane == q, turned[q * 8 : q * 8 + 8, :], out)
    return out


def hot_of(code, count):
    rows = iota((count, code.shape[1]), 0).astype(jnp.int16)
    return jnp.where(rows == code.astype(jnp.int16), bf16(1.0), bf16(0.0))


def model_kernel(
    req_in, tab_in, win, wout, cot_in, slots_in, dense_in, dense_weight_in, gate_weight_in, tower_weight_in, head_in,
    pred_out, dense_grad_out, table_out, in_total, rest_total, weight_grad_out, head_grad_out,
    req, tab, cot, slots, dense, dense_weight, gate_weight, tower_weight, head,
    id_turned, id_send, id_recv, ids, row_send, rows, tab_split, win_all, wout_all, cot_all,
    wh, wl, oh, ol, gate_h, gate_l, tower_h, tower_l, dense_h, dense_l, lists, feat_h, feat_l,
    dense_pad, weight_pad, head_pad,
    inner_h, inner_l, slope, ig_h, ig_l, eo, eslope, ep_h, ep_l, gates, gate_slope, mixed, mixed_grad, pred,
    towers, pre_grads, scores, lgh, lgl, fg, slot_sum,
    in_sums, rest_sums, in_swap, rest_swap, in_pieces, rest_pieces,
    message, got, weight_part, weight_swap, weight_got, weight_total, hot_rows, hot_slots,
    local_sem, y_rsem, p_rsem, c_rsem, wo_rsem, woc_rsem, cot_ssem, cot_rsem,
    id_rsem, row_rsem, slot_rsem, weight_rsem, weight_send, weight_recv, swap_rsem, piece_rsem, full_rsem, last_rsem,
    small_ssem, sum_ssem, side_ssem, piece_ssem, full_ssem,
):
    b, h = lax.axis_index("batch"), lax.axis_index("hidden")
    core, x, z, chip = lax.rem(b, 2), lax.rem(b // 2, 4), b // 8, b // 2
    me = b * HIDDEN + h
    sibling = b + 1 - 2 * core
    zs = [lax.rem(z + d, 4) * 8 for d in range(4)]
    xs = [lax.rem(x + d, 4) * 2 for d in range(4)]
    cores = [core, 1 - core]
    hs = [lax.rem(h + d, HIDDEN) for d in range(HIDDEN)]
    chips = [(zs[dz] + xs[dx]) // 2 for dz, dx in CHIPS]
    plane = [zs[dz] + xs[dx] + cores[dc] for dz, dx, dc in PLANE]
    order = (1, 3, 2)
    block = pl.when(core >= 0)

    def bring(source, home, i):
        copy = pltpu.make_async_copy(source, home, local_sem.at[i])
        copy.start()
        return copy

    def units_of(s, e):
        return pl.ds(pl.multiple_of(s * 512 + e * UNITS, UNITS), UNITS)

    def block_of(s):
        return pl.ds(pl.multiple_of(s * 512, 512), 512)

    req_copy = bring(req_in, req, 0)
    barrier = pltpu.get_barrier_semaphore()
    for other in plane:
        pl.semaphore_signal(barrier, inc=1, device_id=target(other, h), device_id_type=MESH)
    for i in (2, 1, 3):
        pl.semaphore_signal(barrier, inc=1, device_id=target(b, hs[i]), device_id_type=MESH)
    tab_copy = bring(tab_in, tab, 1)
    win_copy = bring(win, win_all.at[h], 2)
    wout_copy = bring(wout, wout_all.at[h], 3)
    small = ((cot_in, cot), (slots_in, slots), (dense_in, dense), (dense_weight_in, dense_weight),
             (gate_weight_in, gate_weight), (tower_weight_in, tower_weight), (head_in, head))
    small_copies = [bring(source, home, 4 + i) for i, (source, home) in enumerate(small)]
    req_copy.wait()
    id_turned[...] = jnp.concatenate([req[...]] * 4, 0).T
    id_send[...] = id_turned[pl.ds(h, BATCH, stride=HIDDEN), :]
    pl.semaphore_wait(barrier, BATCH - 1 + HIDDEN - 1)

    for other in plane:
        remote(id_send.at[pl.ds(other, 1)], id_recv.at[pl.ds(b, 1)], small_ssem, id_rsem, other, h).start()
    spots = (
        pl.ds(pl.multiple_of(core * 128 + x * 32, 32), 32),
        pl.ds(pl.multiple_of(256 + core * 128 + z * 32, 32), 32),
    )
    spans = (pl.ds(pl.multiple_of(core * 128, 128), 128), pl.ds(pl.multiple_of(256 + core * 128, 128), 128))
    half = pl.ds(pl.multiple_of(core * 256, 256), 256)
    source_of = [lax.rem(h - i + HIDDEN, HIDDEN) for i in range(HIDDEN)]
    for i in order:
        for spot in spots:
            remote(win.at[spot], win_all.at[h, spot], side_ssem, y_rsem.at[i - 1], b, hs[i]).start()

    def spread(i):
        source = source_of[i]
        bulk_wait(win_all.at[source, pl.ds(0, 64)], y_rsem.at[i - 1])
        for j in (2, 1, 3):
            for spot, other in ((spots[0], z * 8 + xs[j] + core), (spots[1], zs[j] + x * 2 + core)):
                piece = win_all.at[source, spot]
                remote(piece, piece, side_ssem, p_rsem.at[i - 1], other, h).start()

    def to_core(i):
        source = source_of[i]
        bulk_wait(win_all.at[source, pl.ds(0, 192)], p_rsem.at[i - 1])
        for span in spans:
            piece = win_all.at[source, span]
            remote(piece, piece, side_ssem, c_rsem.at[i - 1], sibling, h).start()

    def out_to_core(i):
        bulk_wait(wout_all.at[source_of[i], half], wo_rsem.at[i - 1])
        piece = wout_all.at[source_of[i], half]
        remote(piece, piece, side_ssem, woc_rsem, sibling, h).start()

    tab_copy.wait()

    @block
    def _():
        high, low = split(tab[...])
        tab_split[0:EMBED, :] = high
        tab_split[EMBED : 2 * EMBED, :] = low

    id_recv[pl.ds(b, 1), :] = id_send[pl.ds(b, 1), :]
    bulk_wait(id_recv.at[pl.ds(0, BATCH - 1)], id_rsem)

    @block
    def _():
        found = ids_by_query(id_recv[...])
        ids[...] = found
        table, row = found // ROWS, lax.rem(found, ROWS)
        entries = []
        for pair in range(4):
            hot = jnp.concatenate([hot_of(row[j : j + 1, :], ROWS) for j in (2 * pair, 2 * pair + 1)], 1)
            value = dot_nn(tab_split[...], hot)
            for part in range(2):
                wanted = table[2 * pair + part : 2 * pair + part + 1, :]
                entry = jnp.zeros((ENTRY, 128), f32)
                for t in range(TABLES):
                    high = value[t * ENTRY : (t + 1) * ENTRY, part * 128 : part * 128 + 128]
                    low = value[EMBED + t * ENTRY : EMBED + (t + 1) * ENTRY, part * 128 : part * 128 + 128]
                    entry = jnp.where(wanted == t, high + low, entry)
                entries.append(entry)
        turned = jnp.concatenate(entries, 0).T
        for q in range(4):
            row_send[pl.ds(q, BATCH, stride=4), :] = turned[q * 32 : q * 32 + 32, :]

    mine = pl.ds(me * 4, 4)
    for dz, dx, dc, dy in EVERYWHERE:
        group = zs[dz] + xs[dx] + cores[dc]
        remote(row_send.at[pl.ds(group * 4, 4)], rows.at[mine], small_ssem, row_rsem, group, hs[dy]).start()
    rows[mine, :] = row_send[pl.ds(b * 4, 4), :]
    for i in order:
        spread(i)
    for copy in small_copies:
        copy.wait()
    wout_copy.wait()
    for i in order:
        remote(cot, cot_all.at[h], cot_ssem, cot_rsem, b, hs[i]).start()
        piece = wout_all.at[h, half]
        remote(piece, piece, side_ssem, wo_rsem.at[i - 1], b, hs[i]).start()
    win_copy.wait()

    @block
    def _():
        cot_all[pl.ds(h, 1)] = cot[...].reshape(1, TASKS, 128)
        dense_pad[...] = jnp.zeros_like(dense_pad)
        dense_pad[0:DENSE, :] = dense[...]
        weight_pad[...] = jnp.zeros_like(weight_pad)
        weight_pad[0:DENSE, 0:PROJ] = dense_weight[...]
        head_pad[...] = jnp.zeros_like(head_pad)
        head_pad[0:TASKS, 0:TOWER] = head[...]
        dense_h[...], dense_l[...] = split(dense_pad[...])
        projected = dot3_nn(split(weight_pad[...].T), (dense_h[...], dense_l[...]))
        feat_h[EMBED:WIDTH, :], feat_l[EMBED:WIDTH, :] = split(projected[0:PROJ, :])
        tower_h[...], tower_l[...] = split(tower_weight[...])
        gate_h[...], gate_l[...] = split(gate_weight[...])
        wh[block_of(h), :], wl[block_of(h), :] = split(win_all[h])

    @block
    def _():
        row = lax.rem(ids[...], ROWS)
        for j in range(8):
            hot_rows[:, j * 128 : (j + 1) * 128] = hot_of(row[j : j + 1, :], ROWS)

    @block
    def _():
        for t in range(TABLES):
            slot = slots[t : t + 1, :]
            owner = slot // 32
            code = jnp.where(lax.rem(owner, HIDDEN) == h, lax.rem(slot, 32) // 8 * 32 + owner // HIDDEN, -1)
            hot_slots[:, t * EXAMPLES : (t + 1) * EXAMPLES] = hot_of(code, 128)

    bulk_wait(rows.at[pl.ds(0, (DEVICES - 1) * 4)], row_rsem)

    def gather(first, last):
        for t in range(first, last):
            slot = slots[t : t + 1, :]
            low = lax.rem(slot, 8)
            value = dot_nn(lists[...], hot_of(lax.rem(slot, 32) // 8 * 128 + slot // 32, 512))
            high_sum = jnp.zeros((ENTRY, EXAMPLES), f32)
            low_sum = jnp.zeros((ENTRY, EXAMPLES), f32)
            for j in range(8):
                high_sum = jnp.where(low == j, value[j * 16 : j * 16 + 16, :], high_sum)
                low_sum = jnp.where(low == j, value[128 + j * 16 : 128 + j * 16 + 16, :], low_sum)
            feat_h[t * ENTRY : (t + 1) * ENTRY, :] = high_sum.astype(bf16)
            feat_l[t * ENTRY : (t + 1) * ENTRY, :] = low_sum.astype(bf16)

    @block
    def _():
        for q in range(4):
            at = slice(q * 128, q * 128 + 128)
            lists[0:128, at], lists[128:256, at] = split(rows[pl.ds(q, DEVICES, stride=4), :].T)
        gather(0, 13)

    to_core(1)
    block(lambda: gather(13, TABLES))

    def first_layer(s):
        at = block_of(s)
        inner, slope[at, :] = silu_both(dot3_nn((wh[at, :], wl[at, :]), (feat_h[...], feat_l[...])))
        inner_h[at, :], inner_l[at, :] = split(inner)

    def next_layer(*which):
        for i in which:
            bulk_wait(win_all.at[source_of[i], pl.ds(0, 256)], c_rsem.at[i - 1])

        @block
        def _():
            for i in which:
                s = source_of[i]
                wh[block_of(s), :], wl[block_of(s), :] = split(win_all[s])
                first_layer(s)

    @block
    def _():
        first_layer(h)
        logits = dot3_nn((gate_h[...], gate_l[...]), (feat_h[...], feat_l[...]))
        for k in range(TASKS):
            part = logits[k * 8 : k * 8 + 8, :]
            raised = jnp.exp(part - jnp.max(part, axis=0, keepdims=True))
            gates[k * 8 : k * 8 + 8, :] = raised / jnp.sum(raised, axis=0, keepdims=True)

    to_core(3)
    next_layer(1)
    to_core(2)
    next_layer(3)
    for i in order:
        out_to_core(i)
    next_layer(2)
    bulk_wait(wout_all.at[pl.ds(0, 3), pl.ds(0, 256)], woc_rsem)
    bulk_wait(cot_all.at[pl.ds(0, 3)], cot_rsem)

    def of_expert(refs, e):
        return tuple(
            jnp.concatenate([ref[s * 512 + e * UNITS : s * 512 + (e + 1) * UNITS, :] for s in range(HIDDEN)], 0)
            for ref in refs
        )

    def second_layer():
        mixed[...] = jnp.zeros_like(mixed)
        for s in range(HIDDEN):
            at = slice(s * 512, s * 512 + 512)
            oh[at, :], ol[at, :] = split(wout_all[s])
        for e in range(EXPERTS):
            outputs, eslope[e] = silu_both(dot3_tn(of_expert((oh, ol), e), of_expert((inner_h, inner_l), e)))
            eo[e] = outputs
            for k in range(TASKS):
                mixed[k] = mixed[k] + gates[k * 8 + e : k * 8 + e + 1, :] * outputs

    def tower_pass():
        head_turned = head_pad[...].T
        scores[...] = jnp.zeros_like(scores)
        for k in range(TASKS):
            at = slice(k * TOWER, (k + 1) * TOWER)
            value, tower_slope = silu_both(dot3_nn((tower_h[at, :], tower_l[at, :]), split(mixed[k])))
            column = jnp.broadcast_to(head_turned[0:TOWER, k : k + 1], (TOWER, EXAMPLES))
            predicted = sigmoid(jnp.sum(value * column, axis=0, keepdims=True))
            pred[k : k + 1, :] = predicted
            cotangent = jnp.concatenate([cot_all[i, k : k + 1, :] for i in range(HIDDEN)], 1)
            score = cotangent * predicted * (1.0 - predicted)
            scores[k : k + 1, :] = score
            towers[at, :] = value
            pre_grad = score * column * tower_slope
            pre_grads[at, :] = pre_grad
            mixed_grad[k] = dot3_tn((tower_h[at, :], tower_l[at, :]), split(pre_grad))

    def expert_grads(first, last):
        for e in range(first, last):
            outputs = eo[e]
            grad = jnp.zeros((OUT, EXAMPLES), f32)
            for k in range(TASKS):
                gate_slope[k * 8 + e : k * 8 + e + 1, :] = jnp.sum(mixed_grad[k] * outputs, axis=0, keepdims=True)
                grad = grad + gates[k * 8 + e : k * 8 + e + 1, :] * mixed_grad[k]
            out_split = split(grad * eslope[e])
            ep_h[e], ep_l[e] = out_split
            at = units_of(h, e)
            ig_h[at, :], ig_l[at, :] = split(dot3_nn((oh[at, :], ol[at, :]), out_split) * slope[at, :])

    def other_grads():
        for e in range(EXPERTS):
            places = [units_of(source_of[i], e) for i in order]
            side = tuple(jnp.concatenate([ref[at, :] for at in places], 0) for ref in (oh, ol))
            inner_grad = dot3_nn(side, (ep_h[e], ep_l[e]))
            for n, at in enumerate(places):
                ig_h[at, :], ig_l[at, :] = split(inner_grad[n * UNITS : (n + 1) * UNITS, :] * slope[at, :])

    def first_layer_grad(first, last):
        count = (last - first) * UNITS
        at = pl.ds(pl.multiple_of(h * 512 + first * UNITS, UNITS), count)
        in_grad = dot3_nt((ig_h[at, :], ig_l[at, :]), (feat_h[...], feat_l[...]))
        for q in range(4):
            start = 4 * first * UNITS + q * count
            in_sums[start : start + count, :] = in_grad[:, q * 128 : (q + 1) * 128]

    parts = []
    for first, last in IN_PARTS:
        start, size = 4 * first * UNITS, 4 * (last - first) * UNITS
        whole, halves = pl.ds(start, size), pl.ds(start // 2, size // 2)
        parts.append((in_sums.at[whole], in_swap.at[halves], in_pieces.at[halves], in_total.at[whole], size // 32))
    parts.append((rest_sums, rest_swap, rest_pieces, rest_total, REST_PIECE))

    def swap(n):
        sums, swapped, _, _, piece = parts[n]
        half_rows = 16 * piece
        theirs = sums.at[pl.ds(pl.multiple_of((1 - core) * half_rows, 8), half_rows)]
        remote(theirs, swapped, sum_ssem, swap_rsem.at[n], sibling, h).start()

    def send_pieces(n):
        sums, swapped, pieces, _, piece = parts[n]
        half_rows = 16 * piece
        bulk_wait(swapped, swap_rsem.at[n])
        swapped[...] += sums[pl.ds(pl.multiple_of(core * half_rows, 8), half_rows), :]
        own = pl.ds(pl.multiple_of(chip * piece, 8), piece)
        for other in chips:
            remote(
                swapped.at[pl.ds(pl.multiple_of(other * piece, 8), piece)], pieces.at[own],
                piece_ssem, piece_rsem.at[n], other * 2 + core, h,
            ).start()
        pieces[own, :] = swapped[own, :]

    def send_sums(n):
        _, _, pieces, total, piece = parts[n]
        half_rows = 16 * piece
        bulk_wait(pieces.at[pl.ds(0, 15 * piece)], piece_rsem.at[n])
        value = pieces[0:piece, :]
        for i in range(1, 16):
            value = value + pieces[i * piece : (i + 1) * piece, :]
        at = pl.ds(pl.multiple_of(core * half_rows + chip * piece, 8), piece)
        total[at, :] = value
        for other in chips:
            remote(total.at[at], total.at[at], full_ssem, full_rsem.at[n], other * 2 + core, h).start()

    def hand_on(n):
        _, _, _, total, piece = parts[n]
        bulk_wait(total.at[pl.ds(0, 15 * piece)], full_rsem.at[n])
        ours = total.at[pl.ds(pl.multiple_of(core * 16 * piece, 8), 16 * piece)]
        remote(ours, ours, sum_ssem, last_rsem, sibling, h).start()

    for n, (first, last) in enumerate(IN_PARTS):

        @block
        def _():
            if n == 0:
                second_layer()
                tower_pass()
            expert_grads(first, last)
            first_layer_grad(first, last)

        swap(n)
        if n:
            send_pieces(n - 1)

    @block
    def _():
        for k in range(TASKS):
            at = slice(k * TOWER, (k + 1) * TOWER)
            rest_sums[TOWER_AT + k * TOWER : TOWER_AT + (k + 1) * TOWER, :] = dot3_nt(
                split(pre_grads[at, :]), split(mixed[k])
            )
        head_rows = dot3_nt(split(scores[...]), split(towers[...]))
        rest_sums[HEAD_AT:REST_ROWS, :] = jnp.zeros((REST_ROWS - HEAD_AT, 128), f32)
        rest_sums[HEAD_AT : HEAD_AT + 1, :] = jnp.where(
            iota((1, 128), 1) < TOWER, head_rows[0:1, :], head_rows[1:2, :]
        )
        logit_grads = []
        for k in range(TASKS):
            gate, slopes = gates[k * 8 : k * 8 + 8, :], gate_slope[k * 8 : k * 8 + 8, :]
            logit_grads.append(gate * (slopes - jnp.sum(gate * slopes, axis=0, keepdims=True)))
        lgh[...], lgl[...] = split(jnp.concatenate(logit_grads, 0))
        gate_grad = dot3_nt((lgh[...], lgl[...]), (feat_h[...], feat_l[...]))
        for q in range(4):
            rest_sums[GATE_AT + q * 16 : GATE_AT + q * 16 + 16, :] = gate_grad[:, q * 128 : (q + 1) * 128]

        for e in range(EXPERTS):
            at = units_of(h, e)
            rest_sums[OUT_AT + e * UNITS : OUT_AT + (e + 1) * UNITS, :] = dot3_nt(
                (inner_h[at, :], inner_l[at, :]), (ep_h[e], ep_l[e])
            )

    swap(3)
    send_pieces(2)

    def feature_grad(low, high):
        at = slice(low, high)
        fg[at, :] = dot3_tn((wh[:, at], wl[:, at]), (ig_h[...], ig_l[...])) + dot3_tn(
            (gate_h[:, at], gate_l[:, at]), (lgh[...], lgl[...])
        )

    def scatter(first, last):
        spreads = []
        for t in range(first, last):
            low = lax.rem(slots[t : t + 1, :], 8)
            high, rest = split(fg[t * ENTRY : (t + 1) * ENTRY, :])
            where = jnp.broadcast_to(low, (ENTRY, EXAMPLES)).astype(jnp.int16)
            nothing = jnp.zeros((ENTRY, EXAMPLES), bf16)
            spreads.append(
                jnp.concatenate([jnp.where(where == j, value, nothing) for value in (high, rest) for j in range(8)], 0)
            )
        return dot_nt(jnp.concatenate(spreads, 1), hot_slots[:, first * EXAMPLES : last * EXAMPLES])

    block(other_grads)
    send_pieces(3)
    block(lambda: feature_grad(256, WIDTH))
    send_sums(0)

    @block
    def _():
        projected_grad = split(jnp.concatenate([fg[EMBED:WIDTH, :], jnp.zeros((32, EXAMPLES), f32)], 0))
        weight_part[...] = dot3_nt((dense_h[...], dense_l[...]), projected_grad)[0:16, :]
        dense_grad_out[...] = dot3_nn(split(weight_pad[...]), projected_grad)[0:DENSE, :]

    weight_copies = [
        remote(
            weight_part.at[pl.ds(pl.multiple_of((1 - core) * 8, 8), 8)], weight_swap,
            weight_send.at[0], weight_recv.at[0], sibling, h,
        )
    ]
    weight_copies[0].start()

    @block
    def _():
        slot_sum[...] = scatter(16, TABLES)

    weight_copies[0].wait_recv()
    weight_swap[...] += weight_part[pl.ds(pl.multiple_of(core * 8, 8), 8), :]
    weight_at = pl.ds(pl.multiple_of(chip * 8, 8), 8)
    for other in chips:
        remote(weight_swap, weight_got.at[weight_at], small_ssem, weight_rsem, other * 2 + core, h).start()
    weight_got[weight_at, :] = weight_swap[...]
    send_sums(1)

    @block
    def _():
        feature_grad(0, 256)
        slot_turned = slot_sum[...] + scatter(0, 16)
        slot_turned = (slot_turned[0:128, :] + slot_turned[128:256, :]).T
        for q in range(4):
            message[pl.ds(q, BATCH, stride=4), :] = slot_turned[q * 32 : q * 32 + 32, :]

    for other in plane:
        remote(message.at[pl.ds(other * 4, 4)], got.at[pl.ds(b * 4, 4)], small_ssem, slot_rsem, other, h).start()
    got[pl.ds(b * 4, 4), :] = message[pl.ds(b * 4, 4), :]
    send_sums(2)
    send_sums(3)
    bulk_wait(weight_got.at[pl.ds(0, 15 * 8)], weight_rsem)
    value = weight_got[0:8, :]
    for i in range(1, 16):
        value = value + weight_got[i * 8 : i * 8 + 8, :]
    weight_at = pl.ds(pl.multiple_of(core * 8, 8), 8)
    weight_total[weight_at, :] = value
    weight_copies.append(
        remote(
            weight_total.at[weight_at], weight_total.at[weight_at], weight_send.at[1], weight_recv.at[1], sibling, h
        )
    )
    weight_copies[1].start()
    for k in range(TASKS):
        pred_out[k : k + 1, :] = pred[k : k + 1, pl.ds(pl.multiple_of(h * 128, 128), 128)]

    hand_on(0)
    hand_on(1)
    bulk_wait(got.at[pl.ds(0, (BATCH - 1) * 4)], slot_rsem)

    @block
    def _():
        high, rest = split(jnp.concatenate([got[pl.ds(q, BATCH, stride=4), :] for q in range(4)], 0).T)
        table = ids[...] // ROWS
        spreads = []
        for j in range(8):
            where = jnp.broadcast_to(table[j : j + 1, :], (ENTRY, 128)).astype(jnp.int16)
            nothing = jnp.zeros((ENTRY, 128), bf16)
            chosen = [
                jnp.where(where == t, value[j * 16 : j * 16 + 16, :], nothing)
                for value in (high, rest)
                for t in range(TABLES)
            ]
            spreads.append(jnp.concatenate(chosen, 0))
        both = dot_nt(jnp.concatenate(spreads, 1), hot_rows[...])
        table_out[...] = both[0:EMBED, :] + both[EMBED : 2 * EMBED, :]

    weight_copies[1].wait_recv()
    weight_grad_out[...] = weight_total[0:DENSE, 0:PROJ]
    hand_on(2)
    hand_on(3)
    whole = in_total.at[pl.ds(0, IN_ROWS // 2 + 16 * REST_PIECE)]
    bulk_wait(whole, last_rsem)
    head_grad_out[0:1, :] = rest_total[HEAD_AT : HEAD_AT + 1, 0:TOWER]
    head_grad_out[1:2, :] = rest_total[HEAD_AT : HEAD_AT + 1, TOWER : 2 * TOWER]
    for copy in weight_copies:
        copy.wait_send()
    bulk_wait(cot_all.at[pl.ds(0, 3)], cot_ssem)
    bulk_wait(slope.at[pl.ds(0, 2 * 16 * (IN_ROWS // 32 + REST_PIECE) // 4)], sum_ssem)
    most = in_total.at[pl.ds(0, 15 * (IN_ROWS // 32 + REST_PIECE))]
    bulk_wait(most, piece_ssem)
    bulk_wait(most, full_ssem)
    bulk_wait(in_total.at[pl.ds(0, BATCH - 1 + (DEVICES - 1) * 4 + (BATCH - 1) * 4 + 15 * 8)], small_ssem)
    bulk_wait(slope.at[pl.ds(0, 192 + 576 + 768 + 2 * 192)], side_ssem)


def write_kernel(
    table, in_total, rest_total, weight_grad, head_grad, pred, dense_grad,
    table_out, in_out, out_out, tower_out, gate_out, weight_out, head_out, pred_out, dense_out, sems,
):
    copies = [(table, table_out), (rest_total.at[OUT_AT:GATE_AT], out_out), (rest_total.at[TOWER_AT:HEAD_AT], tower_out)]
    copies += [
        (
            in_total.at[pl.ds((4 * first + q * (last - first)) * UNITS, (last - first) * UNITS)],
            in_out.at[first * UNITS : last * UNITS, q * 128 : (q + 1) * 128],
        )
        for first, last in IN_PARTS
        for q in range(4)
    ]
    copies += [
        (rest_total.at[GATE_AT + q * 16 : GATE_AT + q * 16 + 16], gate_out.at[:, q * 128 : q * 128 + 128])
        for q in range(4)
    ]
    copies += [(weight_grad, weight_out), (head_grad, head_out), (pred, pred_out), (dense_grad, dense_out)]
    copies = [pltpu.make_async_copy(source, home, sems.at[i]) for i, (source, home) in enumerate(copies)]
    for copy in copies:
        copy.start()
    for copy in copies:
        copy.wait()


def on_device(
    tables, dense, dense_weight, expert_in, expert_out, gate_weight, tower_weight, head_weight, slots, requests, pred_cot
):
    i32 = jnp.int32
    dma = pltpu.SemaphoreType.DMA
    vmem = pltpu.VMEM
    anywhere = pl.BlockSpec(memory_space=pl.ANY)
    arrays = (
        requests[0].T,
        tables.transpose(0, 2, 1).reshape(EMBED, ROWS),
        expert_in.transpose(1, 2, 0).reshape(EXPERTS * UNITS, WIDTH),
        expert_out.reshape(EXPERTS * UNITS, OUT),
        pred_cot.T,
        slots.T,
        dense.T,
        dense_weight,
        gate_weight.transpose(0, 2, 1).reshape(TASKS * EXPERTS, WIDTH),
        tower_weight.transpose(0, 2, 1).reshape(TASKS * TOWER, OUT),
        head_weight,
    )
    shape = lambda *dims: jax.ShapeDtypeStruct(dims, f32)
    units = HIDDEN * 512, EXAMPLES
    outputs = EXPERTS, OUT, EXAMPLES
    results = pl.pallas_call(
        model_kernel,
        out_shape=[
            vmem((TASKS, 128), f32), vmem((DENSE, EXAMPLES), f32), vmem((EMBED, ROWS), f32), vmem((IN_ROWS, 128), f32),
            vmem((REST_ROWS, 128), f32), vmem((DENSE, PROJ), f32), vmem((TASKS, TOWER), f32),
        ],
        in_specs=[anywhere] * 11,
        out_specs=[VMEM] * 7,
        scratch_shapes=[
            vmem((32, 128), i32), vmem((EMBED, ROWS), f32), vmem((TASKS, 128), f32), vmem((TABLES, EXAMPLES), i32),
            vmem((DENSE, EXAMPLES), f32), vmem((DENSE, PROJ), f32), vmem((16, WIDTH), f32), vmem((128, OUT), f32),
            vmem((TASKS, TOWER), f32),
            vmem((128, 128), i32), vmem((32, 128), i32), vmem((32, 128), i32), vmem((8, 128), i32), vmem((128, 128), f32),
            vmem((512, 128), f32), vmem((2 * EMBED, ROWS), bf16),
            vmem((HIDDEN, 512, WIDTH), f32), vmem((HIDDEN, 512, OUT), f32), vmem((HIDDEN, TASKS, 128), f32),
            vmem((2048, WIDTH), bf16), vmem((2048, WIDTH), bf16), vmem((2048, OUT), bf16), vmem((2048, OUT), bf16),
            vmem((16, WIDTH), bf16), vmem((16, WIDTH), bf16), vmem((128, OUT), bf16), vmem((128, OUT), bf16),
            vmem((128, EXAMPLES), bf16), vmem((128, EXAMPLES), bf16),
            vmem((256, 512), bf16), vmem((WIDTH, EXAMPLES), bf16), vmem((WIDTH, EXAMPLES), bf16),
            vmem((128, EXAMPLES), f32), vmem((128, 128), f32), vmem((128, 128), f32),
            vmem(units, bf16), vmem(units, bf16), vmem(units, f32), vmem(units, bf16), vmem(units, bf16),
            vmem(outputs, f32), vmem(outputs, f32), vmem(outputs, bf16), vmem(outputs, bf16),
            vmem((16, EXAMPLES), f32), vmem((16, EXAMPLES), f32),
            vmem((TASKS, OUT, EXAMPLES), f32), vmem((TASKS, OUT, EXAMPLES), f32), vmem((TASKS, EXAMPLES), f32),
            vmem((128, EXAMPLES), f32), vmem((128, EXAMPLES), f32), vmem((16, EXAMPLES), f32),
            vmem((16, EXAMPLES), bf16), vmem((16, EXAMPLES), bf16),
            vmem((WIDTH, EXAMPLES), f32), vmem((256, 128), f32),
            vmem((IN_ROWS, 128), f32), vmem((REST_ROWS, 128), f32), vmem((IN_ROWS // 2, 128), f32),
            vmem((16 * REST_PIECE, 128), f32), vmem((IN_ROWS // 2, 128), f32), vmem((16 * REST_PIECE, 128), f32),
            vmem((128, 128), f32), vmem((128, 128), f32), vmem((16, 128), f32), vmem((8, 128), f32),
            vmem((128, 128), f32), vmem((16, 128), f32), vmem((ROWS, ROWS), bf16),
            vmem((128, TABLES * EXAMPLES), bf16),
            dma((11,)), dma((3,)), dma((3,)), dma((3,)), dma((3,)), dma, dma, dma,
            dma, dma, dma, dma, dma((2,)), dma((2,)), dma((4,)), dma((4,)), dma((4,)), dma,
            dma, dma, dma, dma, dma,
        ],
        compiler_params=pltpu.CompilerParams(vmem_limit_bytes=LIMIT, collective_id=0, has_side_effects=True),
        name="model",
    )(*arrays)
    results = [pltpu.with_memory_space_constraint(result, pltpu.VMEM) for result in results]
    pred, dense_grad, table_grad, in_total, rest_total, weight_grad, head_grad = results
    table_grad, in_grad, out_grad, tower_grad, gate_grad, weight_grad, head_grad, pred, dense_grad = pl.pallas_call(
        write_kernel,
        out_shape=[
            shape(EMBED, ROWS), shape(512, WIDTH), shape(512, OUT), shape(TASKS * TOWER, OUT),
            shape(TASKS * EXPERTS, WIDTH), shape(DENSE, PROJ), shape(TASKS, TOWER), shape(TASKS, 128),
            shape(DENSE, EXAMPLES),
        ],
        in_specs=[anywhere] * 7,
        out_specs=[anywhere] * 9,
        scratch_shapes=[dma((23,))],
        compiler_params=pltpu.CompilerParams(vmem_limit_bytes=LIMIT),
        name="write",
    )(table_grad, in_total, rest_total, weight_grad, head_grad, pred, dense_grad)
    return (
        pred.T,
        dense_grad.T,
        table_grad.reshape(TABLES, ENTRY, ROWS).transpose(0, 2, 1),
        weight_grad,
        in_grad.reshape(EXPERTS, UNITS, WIDTH).transpose(2, 0, 1),
        out_grad.reshape(EXPERTS, UNITS, OUT),
        gate_grad.reshape(TASKS, EXPERTS, WIDTH).transpose(0, 2, 1),
        tower_grad.reshape(TASKS, TOWER, OUT).transpose(0, 2, 1),
        head_grad,
    )


def solution(mesh):
    placed = (
        P(None, ("batch", "hidden"), None),
        P("batch", None),
        P(),
        P(None, None, "hidden"),
        P(None, "hidden", None),
        P(),
        P(),
        P(),
        P("batch", None),
        P("batch", None, None),
        P(("batch", "hidden"), None),
    )
    return jax.shard_map(
        on_device,
        mesh=mesh,
        in_specs=placed,
        out_specs=(
            P(("batch", "hidden"), None),
            P("batch", None),
            P(None, ("batch", "hidden"), None),
            P(),
            P(None, None, "hidden"),
            P(None, "hidden", None),
            P(),
            P(),
            P(),
        ),
        check_vma=False,
    )
```

```python
import jax
import jax.numpy as jnp
from jax import lax
from jax.experimental import pallas as pl
from jax.experimental.pallas import tpu as pltpu
from jax.sharding import PartitionSpec as P

f32 = jnp.float32
bf16 = jnp.bfloat16
MESH = pl.DeviceIdType.MESH
VMEM = pl.BlockSpec(memory_space=pltpu.VMEM)
LIMIT = 56 * 2**20

TABLES, ROWS, ENTRY = 26, 1024, 16
BATCH, HIDDEN = 32, 4
DEVICES = BATCH * HIDDEN
EXPERTS, UNITS, OUT, WIDTH = 8, 64, 128, 512
TASKS, TOWER, DENSE, PROJ = 2, 64, 13, 96
EXAMPLES = 512
EMBED = TABLES * ENTRY

IN_PARTS = ((0, 3), (3, 6), (6, 8))
IN_ROWS = 2048
OUT_AT, GATE_AT, TOWER_AT, HEAD_AT = 0, 512, 576, 704
REST_ROWS, REST_PIECE = 768, 24


def split(value):
    high = value.astype(bf16)
    return high, (value - high.astype(f32)).astype(bf16)


def dot_nn(a, b):
    return lax.dot_general(a, b, (((1,), (0,)), ((), ())), preferred_element_type=f32)


def dot_nt(a, b):
    return lax.dot_general(a, b, (((1,), (1,)), ((), ())), preferred_element_type=f32)


def dot_tn(a, b):
    return lax.dot_general(a, b, (((0,), (0,)), ((), ())), preferred_element_type=f32)


def dot3_tn(a, b):
    (ah, al), (bh, bl) = a, b
    return dot_tn(ah, bh) + dot_tn(al, bh) + dot_tn(ah, bl)


def dot3_nn(a, b):
    (ah, al), (bh, bl) = a, b
    return dot_nn(jnp.concatenate([ah, al, ah], 1), jnp.concatenate([bh, bh, bl], 0))


def dot3_nt(a, b):
    (ah, al), (bh, bl) = a, b
    count = ah.shape[0]
    both = dot_nt(jnp.concatenate([ah, al], 0), bh)
    return both[0:count, :] + both[count : 2 * count, :] + dot_nt(ah, bl)


def sigmoid(value):
    return 0.5 * jnp.tanh(0.5 * value) + 0.5


def silu_both(value):
    sigma = sigmoid(value)
    result = value * sigma
    return result, sigma + result * (1.0 - sigma)


def iota(shape, axis):
    return lax.broadcasted_iota(jnp.int32, shape, axis)


def hops(offset):
    return min(offset, 4 - offset)


PLANE = sorted(
    ((dz, dx, dc) for dz in range(4) for dx in range(4) for dc in range(2) if dz or dx or dc),
    key=lambda d: -(2 * hops(d[0]) + 2 * hops(d[1]) + d[2]),
)
EVERYWHERE = sorted(
    ((dz, dx, dc, dy) for dz in range(4) for dx in range(4) for dc in range(2) for dy in range(4) if dz or dx or dc or dy),
    key=lambda d: -(2 * hops(d[0]) + 2 * hops(d[1]) + d[2] + 2 * hops(d[3])),
)
CHIPS = [(dz, dx) for dz, dx, dc in PLANE if not dc and (dz or dx)]


def target(b, h):
    return {"batch": b, "hidden": h}


def remote(src, dst, send, recv, b, h):
    return pltpu.make_async_remote_copy(src, dst, send, recv, device_id=target(b, h), device_id_type=MESH)


def bulk_wait(ref, sem):
    pltpu.make_async_copy(ref, ref, sem).wait()


def ids_by_query(received):
    turned = jnp.concatenate([received] * 4, 0).T
    lane = iota((8, 128), 1) // 32
    out = jnp.zeros((8, 128), jnp.int32)
    for q in range(4):
        out = jnp.where(lane == q, turned[q * 8 : q * 8 + 8, :], out)
    return out


def hot_of(code, count):
    rows = iota((count, code.shape[1]), 0).astype(jnp.int16)
    return jnp.where(rows == code.astype(jnp.int16), bf16(1.0), bf16(0.0))


def model_kernel(
    req_in, tab_in, win, wout, cot_in, slots_in, dense_in, dense_weight_in, gate_weight_in, tower_weight_in, head_in,
    pred_out, dense_grad_out, table_out, in_total, rest_total, weight_grad_out, head_grad_out,
    req, tab, cot, slots, dense, dense_weight, gate_weight, tower_weight, head,
    id_turned, id_send, id_recv, ids, row_send, rows, tab_split, win_all, wout_all, cot_all,
    wh, wl, oh, ol, gate_h, gate_l, tower_h, tower_l, dense_h, dense_l, lists, feat_h, feat_l,
    dense_pad, weight_pad, head_pad,
    inner_h, inner_l, slope, ig_h, ig_l, eo, eslope, ep_h, ep_l, gates, gate_slope, mixed, mixed_grad, pred,
    towers, pre_grads, scores, lgh, lgl, fg, slot_sum,
    in_sums, rest_sums, in_swap, rest_swap, in_pieces, rest_pieces,
    message, got, weight_part, weight_swap, weight_got, weight_total, hot_rows, hot_slots,
    local_sem, y_rsem, p_rsem, c_rsem, wo_rsem, woc_rsem, cot_ssem, cot_rsem,
    id_rsem, row_rsem, slot_rsem, weight_rsem, weight_send, weight_recv, swap_rsem, piece_rsem, full_rsem, last_rsem,
    small_ssem, sum_ssem, side_ssem, piece_ssem, full_ssem,
):
    b, h = lax.axis_index("batch"), lax.axis_index("hidden")
    core, x, z, chip = lax.rem(b, 2), lax.rem(b // 2, 4), b // 8, b // 2
    me = b * HIDDEN + h
    sibling = b + 1 - 2 * core
    zs = [lax.rem(z + d, 4) * 8 for d in range(4)]
    xs = [lax.rem(x + d, 4) * 2 for d in range(4)]
    cores = [core, 1 - core]
    hs = [lax.rem(h + d, HIDDEN) for d in range(HIDDEN)]
    chips = [(zs[dz] + xs[dx]) // 2 for dz, dx in CHIPS]
    plane = [zs[dz] + xs[dx] + cores[dc] for dz, dx, dc in PLANE]
    order = (1, 3, 2)
    block = pl.when(core >= 0)

    def bring(source, home, i):
        copy = pltpu.make_async_copy(source, home, local_sem.at[i])
        copy.start()
        return copy

    def units_of(s, e):
        return pl.ds(pl.multiple_of(s * 512 + e * UNITS, UNITS), UNITS)

    def block_of(s):
        return pl.ds(pl.multiple_of(s * 512, 512), 512)

    req_copy = bring(req_in, req, 0)
    barrier = pltpu.get_barrier_semaphore()
    for other in plane:
        pl.semaphore_signal(barrier, inc=1, device_id=target(other, h), device_id_type=MESH)
    for i in (2, 1, 3):
        pl.semaphore_signal(barrier, inc=1, device_id=target(b, hs[i]), device_id_type=MESH)
    tab_copy = bring(tab_in, tab, 1)
    win_copy = bring(win, win_all.at[h], 2)
    wout_copy = bring(wout, wout_all.at[h], 3)
    small = ((cot_in, cot), (slots_in, slots), (dense_in, dense), (dense_weight_in, dense_weight),
             (gate_weight_in, gate_weight), (tower_weight_in, tower_weight), (head_in, head))
    small_copies = [bring(source, home, 4 + i) for i, (source, home) in enumerate(small)]
    req_copy.wait()
    id_turned[...] = jnp.concatenate([req[...]] * 4, 0).T
    id_send[...] = id_turned[pl.ds(h, BATCH, stride=HIDDEN), :]
    pl.semaphore_wait(barrier, BATCH - 1 + HIDDEN - 1)

    for other in plane:
        remote(id_send.at[pl.ds(other, 1)], id_recv.at[pl.ds(b, 1)], small_ssem, id_rsem, other, h).start()
    spots = (
        pl.ds(pl.multiple_of(core * 128 + x * 32, 32), 32),
        pl.ds(pl.multiple_of(256 + core * 128 + z * 32, 32), 32),
    )
    spans = (pl.ds(pl.multiple_of(core * 128, 128), 128), pl.ds(pl.multiple_of(256 + core * 128, 128), 128))
    half = pl.ds(pl.multiple_of(core * 256, 256), 256)
    source_of = [lax.rem(h - i + HIDDEN, HIDDEN) for i in range(HIDDEN)]
    for i in order:
        for spot in spots:
            remote(win.at[spot], win_all.at[h, spot], side_ssem, y_rsem.at[i - 1], b, hs[i]).start()

    def spread(i):
        source = source_of[i]
        bulk_wait(win_all.at[source, pl.ds(0, 64)], y_rsem.at[i - 1])
        for j in (2, 1, 3):
            for spot, other in ((spots[0], z * 8 + xs[j] + core), (spots[1], zs[j] + x * 2 + core)):
                piece = win_all.at[source, spot]
                remote(piece, piece, side_ssem, p_rsem.at[i - 1], other, h).start()

    def to_core(i):
        source = source_of[i]
        bulk_wait(win_all.at[source, pl.ds(0, 192)], p_rsem.at[i - 1])
        for span in spans:
            piece = win_all.at[source, span]
            remote(piece, piece, side_ssem, c_rsem.at[i - 1], sibling, h).start()

    def out_to_core(i):
        bulk_wait(wout_all.at[source_of[i], half], wo_rsem.at[i - 1])
        piece = wout_all.at[source_of[i], half]
        remote(piece, piece, side_ssem, woc_rsem, sibling, h).start()

    tab_copy.wait()

    @block
    def _():
        high, low = split(tab[...])
        tab_split[0:EMBED, :] = high
        tab_split[EMBED : 2 * EMBED, :] = low

    id_recv[pl.ds(b, 1), :] = id_send[pl.ds(b, 1), :]
    bulk_wait(id_recv.at[pl.ds(0, BATCH - 1)], id_rsem)

    @block
    def _():
        found = ids_by_query(id_recv[...])
        ids[...] = found
        table, row = found // ROWS, lax.rem(found, ROWS)
        entries = []
        for pair in range(4):
            hot = jnp.concatenate([hot_of(row[j : j + 1, :], ROWS) for j in (2 * pair, 2 * pair + 1)], 1)
            value = dot_nn(tab_split[...], hot)
            for part in range(2):
                wanted = table[2 * pair + part : 2 * pair + part + 1, :]
                entry = jnp.zeros((ENTRY, 128), f32)
                for t in range(TABLES):
                    high = value[t * ENTRY : (t + 1) * ENTRY, part * 128 : part * 128 + 128]
                    low = value[EMBED + t * ENTRY : EMBED + (t + 1) * ENTRY, part * 128 : part * 128 + 128]
                    entry = jnp.where(wanted == t, high + low, entry)
                entries.append(entry)
        turned = jnp.concatenate(entries, 0).T
        for q in range(4):
            row_send[pl.ds(q, BATCH, stride=4), :] = turned[q * 32 : q * 32 + 32, :]

    mine = pl.ds(me * 4, 4)
    for dz, dx, dc, dy in EVERYWHERE:
        group = zs[dz] + xs[dx] + cores[dc]
        remote(row_send.at[pl.ds(group * 4, 4)], rows.at[mine], small_ssem, row_rsem, group, hs[dy]).start()
    rows[mine, :] = row_send[pl.ds(b * 4, 4), :]
    for i in order:
        spread(i)
    for copy in small_copies:
        copy.wait()
    wout_copy.wait()
    for i in order:
        remote(cot, cot_all.at[h], cot_ssem, cot_rsem, b, hs[i]).start()
        piece = wout_all.at[h, half]
        remote(piece, piece, side_ssem, wo_rsem.at[i - 1], b, hs[i]).start()
    win_copy.wait()

    @block
    def _():
        cot_all[pl.ds(h, 1)] = cot[...].reshape(1, TASKS, 128)
        dense_pad[...] = jnp.zeros_like(dense_pad)
        dense_pad[0:DENSE, :] = dense[...]
        weight_pad[...] = jnp.zeros_like(weight_pad)
        weight_pad[0:DENSE, 0:PROJ] = dense_weight[...]
        head_pad[...] = jnp.zeros_like(head_pad)
        head_pad[0:TASKS, 0:TOWER] = head[...]
        dense_h[...], dense_l[...] = split(dense_pad[...])
        projected = dot3_nn(split(weight_pad[...].T), (dense_h[...], dense_l[...]))
        feat_h[EMBED:WIDTH, :], feat_l[EMBED:WIDTH, :] = split(projected[0:PROJ, :])
        tower_h[...], tower_l[...] = split(tower_weight[...])
        gate_h[...], gate_l[...] = split(gate_weight[...])
        wh[block_of(h), :], wl[block_of(h), :] = split(win_all[h])

    @block
    def _():
        row = lax.rem(ids[...], ROWS)
        for j in range(8):
            hot_rows[:, j * 128 : (j + 1) * 128] = hot_of(row[j : j + 1, :], ROWS)

    @block
    def _():
        for t in range(TABLES):
            slot = slots[t : t + 1, :]
            owner = slot // 32
            code = jnp.where(lax.rem(owner, HIDDEN) == h, lax.rem(slot, 32) // 8 * 32 + owner // HIDDEN, -1)
            hot_slots[:, t * EXAMPLES : (t + 1) * EXAMPLES] = hot_of(code, 128)

    bulk_wait(rows.at[pl.ds(0, (DEVICES - 1) * 4)], row_rsem)

    def gather(first, last):
        for t in range(first, last):
            slot = slots[t : t + 1, :]
            low = lax.rem(slot, 8)
            value = dot_nn(lists[...], hot_of(lax.rem(slot, 32) // 8 * 128 + slot // 32, 512))
            high_sum = jnp.zeros((ENTRY, EXAMPLES), f32)
            low_sum = jnp.zeros((ENTRY, EXAMPLES), f32)
            for j in range(8):
                high_sum = jnp.where(low == j, value[j * 16 : j * 16 + 16, :], high_sum)
                low_sum = jnp.where(low == j, value[128 + j * 16 : 128 + j * 16 + 16, :], low_sum)
            feat_h[t * ENTRY : (t + 1) * ENTRY, :] = high_sum.astype(bf16)
            feat_l[t * ENTRY : (t + 1) * ENTRY, :] = low_sum.astype(bf16)

    @block
    def _():
        for q in range(4):
            at = slice(q * 128, q * 128 + 128)
            lists[0:128, at], lists[128:256, at] = split(rows[pl.ds(q, DEVICES, stride=4), :].T)
        gather(0, 13)

    to_core(1)
    block(lambda: gather(13, TABLES))

    def first_layer(s):
        at = block_of(s)
        inner, slope[at, :] = silu_both(dot3_nn((wh[at, :], wl[at, :]), (feat_h[...], feat_l[...])))
        inner_h[at, :], inner_l[at, :] = split(inner)

    def next_layer(*which):
        for i in which:
            bulk_wait(win_all.at[source_of[i], pl.ds(0, 256)], c_rsem.at[i - 1])

        @block
        def _():
            for i in which:
                s = source_of[i]
                wh[block_of(s), :], wl[block_of(s), :] = split(win_all[s])
                first_layer(s)

    @block
    def _():
        first_layer(h)
        logits = dot3_nn((gate_h[...], gate_l[...]), (feat_h[...], feat_l[...]))
        for k in range(TASKS):
            part = logits[k * 8 : k * 8 + 8, :]
            raised = jnp.exp(part - jnp.max(part, axis=0, keepdims=True))
            gates[k * 8 : k * 8 + 8, :] = raised / jnp.sum(raised, axis=0, keepdims=True)

    to_core(3)
    next_layer(1)
    to_core(2)
    next_layer(3)
    for i in order:
        out_to_core(i)
    next_layer(2)
    bulk_wait(wout_all.at[pl.ds(0, 3), pl.ds(0, 256)], woc_rsem)
    bulk_wait(cot_all.at[pl.ds(0, 3)], cot_rsem)

    def of_expert(refs, e):
        return tuple(
            jnp.concatenate([ref[s * 512 + e * UNITS : s * 512 + (e + 1) * UNITS, :] for s in range(HIDDEN)], 0)
            for ref in refs
        )

    def second_layer():
        mixed[...] = jnp.zeros_like(mixed)
        for s in range(HIDDEN):
            at = slice(s * 512, s * 512 + 512)
            oh[at, :], ol[at, :] = split(wout_all[s])
        for e in range(EXPERTS):
            outputs, eslope[e] = silu_both(dot3_tn(of_expert((oh, ol), e), of_expert((inner_h, inner_l), e)))
            eo[e] = outputs
            for k in range(TASKS):
                mixed[k] = mixed[k] + gates[k * 8 + e : k * 8 + e + 1, :] * outputs

    def tower_pass():
        head_turned = head_pad[...].T
        scores[...] = jnp.zeros_like(scores)
        for k in range(TASKS):
            at = slice(k * TOWER, (k + 1) * TOWER)
            value, tower_slope = silu_both(dot3_nn((tower_h[at, :], tower_l[at, :]), split(mixed[k])))
            column = jnp.broadcast_to(head_turned[0:TOWER, k : k + 1], (TOWER, EXAMPLES))
            predicted = sigmoid(jnp.sum(value * column, axis=0, keepdims=True))
            pred[k : k + 1, :] = predicted
            cotangent = jnp.concatenate([cot_all[i, k : k + 1, :] for i in range(HIDDEN)], 1)
            score = cotangent * predicted * (1.0 - predicted)
            scores[k : k + 1, :] = score
            towers[at, :] = value
            pre_grad = score * column * tower_slope
            pre_grads[at, :] = pre_grad
            mixed_grad[k] = dot3_tn((tower_h[at, :], tower_l[at, :]), split(pre_grad))

    @block
    def _():
        second_layer()
        tower_pass()

    def expert_grads(first, last):
        for e in range(first, last):
            outputs = eo[e]
            grad = jnp.zeros((OUT, EXAMPLES), f32)
            for k in range(TASKS):
                gate_slope[k * 8 + e : k * 8 + e + 1, :] = jnp.sum(mixed_grad[k] * outputs, axis=0, keepdims=True)
                grad = grad + gates[k * 8 + e : k * 8 + e + 1, :] * mixed_grad[k]
            out_split = split(grad * eslope[e])
            ep_h[e], ep_l[e] = out_split
            at = units_of(h, e)
            ig_h[at, :], ig_l[at, :] = split(dot3_nn((oh[at, :], ol[at, :]), out_split) * slope[at, :])

    def other_grads():
        for e in range(EXPERTS):
            places = [units_of(source_of[i], e) for i in order]
            side = tuple(jnp.concatenate([ref[at, :] for at in places], 0) for ref in (oh, ol))
            inner_grad = dot3_nn(side, (ep_h[e], ep_l[e]))
            for n, at in enumerate(places):
                ig_h[at, :], ig_l[at, :] = split(inner_grad[n * UNITS : (n + 1) * UNITS, :] * slope[at, :])

    def first_layer_grad(first, last):
        count = (last - first) * UNITS
        at = pl.ds(pl.multiple_of(h * 512 + first * UNITS, UNITS), count)
        in_grad = dot3_nt((ig_h[at, :], ig_l[at, :]), (feat_h[...], feat_l[...]))
        for q in range(4):
            start = 4 * first * UNITS + q * count
            in_sums[start : start + count, :] = in_grad[:, q * 128 : (q + 1) * 128]

    parts = []
    for first, last in IN_PARTS:
        start, size = 4 * first * UNITS, 4 * (last - first) * UNITS
        whole, halves = pl.ds(start, size), pl.ds(start // 2, size // 2)
        parts.append((in_sums.at[whole], in_swap.at[halves], in_pieces.at[halves], in_total.at[whole], size // 32))
    parts.append((rest_sums, rest_swap, rest_pieces, rest_total, REST_PIECE))

    def swap(n):
        sums, swapped, _, _, piece = parts[n]
        half_rows = 16 * piece
        theirs = sums.at[pl.ds(pl.multiple_of((1 - core) * half_rows, 8), half_rows)]
        remote(theirs, swapped, sum_ssem, swap_rsem.at[n], sibling, h).start()

    def send_pieces(n):
        sums, swapped, pieces, _, piece = parts[n]
        half_rows = 16 * piece
        bulk_wait(swapped, swap_rsem.at[n])
        swapped[...] += sums[pl.ds(pl.multiple_of(core * half_rows, 8), half_rows), :]
        own = pl.ds(pl.multiple_of(chip * piece, 8), piece)
        for other in chips:
            remote(
                swapped.at[pl.ds(pl.multiple_of(other * piece, 8), piece)], pieces.at[own],
                piece_ssem, piece_rsem.at[n], other * 2 + core, h,
            ).start()
        pieces[own, :] = swapped[own, :]

    def send_sums(n):
        _, _, pieces, total, piece = parts[n]
        half_rows = 16 * piece
        bulk_wait(pieces.at[pl.ds(0, 15 * piece)], piece_rsem.at[n])
        value = pieces[0:piece, :]
        for i in range(1, 16):
            value = value + pieces[i * piece : (i + 1) * piece, :]
        at = pl.ds(pl.multiple_of(core * half_rows + chip * piece, 8), piece)
        total[at, :] = value
        for other in chips:
            remote(total.at[at], total.at[at], full_ssem, full_rsem.at[n], other * 2 + core, h).start()

    def hand_on(n):
        _, _, _, total, piece = parts[n]
        bulk_wait(total.at[pl.ds(0, 15 * piece)], full_rsem.at[n])
        ours = total.at[pl.ds(pl.multiple_of(core * 16 * piece, 8), 16 * piece)]
        remote(ours, ours, sum_ssem, last_rsem, sibling, h).start()

    for n, (first, last) in enumerate(IN_PARTS):

        @block
        def _():
            expert_grads(first, last)
            first_layer_grad(first, last)

        swap(n)
        if n:
            send_pieces(n - 1)

    @block
    def _():
        for k in range(TASKS):
            at = slice(k * TOWER, (k + 1) * TOWER)
            rest_sums[TOWER_AT + k * TOWER : TOWER_AT + (k + 1) * TOWER, :] = dot3_nt(
                split(pre_grads[at, :]), split(mixed[k])
            )
        head_rows = dot3_nt(split(scores[...]), split(towers[...]))
        rest_sums[HEAD_AT:REST_ROWS, :] = jnp.zeros((REST_ROWS - HEAD_AT, 128), f32)
        rest_sums[HEAD_AT : HEAD_AT + 1, :] = jnp.where(
            iota((1, 128), 1) < TOWER, head_rows[0:1, :], head_rows[1:2, :]
        )
        logit_grads = []
        for k in range(TASKS):
            gate, slopes = gates[k * 8 : k * 8 + 8, :], gate_slope[k * 8 : k * 8 + 8, :]
            logit_grads.append(gate * (slopes - jnp.sum(gate * slopes, axis=0, keepdims=True)))
        lgh[...], lgl[...] = split(jnp.concatenate(logit_grads, 0))
        gate_grad = dot3_nt((lgh[...], lgl[...]), (feat_h[...], feat_l[...]))
        for q in range(4):
            rest_sums[GATE_AT + q * 16 : GATE_AT + q * 16 + 16, :] = gate_grad[:, q * 128 : (q + 1) * 128]

        for e in range(EXPERTS):
            at = units_of(h, e)
            rest_sums[OUT_AT + e * UNITS : OUT_AT + (e + 1) * UNITS, :] = dot3_nt(
                (inner_h[at, :], inner_l[at, :]), (ep_h[e], ep_l[e])
            )

    swap(3)
    send_pieces(2)

    def feature_grad(low, high):
        at = slice(low, high)
        fg[at, :] = dot3_tn((wh[:, at], wl[:, at]), (ig_h[...], ig_l[...])) + dot3_tn(
            (gate_h[:, at], gate_l[:, at]), (lgh[...], lgl[...])
        )

    def scatter(first, last):
        spreads = []
        for t in range(first, last):
            low = lax.rem(slots[t : t + 1, :], 8)
            high, rest = split(fg[t * ENTRY : (t + 1) * ENTRY, :])
            where = jnp.broadcast_to(low, (ENTRY, EXAMPLES)).astype(jnp.int16)
            nothing = jnp.zeros((ENTRY, EXAMPLES), bf16)
            spreads.append(
                jnp.concatenate([jnp.where(where == j, value, nothing) for value in (high, rest) for j in range(8)], 0)
            )
        return dot_nt(jnp.concatenate(spreads, 1), hot_slots[:, first * EXAMPLES : last * EXAMPLES])

    block(other_grads)
    send_pieces(3)
    block(lambda: feature_grad(256, WIDTH))
    send_sums(0)

    @block
    def _():
        projected_grad = split(jnp.concatenate([fg[EMBED:WIDTH, :], jnp.zeros((32, EXAMPLES), f32)], 0))
        weight_part[...] = dot3_nt((dense_h[...], dense_l[...]), projected_grad)[0:16, :]
        dense_grad_out[...] = dot3_nn(split(weight_pad[...]), projected_grad)[0:DENSE, :]

    weight_copies = [
        remote(
            weight_part.at[pl.ds(pl.multiple_of((1 - core) * 8, 8), 8)], weight_swap,
            weight_send.at[0], weight_recv.at[0], sibling, h,
        )
    ]
    weight_copies[0].start()

    @block
    def _():
        slot_sum[...] = scatter(16, TABLES)

    weight_copies[0].wait_recv()
    weight_swap[...] += weight_part[pl.ds(pl.multiple_of(core * 8, 8), 8), :]
    weight_at = pl.ds(pl.multiple_of(chip * 8, 8), 8)
    for other in chips:
        remote(weight_swap, weight_got.at[weight_at], small_ssem, weight_rsem, other * 2 + core, h).start()
    weight_got[weight_at, :] = weight_swap[...]
    send_sums(1)

    @block
    def _():
        feature_grad(0, 256)
        slot_turned = slot_sum[...] + scatter(0, 16)
        slot_turned = (slot_turned[0:128, :] + slot_turned[128:256, :]).T
        for q in range(4):
            message[pl.ds(q, BATCH, stride=4), :] = slot_turned[q * 32 : q * 32 + 32, :]

    for other in plane:
        remote(message.at[pl.ds(other * 4, 4)], got.at[pl.ds(b * 4, 4)], small_ssem, slot_rsem, other, h).start()
    got[pl.ds(b * 4, 4), :] = message[pl.ds(b * 4, 4), :]
    send_sums(2)
    send_sums(3)
    bulk_wait(weight_got.at[pl.ds(0, 15 * 8)], weight_rsem)
    value = weight_got[0:8, :]
    for i in range(1, 16):
        value = value + weight_got[i * 8 : i * 8 + 8, :]
    weight_at = pl.ds(pl.multiple_of(core * 8, 8), 8)
    weight_total[weight_at, :] = value
    weight_copies.append(
        remote(
            weight_total.at[weight_at], weight_total.at[weight_at], weight_send.at[1], weight_recv.at[1], sibling, h
        )
    )
    weight_copies[1].start()
    for k in range(TASKS):
        pred_out[k : k + 1, :] = pred[k : k + 1, pl.ds(pl.multiple_of(h * 128, 128), 128)]

    hand_on(0)
    hand_on(1)
    bulk_wait(got.at[pl.ds(0, (BATCH - 1) * 4)], slot_rsem)

    @block
    def _():
        high, rest = split(jnp.concatenate([got[pl.ds(q, BATCH, stride=4), :] for q in range(4)], 0).T)
        table = ids[...] // ROWS
        spreads = []
        for j in range(8):
            where = jnp.broadcast_to(table[j : j + 1, :], (ENTRY, 128)).astype(jnp.int16)
            nothing = jnp.zeros((ENTRY, 128), bf16)
            chosen = [
                jnp.where(where == t, value[j * 16 : j * 16 + 16, :], nothing)
                for value in (high, rest)
                for t in range(TABLES)
            ]
            spreads.append(jnp.concatenate(chosen, 0))
        both = dot_nt(jnp.concatenate(spreads, 1), hot_rows[...])
        table_out[...] = both[0:EMBED, :] + both[EMBED : 2 * EMBED, :]

    weight_copies[1].wait_recv()
    weight_grad_out[...] = weight_total[0:DENSE, 0:PROJ]
    hand_on(2)
    hand_on(3)
    whole = in_total.at[pl.ds(0, IN_ROWS // 2 + 16 * REST_PIECE)]
    bulk_wait(whole, last_rsem)
    head_grad_out[0:1, :] = rest_total[HEAD_AT : HEAD_AT + 1, 0:TOWER]
    head_grad_out[1:2, :] = rest_total[HEAD_AT : HEAD_AT + 1, TOWER : 2 * TOWER]
    for copy in weight_copies:
        copy.wait_send()
    bulk_wait(cot_all.at[pl.ds(0, 3)], cot_ssem)
    bulk_wait(slope.at[pl.ds(0, 2 * 16 * (IN_ROWS // 32 + REST_PIECE) // 4)], sum_ssem)
    most = in_total.at[pl.ds(0, 15 * (IN_ROWS // 32 + REST_PIECE))]
    bulk_wait(most, piece_ssem)
    bulk_wait(most, full_ssem)
    bulk_wait(in_total.at[pl.ds(0, BATCH - 1 + (DEVICES - 1) * 4 + (BATCH - 1) * 4 + 15 * 8)], small_ssem)
    bulk_wait(slope.at[pl.ds(0, 192 + 576 + 768 + 2 * 192)], side_ssem)


def write_kernel(
    table, in_total, rest_total, weight_grad, head_grad, pred, dense_grad,
    table_out, in_out, out_out, tower_out, gate_out, weight_out, head_out, pred_out, dense_out, sems,
):
    copies = [(table, table_out), (rest_total.at[OUT_AT:GATE_AT], out_out), (rest_total.at[TOWER_AT:HEAD_AT], tower_out)]
    copies += [
        (
            in_total.at[pl.ds((4 * first + q * (last - first)) * UNITS, (last - first) * UNITS)],
            in_out.at[first * UNITS : last * UNITS, q * 128 : (q + 1) * 128],
        )
        for first, last in IN_PARTS
        for q in range(4)
    ]
    copies += [
        (rest_total.at[GATE_AT + q * 16 : GATE_AT + q * 16 + 16], gate_out.at[:, q * 128 : q * 128 + 128])
        for q in range(4)
    ]
    copies += [(weight_grad, weight_out), (head_grad, head_out), (pred, pred_out), (dense_grad, dense_out)]
    copies = [pltpu.make_async_copy(source, home, sems.at[i]) for i, (source, home) in enumerate(copies)]
    for copy in copies:
        copy.start()
    for copy in copies:
        copy.wait()


def on_device(
    tables, dense, dense_weight, expert_in, expert_out, gate_weight, tower_weight, head_weight, slots, requests, pred_cot
):
    i32 = jnp.int32
    dma = pltpu.SemaphoreType.DMA
    vmem = pltpu.VMEM
    anywhere = pl.BlockSpec(memory_space=pl.ANY)
    arrays = (
        requests[0].T,
        tables.transpose(0, 2, 1).reshape(EMBED, ROWS),
        expert_in.transpose(1, 2, 0).reshape(EXPERTS * UNITS, WIDTH),
        expert_out.reshape(EXPERTS * UNITS, OUT),
        pred_cot.T,
        slots.T,
        dense.T,
        dense_weight,
        gate_weight.transpose(0, 2, 1).reshape(TASKS * EXPERTS, WIDTH),
        tower_weight.transpose(0, 2, 1).reshape(TASKS * TOWER, OUT),
        head_weight,
    )
    shape = lambda *dims: jax.ShapeDtypeStruct(dims, f32)
    units = HIDDEN * 512, EXAMPLES
    outputs = EXPERTS, OUT, EXAMPLES
    results = pl.pallas_call(
        model_kernel,
        out_shape=[
            vmem((TASKS, 128), f32), vmem((DENSE, EXAMPLES), f32), vmem((EMBED, ROWS), f32), vmem((IN_ROWS, 128), f32),
            vmem((REST_ROWS, 128), f32), vmem((DENSE, PROJ), f32), vmem((TASKS, TOWER), f32),
        ],
        in_specs=[anywhere] * 11,
        out_specs=[VMEM] * 7,
        scratch_shapes=[
            vmem((32, 128), i32), vmem((EMBED, ROWS), f32), vmem((TASKS, 128), f32), vmem((TABLES, EXAMPLES), i32),
            vmem((DENSE, EXAMPLES), f32), vmem((DENSE, PROJ), f32), vmem((16, WIDTH), f32), vmem((128, OUT), f32),
            vmem((TASKS, TOWER), f32),
            vmem((128, 128), i32), vmem((32, 128), i32), vmem((32, 128), i32), vmem((8, 128), i32), vmem((128, 128), f32),
            vmem((512, 128), f32), vmem((2 * EMBED, ROWS), bf16),
            vmem((HIDDEN, 512, WIDTH), f32), vmem((HIDDEN, 512, OUT), f32), vmem((HIDDEN, TASKS, 128), f32),
            vmem((2048, WIDTH), bf16), vmem((2048, WIDTH), bf16), vmem((2048, OUT), bf16), vmem((2048, OUT), bf16),
            vmem((16, WIDTH), bf16), vmem((16, WIDTH), bf16), vmem((128, OUT), bf16), vmem((128, OUT), bf16),
            vmem((128, EXAMPLES), bf16), vmem((128, EXAMPLES), bf16),
            vmem((256, 512), bf16), vmem((WIDTH, EXAMPLES), bf16), vmem((WIDTH, EXAMPLES), bf16),
            vmem((128, EXAMPLES), f32), vmem((128, 128), f32), vmem((128, 128), f32),
            vmem(units, bf16), vmem(units, bf16), vmem(units, f32), vmem(units, bf16), vmem(units, bf16),
            vmem(outputs, f32), vmem(outputs, f32), vmem(outputs, bf16), vmem(outputs, bf16),
            vmem((16, EXAMPLES), f32), vmem((16, EXAMPLES), f32),
            vmem((TASKS, OUT, EXAMPLES), f32), vmem((TASKS, OUT, EXAMPLES), f32), vmem((TASKS, EXAMPLES), f32),
            vmem((128, EXAMPLES), f32), vmem((128, EXAMPLES), f32), vmem((16, EXAMPLES), f32),
            vmem((16, EXAMPLES), bf16), vmem((16, EXAMPLES), bf16),
            vmem((WIDTH, EXAMPLES), f32), vmem((256, 128), f32),
            vmem((IN_ROWS, 128), f32), vmem((REST_ROWS, 128), f32), vmem((IN_ROWS // 2, 128), f32),
            vmem((16 * REST_PIECE, 128), f32), vmem((IN_ROWS // 2, 128), f32), vmem((16 * REST_PIECE, 128), f32),
            vmem((128, 128), f32), vmem((128, 128), f32), vmem((16, 128), f32), vmem((8, 128), f32),
            vmem((128, 128), f32), vmem((16, 128), f32), vmem((ROWS, ROWS), bf16),
            vmem((128, TABLES * EXAMPLES), bf16),
            dma((11,)), dma((3,)), dma((3,)), dma((3,)), dma((3,)), dma, dma, dma,
            dma, dma, dma, dma, dma((2,)), dma((2,)), dma((4,)), dma((4,)), dma((4,)), dma,
            dma, dma, dma, dma, dma,
        ],
        compiler_params=pltpu.CompilerParams(vmem_limit_bytes=LIMIT, collective_id=0, has_side_effects=True),
        name="model",
    )(*arrays)
    results = [pltpu.with_memory_space_constraint(result, pltpu.VMEM) for result in results]
    pred, dense_grad, table_grad, in_total, rest_total, weight_grad, head_grad = results
    table_grad, in_grad, out_grad, tower_grad, gate_grad, weight_grad, head_grad, pred, dense_grad = pl.pallas_call(
        write_kernel,
        out_shape=[
            shape(EMBED, ROWS), shape(512, WIDTH), shape(512, OUT), shape(TASKS * TOWER, OUT),
            shape(TASKS * EXPERTS, WIDTH), shape(DENSE, PROJ), shape(TASKS, TOWER), shape(TASKS, 128),
            shape(DENSE, EXAMPLES),
        ],
        in_specs=[anywhere] * 7,
        out_specs=[anywhere] * 9,
        scratch_shapes=[dma((23,))],
        compiler_params=pltpu.CompilerParams(vmem_limit_bytes=LIMIT),
        name="write",
    )(table_grad, in_total, rest_total, weight_grad, head_grad, pred, dense_grad)
    return (
        pred.T,
        dense_grad.T,
        table_grad.reshape(TABLES, ENTRY, ROWS).transpose(0, 2, 1),
        weight_grad,
        in_grad.reshape(EXPERTS, UNITS, WIDTH).transpose(2, 0, 1),
        out_grad.reshape(EXPERTS, UNITS, OUT),
        gate_grad.reshape(TASKS, EXPERTS, WIDTH).transpose(0, 2, 1),
        tower_grad.reshape(TASKS, TOWER, OUT).transpose(0, 2, 1),
        head_grad,
    )


def solution(mesh):
    placed = (
        P(None, ("batch", "hidden"), None),
        P("batch", None),
        P(),
        P(None, None, "hidden"),
        P(None, "hidden", None),
        P(),
        P(),
        P(),
        P("batch", None),
        P("batch", None, None),
        P(("batch", "hidden"), None),
    )
    return jax.shard_map(
        on_device,
        mesh=mesh,
        in_specs=placed,
        out_specs=(
            P(("batch", "hidden"), None),
            P("batch", None),
            P(None, ("batch", "hidden"), None),
            P(),
            P(None, None, "hidden"),
            P(None, "hidden", None),
            P(),
            P(),
            P(),
        ),
        check_vma=False,
    )
```
